256 devices in a mesh: dp: 2 (over y_lo), lat: 16 (over y_hi, x, core), lon: 8 (over z).
Axes of the slice: x: 4, y: 4 (y_hi: 2, y_lo: 2; y = y_hi * 2 + y_lo), z: 8, core: 2. Of those that a mesh axis runs over, the one named last changes fastest.
Arguments:
- inputs: bfloat16 [2, 2, 96, 192, 512], P('dp', None, 'lat', 'lon'), may hold values from -6 to 6
- cotangent: bfloat16 [2, 2, 96, 192, 512], P('dp', None, 'lat', 'lon'), may hold values from -6 to 6
- mask_ids: int32 [96, 192], P('lat', 'lon'), may hold values from 0 to 3
- w_qkv: bfloat16 [512, 1536], replicated, may hold values from -4 to 4
- w_proj: bfloat16 [512, 512], replicated, may hold values from -0.25 to 0.25
Outputs:
- output: bfloat16 [2, 2, 96, 192, 512], P('dp', None, 'lat', 'lon')
- grad_inputs: bfloat16 [2, 2, 96, 192, 512], P('dp', None, 'lat', 'lon')
- grad_qkv: float32 [512, 1536], P(('lat', 'lon'))
- grad_proj: float32 [512, 512], P(('lat', 'lon'))
The draws below stay inside these ranges and needn't reach their ends.
All inputs are finite; a program needn't handle non-finite values.
Results may differ from the reference program's by a relative error of at most 0.011.
Values may be sent and summed in bfloat16 or wider, within the bound.
No kernel may reach another device: no remote copies, remote signals or barrier semaphores. Data moves between devices by JAX's collectives and lax.ppermute only.
A program may use at most 64 MiB of HBM per device.

```python
import math
import jax
import jax.numpy as jnp
from jax import lax

D = 512
HEADS = 16
HD = 32
LEV = 2
WLAT = 6
WLON = 12
SLAT = 3
SLON = 6
SAMPLES = 2
NLAT = 96
NLON = 192


def draw_w_qkv(key, part):
    key = jax.random.fold_in(key, 7)
    base = jax.random.normal(key, (D, 3 * D), jnp.float32) / math.sqrt(D)
    return jnp.clip(base, -4.0, 4.0).astype(jnp.bfloat16)


def place_ends(drawn, own_key, low, top_value):
    place = [jax.random.randint(jax.random.fold_in(own_key, axis), (), 0, length) for axis, length in enumerate(drawn.shape)]
    widest = drawn.shape.index(max(drawn.shape))
    next_to = place[:widest] + [(place[widest] + 1) % drawn.shape[widest]] + place[widest + 1:]
    return drawn.at[tuple(place)].set(low).at[tuple(next_to)].set(top_value)


def block_scale(key, shape, shards, least, high):
    level, own = 1.0, jax.random.fold_in(key, 6)
    for axis_at, parts in shards:
        draws = jnp.exp(jax.random.uniform(jax.random.fold_in(own, axis_at), (parts,), jnp.float32, least / len(shards), high / len(shards)))
        level = level * jnp.repeat(draws, shape[axis_at] // parts).reshape([-1 if axis == axis_at else 1 for axis in range(len(shape))])
    return level


def gaussian(stream_key, extent, scale, most, cuts=(), held_as=jnp.bfloat16):
    entries = scale * jax.random.normal(stream_key, extent, jnp.float32)
    if cuts:
        entries = entries * block_scale(stream_key, extent, cuts, -0.22, 0.18)
    return jnp.clip(entries, -most, most).astype(held_as)


def setup_inputs(seed: int = 0) -> dict:
    splits = jax.random.split(jax.random.key(seed), 6)
    inputs = gaussian(splits[0], (SAMPLES, LEV, NLAT, NLON, D), 1.0, 6.0, ((0, 2), (2, 16), (3, 8)))
    cotangent = gaussian(splits[1], (SAMPLES, LEV, NLAT, NLON, D), 1.0, 6.0, ((0, 2), (2, 16), (3, 8)))
    mask_ids = place_ends(jax.random.randint(splits[2], (NLAT, NLON), 0, 4), jax.random.fold_in(splits[2], 1), 0, 3).astype(jnp.int32)
    w_qkv = draw_w_qkv(jax.random.fold_in(splits[5], 71), 0)
    w_proj = gaussian(splits[4], (D, D), D ** -0.5, 0.25)
    return dict(inputs=inputs, cotangent=cotangent, mask_ids=mask_ids, w_qkv=w_qkv, w_proj=w_proj)


def product(form, left, right):
    return jnp.einsum(form, left.astype(jnp.float32), right.astype(jnp.float32))

def to_windows(array, n_rows, n_cols):
    batch, levels, rows, cols, width = array.shape
    shaped = array.reshape(batch, levels, n_rows, WLAT, n_cols, WLON, width)
    shaped = shaped.transpose(0, 2, 4, 1, 3, 5, 6)
    return shaped.reshape(batch * n_rows * n_cols, levels * WLAT * WLON, width)

def from_windows(array, batch, levels, n_rows, n_cols):
    width = array.shape[-1]
    shaped = array.reshape(batch, n_rows, n_cols, levels, WLAT, WLON, width)
    shaped = shaped.transpose(0, 3, 1, 4, 2, 5, 6)
    return shaped.reshape(batch, levels, n_rows * WLAT, n_cols * WLON, width)

def window_pass(rolled, grad_in, w_qkv, w_proj, groups):
    batch, levels, rows, cols, width = rolled.shape
    n_rows = rows // WLAT
    n_cols = cols // WLON
    labels = groups.reshape(n_rows, WLAT, n_cols, WLON).transpose(0, 2, 1, 3)
    labels = labels.reshape(n_rows * n_cols, 1, WLAT * WLON)
    labels = jnp.broadcast_to(labels, (n_rows * n_cols, levels, WLAT * WLON))
    labels = jnp.tile(labels.reshape(n_rows * n_cols, levels * WLAT * WLON), (batch, 1))
    allowed = (labels[:, :, None] == labels[:, None, :])[:, None]
    tokens = to_windows(rolled, n_rows, n_cols)
    upstream = to_windows(grad_in, n_rows, n_cols)
    windows, tok_count = (tokens.shape[0], tokens.shape[1])
    floats = tokens.astype(jnp.float32)
    center = lax.optimization_barrier(jnp.mean(floats, -1, keepdims=True))
    shifted = floats - center
    inverse = lax.rsqrt(lax.optimization_barrier(jnp.mean(shifted * shifted, -1, keepdims=True)) + 1e-05)
    normed = shifted * inverse
    normed_low = normed.astype(jnp.bfloat16)
    projected = product('wnd,de->wne', normed_low, w_qkv).astype(jnp.bfloat16)
    split = projected.reshape(windows, tok_count, 3, HEADS, HD)
    queries = split[:, :, 0]
    keyset = split[:, :, 1]
    values = split[:, :, 2]
    factor = 1.0 / math.sqrt(HD)
    scores = product('wqhe,wkhe->whqk', queries, keyset) * factor
    scores = jnp.where(allowed, scores, jnp.float32(-1e+30))
    highest = lax.optimization_barrier(jnp.max(scores, -1, keepdims=True))
    exponent = jnp.exp(scores - highest)
    attention = exponent / lax.optimization_barrier(jnp.sum(exponent, -1, keepdims=True))
    attention_low = attention.astype(jnp.bfloat16)
    mixed = product('whqk,wkhe->wqhe', attention_low, values).astype(jnp.bfloat16)
    mixed = mixed.reshape(windows, tok_count, width)
    result = (floats + product('wnd,de->wne', mixed, w_proj)).astype(jnp.bfloat16)
    grad_proj = product('wnd,wne->de', mixed, upstream)
    grad_mixed = product('wne,de->wnd', upstream, w_proj).astype(jnp.bfloat16)
    grad_mixed = grad_mixed.reshape(windows, tok_count, HEADS, HD)
    grad_attn = product('wqhe,wkhe->whqk', grad_mixed, values)
    grad_scores = attention * (grad_attn - lax.optimization_barrier(jnp.sum(grad_attn * attention, -1, keepdims=True)))
    grad_low = (grad_scores * factor).astype(jnp.bfloat16)
    grad_values = product('whqk,wqhe->wkhe', attention_low, grad_mixed).astype(jnp.bfloat16)
    grad_queries = product('whqk,wkhe->wqhe', grad_low, keyset).astype(jnp.bfloat16)
    grad_keys = product('whqk,wqhe->wkhe', grad_low, queries).astype(jnp.bfloat16)
    grad_projected = jnp.stack([grad_queries, grad_keys, grad_values], 2)
    grad_projected = grad_projected.reshape(windows, tok_count, 3 * width)
    grad_qkv = product('wnd,wne->de', normed_low, grad_projected)
    grad_normed = product('wne,de->wnd', grad_projected, w_qkv)
    grad_tokens = inverse * (grad_normed - lax.optimization_barrier(jnp.mean(grad_normed, -1, keepdims=True)) - normed * lax.optimization_barrier(jnp.mean(grad_normed * normed, -1, keepdims=True)))
    grad_total = (upstream.astype(jnp.float32) + grad_tokens).astype(jnp.bfloat16)
    return (from_windows(result, batch, levels, n_rows, n_cols), from_windows(grad_total, batch, levels, n_rows, n_cols), grad_qkv, grad_proj)

def reference(inputs, cotangent, mask_ids, w_qkv, w_proj):
    rolled = jnp.roll(inputs, (SLAT, SLON), axis=(2, 3))
    grad_in = jnp.roll(cotangent, (SLAT, SLON), axis=(2, 3))
    wrapped = (jnp.arange(NLAT) < SLAT).astype(jnp.int32)
    groups = mask_ids + 4 * wrapped[:, None]
    batch = rolled.shape[0]
    bands = NLAT // WLAT

    def blocks(array):
        shaped = array.reshape(batch, LEV, bands, WLAT, NLON, D).transpose(0, 2, 1, 3, 4, 5)
        return shaped.reshape(batch * bands, 1, LEV, WLAT, NLON, D)

    def unblock(array):
        shaped = array.reshape(batch, bands, LEV, WLAT, NLON, D).transpose(0, 2, 1, 3, 4, 5)
        return shaped.reshape(batch, LEV, NLAT, NLON, D)
    band_groups = jnp.tile(groups.reshape(bands, WLAT, NLON), (batch, 1, 1))

    def step(totals, pieces):
        part_x, part_g, part_m = pieces
        result, back, grad_qkv, grad_proj = window_pass(part_x, part_g, w_qkv, w_proj, part_m)
        return ((totals[0] + grad_qkv, totals[1] + grad_proj), (result, back))
    start = (jnp.zeros((D, 3 * D), jnp.float32), jnp.zeros((D, D), jnp.float32))
    totals, stacked = lax.scan(step, start, (blocks(rolled), blocks(grad_in), band_groups))
    output = jnp.roll(unblock(stacked[0]), (-SLAT, -SLON), axis=(2, 3))
    grad_inputs = jnp.roll(unblock(stacked[1]), (-SLAT, -SLON), axis=(2, 3))
    return (output, grad_inputs, totals[0], totals[1])
```

```python
import functools
import math

import jax
import jax.numpy as jnp
from jax import lax
from jax.experimental import pallas as pl
from jax.experimental.pallas import tpu as pltpu
from jax.sharding import Mesh
from jax.sharding import PartitionSpec as P

D = 512
HEADS = 16
HD = 32
LEV = 2
WLAT = 6
WLON = 12
SLAT = 3
SLON = 6
WT = LEV * WLAT * WLON
PER = 4
LANES = PER * HD
UNITS = D // LANES
FACTOR = 1.0 / math.sqrt(HD)
LOG2E = 1.4426950408889634

NN = (((1,), (0,)), ((), ()))
NT = (((1,), (1,)), ((), ()))


def dot(left, right, dims=NN):
    return lax.dot_general(left, right, dims, preferred_element_type=jnp.float32)


def statistics(x_ref):
    x = x_ref[...].astype(jnp.float32)
    center = jnp.mean(x, -1, keepdims=True)
    shifted = x - center
    inverse = lax.rsqrt(jnp.mean(shifted * shifted, -1, keepdims=True) + 1e-05)
    return shifted * inverse, inverse


def store_shares(target_ref, grads, added_ref=None):
    count = grads.shape[0]
    first = lax.broadcasted_iota(jnp.int32, (count, 128), 0) % 8 < 4
    for quad in range(4):
        shares = ([], [])
        for pair in (2 * quad, 2 * quad + 1):
            left = grads[:, pair * 256:pair * 256 + 128]
            right = grads[:, pair * 256 + 128:pair * 256 + 256]
            shares[0].append(jnp.where(first, left, pltpu.roll(right, 4, 0)))
            shares[1].append(jnp.where(first, pltpu.roll(left, count - 4, 0), right))
        rows = slice(quad * 16, quad * 16 + 16)
        for which in range(2):
            piece = jnp.concatenate([p.reshape(count // 8, 8, 128) for p in shares[which]], axis=1)
            if added_ref is not None:
                piece = piece + added_ref[:, which, rows, :].astype(jnp.float32)
            target_ref[:, which, rows, :] = piece.astype(jnp.bfloat16)


def attention_kernel(
    x_ref, u_ref, lrow_ref, lcol_ref, wqkv_ref, wproj_ref,
    send_ref, gp_ref, mix_ref, nkeep_ref, mkeep_ref,
    proj_ref, gm_ref, nt_ref, mt_ref, mixt_ref, al_ref, gl_ref, s_ref, da_ref,
):
    windows = x_ref.shape[0] // WT
    core = lax.axis_index("core")
    half = D // 2
    normed, _ = statistics(x_ref)
    normed_low = normed.astype(jnp.bfloat16)
    proj_ref[...] = dot(normed_low, wqkv_ref[...]).astype(jnp.bfloat16)
    gm_ref[...] = dot(u_ref[...], wproj_ref[...], NT).astype(jnp.bfloat16)

    def place(target_ref, array):
        for b in range(D // 32):
            slot = lax.bitwise_xor(core, b % 2)
            row = pl.multiple_of(slot * half + (b // 2) * 32, 32)
            target_ref[pl.ds(row, 32), :] = array[b * 32:(b + 1) * 32, :]

    place(nt_ref, normed_low.T)

    lane = lax.broadcasted_iota(jnp.int32, (1, LANES), 1) // HD
    masks = [(lane == h).astype(jnp.float32) for h in range(PER)]
    low_masks = [m.astype(jnp.bfloat16) for m in masks]

    def stacked(array):
        return jnp.concatenate([array * m for m in low_masks], axis=0)

    def unstacked(array):
        total = array[:WT] * masks[0]
        for h in range(1, PER):
            total = total + array[h * WT:(h + 1) * WT] * masks[h]
        return total.astype(jnp.bfloat16)

    for w in range(windows):
        rows = slice(w * WT, (w + 1) * WT)
        allowed = lcol_ref[rows, :] == lrow_ref[w:w + 1, :]
        for g in range(UNITS):
            q_cols, k_cols, v_cols = (
                slice(part * D + g * LANES, part * D + (g + 1) * LANES) for part in range(3)
            )
            q = proj_ref[rows, q_cols]
            k = proj_ref[rows, k_cols]
            v = proj_ref[rows, v_cols]
            gm = gm_ref[rows, q_cols]
            s_ref[...] = dot(stacked(k), q, NT)
            da_ref[...] = dot(stacked(v), gm, NT)
            vt = v.T
            kt = k.T
            for h in range(PER):
                part = slice(h * WT, (h + 1) * WT)
                s = jnp.where(allowed, s_ref[part, :], jnp.float32(-1e30))
                e = jnp.exp2((s - jnp.max(s, 0, keepdims=True)) * jnp.float32(FACTOR * LOG2E))
                a = e * (1.0 / jnp.sum(e, 0, keepdims=True))
                al = a.astype(jnp.bfloat16)
                al_ref[part, :] = al
                ga = da_ref[part, :] * a
                gl = ((ga - a * jnp.sum(ga, 0, keepdims=True)) * jnp.float32(FACTOR)).astype(jnp.bfloat16)
                gl_ref[part, :] = gl
                chan = slice(g * LANES + h * HD, g * LANES + (h + 1) * HD)
                mixt_ref[chan, :] = dot(vt[h * HD:(h + 1) * HD, :], al)
                s_ref[h * HD:(h + 1) * HD, :] = dot(kt[h * HD:(h + 1) * HD, :], gl)
            gp_ref[rows, q_cols] = s_ref[:LANES, :].T.astype(jnp.bfloat16)
            gp_ref[rows, k_cols] = unstacked(dot(gl_ref[...], q))
            gp_ref[rows, v_cols] = unstacked(dot(al_ref[...], gm))
        mix_ref[rows, :] = mixt_ref[...].T.astype(jnp.bfloat16)

    place(mt_ref, mix_ref[...].T)
    nkeep_ref[...] = nt_ref[:half, :]
    mkeep_ref[...] = mt_ref[:half, :]
    grads = jnp.concatenate([dot(nt_ref[half:, :], gp_ref[...]), dot(mt_ref[half:, :], u_ref[...])], axis=1)
    store_shares(send_ref, grads)


def gradient_kernel(n_ref, m_ref, gp_ref, u_ref, got_ref, sum_ref):
    grads = jnp.concatenate([dot(n_ref[...], gp_ref[...]), dot(m_ref[...], u_ref[...])], axis=1)
    store_shares(sum_ref, grads, got_ref)


def token_kernel(x_ref, u_ref, mix_ref, gp_ref, wqkv_ref, wproj_ref, out_ref, gin_ref):
    out_ref[...] = (x_ref[...].astype(jnp.float32) + dot(mix_ref[...], wproj_ref[...])).astype(jnp.bfloat16)
    grad_normed = dot(gp_ref[...], wqkv_ref[...], NT)
    normed, inverse = statistics(x_ref)
    grad_tokens = inverse * (
        grad_normed
        - jnp.mean(grad_normed, -1, keepdims=True)
        - normed * jnp.mean(grad_normed * normed, -1, keepdims=True)
    )
    gin_ref[...] = (u_ref[...].astype(jnp.float32) + grad_tokens).astype(jnp.bfloat16)


def call(kernel, name, outs, scratch, flops, *args):
    vmem = pl.BlockSpec(memory_space=pltpu.VMEM)
    size = sum(2 * math.prod(shape) for shape in outs)
    return pl.pallas_call(
        kernel,
        out_shape=tuple(jax.ShapeDtypeStruct(shape, jnp.bfloat16) for shape in outs),
        in_specs=[vmem] * len(args),
        out_specs=(vmem,) * len(outs),
        scratch_shapes=[pltpu.VMEM(shape, dtype) for shape, dtype in scratch],
        compiler_params=pltpu.CompilerParams(vmem_limit_bytes=40 * 1024 * 1024),
        cost_estimate=pl.CostEstimate(flops=flops, bytes_accessed=2 * size, transcendentals=0),
        name=name,
    )(*args)


def attention(x, u, lrow, lcol, w_qkv, w_proj):
    tokens = x.shape[0]
    low, full = jnp.bfloat16, jnp.float32
    return call(
        attention_kernel,
        "window_attention",
        ((32, 2, 64, 128), (tokens, 3 * D), (tokens, D), (D // 2, tokens), (D // 2, tokens)),
        (
            ((tokens, 3 * D), low),
            ((tokens, D), low),
            ((D, tokens), low),
            ((D, tokens), low),
            ((D, WT), full),
            ((PER * WT, WT), low),
            ((PER * WT, WT), low),
            ((PER * WT, WT), full),
            ((PER * WT, WT), full),
        ),
        5_000_000_000,
        x, u, lrow, lcol, w_qkv, w_proj,
    )


def to_windows(array):
    batch, levels, rows, cols, width = array.shape
    shaped = array.reshape(levels, rows, cols // WLON, WLON, width)
    return shaped.transpose(2, 0, 1, 3, 4).reshape(cols // WLON * WT, width)


def from_windows(array):
    windows = array.shape[0] // WT
    shaped = array.reshape(windows, LEV, WLAT, WLON, D).transpose(1, 2, 0, 3, 4)
    return shaped.reshape(1, LEV, WLAT, windows * WLON, D)


LAT = ("yh", "x", "core")


def passed_along(value, axis, steps):
    count = lax.axis_size(axis)
    pairs = [(source, (source + steps) % count) for source in range(count)]
    return lax.ppermute(value, axis, pairs)


def diagonal(value, steps):
    n_lat, n_lon = lax.axis_size(LAT), lax.axis_size("lon")
    pairs = [
        (a * n_lon + b, (a + steps) % n_lat * n_lon + (b + steps) % n_lon)
        for a in range(n_lat)
        for b in range(n_lon)
    ]
    return lax.ppermute(value, (*LAT, "lon"), pairs)


def move_one(inputs, cotangent):
    def cut(rows, cols):
        return jnp.concatenate([inputs[:, :, rows, cols], cotangent[:, :, rows, cols]], axis=0)

    head, last, body, side = slice(0, SLAT), slice(SLAT, None), slice(0, -SLON), slice(-SLON, None)
    corner = diagonal(cut(last, side), 1)
    upper = passed_along(cut(last, body), LAT, 1)
    left = passed_along(cut(head, side), "lon", 1)
    outs = []
    for at, own in enumerate((inputs, cotangent)):
        top = jnp.concatenate([corner[at:at + 1], upper[at:at + 1]], axis=3)
        bottom = jnp.concatenate([left[at:at + 1], own[:, :, head, body]], axis=3)
        outs.append(jnp.concatenate([top, bottom], axis=2))
    return outs


def move_back(both):
    head, last, side, body = slice(0, SLAT), slice(SLAT, None), slice(0, SLON), slice(SLON, None)
    corner = diagonal(both[:, :, head, side], -1)
    lower = passed_along(both[:, :, head, body], LAT, -1)
    right = passed_along(both[:, :, last, side], "lon", -1)
    top = jnp.concatenate([both[:, :, last, body], right], axis=3)
    bottom = jnp.concatenate([lower, corner], axis=3)
    return jnp.concatenate([top, bottom], axis=2)


def per_device(inputs, cotangent, mask_ids, w_qkv, w_proj):
    rolled, grad_in = move_one(inputs, cotangent)
    x = to_windows(rolled)
    u = to_windows(grad_in)
    first_band = lax.axis_index(LAT) == 0
    wrapped = jnp.logical_and(first_band, jnp.arange(WLAT) < SLAT).astype(jnp.int32)
    groups = mask_ids + 4 * wrapped[:, None]
    windows = groups.shape[1] // WLON
    labels = groups.reshape(WLAT, windows, WLON).transpose(1, 0, 2).reshape(windows, WLAT * WLON)
    lrow = jnp.tile(labels, (1, LEV))
    lcol = lrow.reshape(windows * WT, 1)
    send, gp, mix, nkeep, mkeep = attention(x, u, lrow, lcol, w_qkv, w_proj)
    got = passed_along(send, "core", 1)
    result, grad_total = call(
        token_kernel, "token_outputs", (x.shape, x.shape), (), 2_000_000_000,
        x, u, mix, gp, w_qkv, w_proj,
    )
    (sums,) = call(
        gradient_kernel, "gradient_sum", (send.shape,), (), 600_000_000,
        nkeep, mkeep, gp, u, got,
    )
    spread = lax.all_to_all(sums.reshape(64, 64, 128), ("yh", "x", "lon"), 0, 0, tiled=True)
    share = jnp.sum(spread.astype(jnp.float32), 0)
    share = share + passed_along(share, "dp", 1)
    share = share.reshape(16, 4, 128).transpose(1, 0, 2).reshape(4, 4 * D)
    back = move_back(jnp.concatenate([from_windows(result), from_windows(grad_total)], axis=0))
    return (back[:1], back[1:], share[:, :3 * D], share[:, 3 * D:])


def solution(mesh):
    mesh = Mesh(mesh.devices.reshape(2, 2, 4, 2, 8), ("dp", "yh", "x", "core", "lon"))
    tokens = P("dp", None, LAT, "lon", None)
    return jax.shard_map(
        per_device,
        mesh=mesh,
        in_specs=(tokens, tokens, P(LAT, "lon"), P(), P()),
        out_specs=(tokens, tokens, P((*LAT, "lon"), None), P((*LAT, "lon"), None)),
        check_vma=False,
    )
```

```python
import functools
import math

import jax
import jax.numpy as jnp
from jax import lax
from jax.experimental import pallas as pl
from jax.experimental.pallas import tpu as pltpu
from jax.sharding import Mesh
from jax.sharding import PartitionSpec as P

D = 512
HEADS = 16
HD = 32
LEV = 2
WLAT = 6
WLON = 12
SLAT = 3
SLON = 6
WT = LEV * WLAT * WLON
PER = 4
LANES = PER * HD
UNITS = D // LANES
FACTOR = 1.0 / math.sqrt(HD)
LOG2E = 1.4426950408889634

NN = (((1,), (0,)), ((), ()))
NT = (((1,), (1,)), ((), ()))


def dot(left, right, dims=NN):
    return lax.dot_general(left, right, dims, preferred_element_type=jnp.float32)


def statistics(x_ref):
    x = x_ref[...].astype(jnp.float32)
    center = jnp.mean(x, -1, keepdims=True)
    shifted = x - center
    inverse = lax.rsqrt(jnp.mean(shifted * shifted, -1, keepdims=True) + 1e-05)
    return shifted * inverse, inverse


def store_shares(target_ref, grads):
    count = grads.shape[0]
    first = lax.broadcasted_iota(jnp.int32, (count, 128), 0) % 8 < 4
    for quad in range(4):
        shares = ([], [])
        for pair in (2 * quad, 2 * quad + 1):
            left = grads[:, pair * 256:pair * 256 + 128]
            right = grads[:, pair * 256 + 128:pair * 256 + 256]
            shares[0].append(jnp.where(first, left, pltpu.roll(right, 4, 0)))
            shares[1].append(jnp.where(first, pltpu.roll(left, count - 4, 0), right))
        rows = slice(quad * 16, quad * 16 + 16)
        for which in range(2):
            piece = jnp.concatenate([p.reshape(count // 8, 8, 128) for p in shares[which]], axis=1)
            target_ref[:, which, rows, :] = piece.astype(target_ref.dtype)


def attention_kernel(
    x_ref, u_ref, lrow_ref, lcol_ref, wqkv_ref, wproj_ref,
    send_ref, gp_ref, mix_ref, nkeep_ref, mkeep_ref,
    proj_ref, gm_ref, nt_ref, mt_ref, mixt_ref, al_ref, gl_ref, s_ref, da_ref,
):
    windows = x_ref.shape[0] // WT
    core = lax.axis_index("core")
    half = D // 2
    normed, _ = statistics(x_ref)
    normed_low = normed.astype(jnp.bfloat16)
    proj_ref[...] = dot(normed_low, wqkv_ref[...]).astype(jnp.bfloat16)
    gm_ref[...] = dot(u_ref[...], wproj_ref[...], NT).astype(jnp.bfloat16)

    def place(target_ref, array):
        for b in range(D // 32):
            slot = lax.bitwise_xor(core, b % 2)
            row = pl.multiple_of(slot * half + (b // 2) * 32, 32)
            target_ref[pl.ds(row, 32), :] = array[b * 32:(b + 1) * 32, :]

    place(nt_ref, normed_low.T)

    lane = lax.broadcasted_iota(jnp.int32, (1, LANES), 1) // HD
    masks = [(lane == h).astype(jnp.float32) for h in range(PER)]
    low_masks = [m.astype(jnp.bfloat16) for m in masks]

    def stacked(array):
        return jnp.concatenate([array * m for m in low_masks], axis=0)

    def unstacked(array):
        total = array[:WT] * masks[0]
        for h in range(1, PER):
            total = total + array[h * WT:(h + 1) * WT] * masks[h]
        return total.astype(jnp.bfloat16)

    for w in range(windows):
        rows = slice(w * WT, (w + 1) * WT)
        allowed = lcol_ref[rows, :] == lrow_ref[w:w + 1, :]
        for g in range(UNITS):
            q_cols, k_cols, v_cols = (
                slice(part * D + g * LANES, part * D + (g + 1) * LANES) for part in range(3)
            )
            q = proj_ref[rows, q_cols]
            k = proj_ref[rows, k_cols]
            v = proj_ref[rows, v_cols]
            gm = gm_ref[rows, q_cols]
            s_ref[...] = dot(stacked(k), q, NT)
            da_ref[...] = dot(stacked(v), gm, NT)
            vt = v.T
            kt = k.T
            for h in range(PER):
                part = slice(h * WT, (h + 1) * WT)
                s = jnp.where(allowed, s_ref[part, :], jnp.float32(-1e30))
                e = jnp.exp2((s - jnp.max(s, 0, keepdims=True)) * jnp.float32(FACTOR * LOG2E))
                a = e * (1.0 / jnp.sum(e, 0, keepdims=True))
                al = a.astype(jnp.bfloat16)
                al_ref[part, :] = al
                ga = da_ref[part, :] * a
                gl = ((ga - a * jnp.sum(ga, 0, keepdims=True)) * jnp.float32(FACTOR)).astype(jnp.bfloat16)
                gl_ref[part, :] = gl
                chan = slice(g * LANES + h * HD, g * LANES + (h + 1) * HD)
                mixt_ref[chan, :] = dot(vt[h * HD:(h + 1) * HD, :], al)
                s_ref[h * HD:(h + 1) * HD, :] = dot(kt[h * HD:(h + 1) * HD, :], gl)
            gp_ref[rows, q_cols] = s_ref[:LANES, :].T.astype(jnp.bfloat16)
            gp_ref[rows, k_cols] = unstacked(dot(gl_ref[...], q))
            gp_ref[rows, v_cols] = unstacked(dot(al_ref[...], gm))
        mix_ref[rows, :] = mixt_ref[...].T.astype(jnp.bfloat16)

    place(mt_ref, mix_ref[...].T)
    nkeep_ref[...] = nt_ref[:half, :]
    mkeep_ref[...] = mt_ref[:half, :]
    grads = jnp.concatenate([dot(nt_ref[half:, :], gp_ref[...]), dot(mt_ref[half:, :], u_ref[...])], axis=1)
    store_shares(send_ref, grads)


def own_half_kernel(n_ref, m_ref, gp_ref, u_ref, own_ref):
    grads = jnp.concatenate([dot(n_ref[...], gp_ref[...]), dot(m_ref[...], u_ref[...])], axis=1)
    store_shares(own_ref, grads)


def add_kernel(own_ref, got_ref, sum_ref):
    sum_ref[...] = (own_ref[...] + got_ref[...].astype(jnp.float32)).astype(jnp.bfloat16)


def sum_kernel(parts_ref, sum_ref):
    total = parts_ref[0].astype(jnp.float32)
    for part in range(1, parts_ref.shape[0]):
        total = total + parts_ref[part].astype(jnp.float32)
    sum_ref[...] = total.astype(sum_ref.dtype)


def last_kernel(share_ref, other_ref, qkv_ref, proj_ref):
    total = share_ref[...] + other_ref[...]
    for tile in range(16):
        piece = total[tile * 4:tile * 4 + 4, :]
        if tile < 12:
            qkv_ref[:, tile * 128:(tile + 1) * 128] = piece
        else:
            proj_ref[:, (tile - 12) * 128:(tile - 11) * 128] = piece


def stage_kernel(qkv_ref, proj_ref, qkv_out, proj_out, sems):
    copies = [
        pltpu.make_async_copy(qkv_ref, qkv_out, sems.at[0]),
        pltpu.make_async_copy(proj_ref, proj_out, sems.at[1]),
    ]
    for copy in copies:
        copy.start()
    for copy in copies:
        copy.wait()


def staged(w_qkv, w_proj):
    return pl.pallas_call(
        stage_kernel,
        out_shape=(
            pltpu.VMEM(w_qkv.shape, w_qkv.dtype),
            pltpu.VMEM(w_proj.shape, w_proj.dtype),
        ),
        in_specs=[pl.BlockSpec(memory_space=pl.ANY)] * 2,
        out_specs=(pl.BlockSpec(memory_space=pltpu.VMEM),) * 2,
        scratch_shapes=[pltpu.SemaphoreType.DMA((2,))],
        compiler_params=pltpu.CompilerParams(vmem_limit_bytes=40 * 1024 * 1024),
        cost_estimate=pl.CostEstimate(flops=0, bytes_accessed=4 * 1024 * 1024, transcendentals=0),
        name="stage_weights",
    )(w_qkv, w_proj)


def token_kernel(x_ref, u_ref, mix_ref, gp_ref, wqkv_ref, wproj_ref, out_ref, gin_ref):
    out_ref[...] = (x_ref[...].astype(jnp.float32) + dot(mix_ref[...], wproj_ref[...])).astype(jnp.bfloat16)
    grad_normed = dot(gp_ref[...], wqkv_ref[...], NT)
    normed, inverse = statistics(x_ref)
    grad_tokens = inverse * (
        grad_normed
        - jnp.mean(grad_normed, -1, keepdims=True)
        - normed * jnp.mean(grad_normed * normed, -1, keepdims=True)
    )
    gin_ref[...] = (u_ref[...].astype(jnp.float32) + grad_tokens).astype(jnp.bfloat16)


def call(kernel, name, outs, scratch, flops, *args, dtype=jnp.bfloat16):
    vmem = pl.BlockSpec(memory_space=pltpu.VMEM)
    size = sum(2 * math.prod(shape) for shape in outs)
    return pl.pallas_call(
        kernel,
        out_shape=tuple(jax.ShapeDtypeStruct(shape, dtype) for shape in outs),
        in_specs=[vmem] * len(args),
        out_specs=(vmem,) * len(outs),
        scratch_shapes=[pltpu.VMEM(shape, kind) for shape, kind in scratch],
        compiler_params=pltpu.CompilerParams(vmem_limit_bytes=40 * 1024 * 1024),
        cost_estimate=pl.CostEstimate(flops=flops, bytes_accessed=2 * size, transcendentals=0),
        name=name,
    )(*args)


def attention(x, u, lrow, lcol, w_qkv, w_proj):
    tokens = x.shape[0]
    low, full = jnp.bfloat16, jnp.float32
    return call(
        attention_kernel,
        "window_attention",
        ((32, 2, 64, 128), (tokens, 3 * D), (tokens, D), (D // 2, tokens), (D // 2, tokens)),
        (
            ((tokens, 3 * D), low),
            ((tokens, D), low),
            ((D, tokens), low),
            ((D, tokens), low),
            ((D, WT), full),
            ((PER * WT, WT), low),
            ((PER * WT, WT), low),
            ((PER * WT, WT), full),
            ((PER * WT, WT), full),
        ),
        5_000_000_000,
        x, u, lrow, lcol, w_qkv, w_proj,
    )


def to_windows(array):
    batch, levels, rows, cols, width = array.shape
    shaped = array.reshape(levels, rows, cols // WLON, WLON, width)
    return shaped.transpose(2, 0, 1, 3, 4).reshape(cols // WLON * WT, width)


def from_windows(array):
    windows = array.shape[0] // WT
    shaped = array.reshape(windows, LEV, WLAT, WLON, D).transpose(1, 2, 0, 3, 4)
    return shaped.reshape(1, LEV, WLAT, windows * WLON, D)


LAT = ("yh", "x", "core")


def passed_along(value, axis, steps):
    count = lax.axis_size(axis)
    pairs = [(source, (source + steps) % count) for source in range(count)]
    return lax.ppermute(value, axis, pairs)


def diagonal(value, steps):
    n_lat, n_lon = lax.axis_size(LAT), lax.axis_size("lon")
    pairs = [
        (a * n_lon + b, (a + steps) % n_lat * n_lon + (b + steps) % n_lon)
        for a in range(n_lat)
        for b in range(n_lon)
    ]
    return lax.ppermute(value, (*LAT, "lon"), pairs)


def move_one(inputs, cotangent):
    def cut(rows, cols):
        return jnp.concatenate([inputs[:, :, rows, cols], cotangent[:, :, rows, cols]], axis=0)

    head, last, body, side = slice(0, SLAT), slice(SLAT, None), slice(0, -SLON), slice(-SLON, None)
    corner = diagonal(cut(last, side), 1)
    upper = passed_along(cut(last, body), LAT, 1)
    left = passed_along(cut(head, side), "lon", 1)
    outs = []
    for at, own in enumerate((inputs, cotangent)):
        top = jnp.concatenate([corner[at:at + 1], upper[at:at + 1]], axis=3)
        bottom = jnp.concatenate([left[at:at + 1], own[:, :, head, body]], axis=3)
        outs.append(jnp.concatenate([top, bottom], axis=2))
    return outs


def move_back(both):
    head, last, side, body = slice(0, SLAT), slice(SLAT, None), slice(0, SLON), slice(SLON, None)
    corner = diagonal(both[:, :, head, side], -1)
    lower = passed_along(both[:, :, head, body], LAT, -1)
    right = passed_along(both[:, :, last, side], "lon", -1)
    top = jnp.concatenate([both[:, :, last, body], right], axis=3)
    bottom = jnp.concatenate([lower, corner], axis=3)
    return jnp.concatenate([top, bottom], axis=2)


def per_device(inputs, cotangent, mask_ids, w_qkv, w_proj):
    rolled, grad_in = move_one(inputs, cotangent)
    x = to_windows(rolled)
    u = to_windows(grad_in)
    first_band = lax.axis_index(LAT) == 0
    wrapped = jnp.logical_and(first_band, jnp.arange(WLAT) < SLAT).astype(jnp.int32)
    groups = mask_ids + 4 * wrapped[:, None]
    windows = groups.shape[1] // WLON
    labels = groups.reshape(WLAT, windows, WLON).transpose(1, 0, 2).reshape(windows, WLAT * WLON)
    lrow = jnp.tile(labels, (1, LEV))
    lcol = lrow.reshape(windows * WT, 1)
    w_qkv, w_proj = staged(w_qkv, w_proj)
    send, gp, mix, nkeep, mkeep = attention(x, u, lrow, lcol, w_qkv, w_proj)
    got = passed_along(send, "core", 1)
    (own,) = call(
        own_half_kernel, "own_half", (send.shape,), (), 600_000_000,
        nkeep, mkeep, gp, u, dtype=jnp.float32,
    )
    (sums,) = call(add_kernel, "add_halves", (send.shape,), (), 1_000_000, own, got)
    result, grad_total = call(
        token_kernel, "token_outputs", (x.shape, x.shape), (), 2_000_000_000,
        x, u, mix, gp, w_qkv, w_proj,
    )
    result, grad_total, sums = lax.optimization_barrier((result, grad_total, sums))
    spread = lax.all_to_all(sums.reshape(8, 512, 128), ("yh", "x"), 0, 0, tiled=True)
    (sums,) = call(sum_kernel, "sum_parts", ((512, 128),), (), 1_000_000, spread)
    spread = lax.all_to_all(sums.reshape(8, 64, 128), "lon", 0, 0, tiled=True)
    share = jnp.sum(spread.astype(jnp.float32), 0)
    other = passed_along(share, "dp", 1)
    grad_qkv, grad_proj = call(
        last_kernel, "last_sum", ((4, 3 * D), (4, D)), (), 1000, share, other, dtype=jnp.float32
    )
    back = move_back(jnp.concatenate([from_windows(result), from_windows(grad_total)], axis=0))
    return (back[:1], back[1:], grad_qkv, grad_proj)


def solution(mesh):
    mesh = Mesh(mesh.devices.reshape(2, 2, 4, 2, 8), ("dp", "yh", "x", "core", "lon"))
    tokens = P("dp", None, LAT, "lon", None)
    return jax.shard_map(
        per_device,
        mesh=mesh,
        in_specs=(tokens, tokens, P(LAT, "lon"), P(), P()),
        out_specs=(tokens, tokens, P((*LAT, "lon"), None), P((*LAT, "lon"), None)),
        check_vma=False,
    )
```

```python
import functools
import math

import jax
import jax.numpy as jnp
from jax import lax
from jax.experimental import pallas as pl
from jax.experimental.pallas import tpu as pltpu
from jax.sharding import Mesh
from jax.sharding import PartitionSpec as P

D = 512
HEADS = 16
HD = 32
LEV = 2
WLAT = 6
WLON = 12
SLAT = 3
SLON = 6
WT = LEV * WLAT * WLON
PER = 4
LANES = PER * HD
UNITS = D // LANES
FACTOR = 1.0 / math.sqrt(HD)
LOG2E = 1.4426950408889634

NN = (((1,), (0,)), ((), ()))
NT = (((1,), (1,)), ((), ()))


def dot(left, right, dims=NN):
    return lax.dot_general(left, right, dims, preferred_element_type=jnp.float32)


def cut_kernel(x_ref, u_ref, upper_ref, corner_ref, left_ref, held_ref, sems):
    copies = []
    for at, ref in enumerate((x_ref, u_ref)):
        for level in range(LEV):
            copies.append(pltpu.make_async_copy(ref.at[0, level], held_ref.at[at, level], sems.at[at, level]))
    for copy in copies:
        copy.start()
    for copy in copies:
        copy.wait()
    for at in range(2):
        for level in range(LEV):
            for row in range(WLAT):
                tokens = held_ref[at, level, row].astype(jnp.float32)
                side = tokens[-SLON:].astype(jnp.bfloat16)
                if row < SLAT:
                    left_ref[at, level, row] = side
                else:
                    corner_ref[at, level, row - SLAT] = side
                    upper_ref[at, level, row - SLAT] = tokens[:-SLON].astype(jnp.bfloat16)


def join_kernel(own_ref, right_ref, lower_ref, corner_ref, out_ref, gin_ref):
    for at, ref in enumerate((out_ref, gin_ref)):
        for level in range(LEV):
            for row in range(WLAT):
                if row < SLAT:
                    body, side = own_ref[at, level, row], right_ref[at, level, row]
                else:
                    body, side = lower_ref[at, level, row - SLAT], corner_ref[at, level, row - SLAT]
                both = jnp.concatenate([body.astype(jnp.float32), side.astype(jnp.float32)], axis=0)
                ref[0, level, row] = both.astype(jnp.bfloat16)


def assemble(target_ref, at, own_ref, upper_ref, corner_ref, left_ref):
    pieces = ([], [])
    for level in range(LEV):
        for row in range(WLAT):
            if row < SLAT:
                side, body = corner_ref[at, level, row], upper_ref[at, level, row]
            else:
                side, body = left_ref[at, level, row - SLAT], own_ref[0, level, row - SLAT]
            side, body = side.astype(jnp.float32), body.astype(jnp.float32)
            pieces[0].append(side)
            pieces[0].append(body[:WLON - SLON])
            pieces[1].append(body[WLON - SLON:2 * WLON - SLON])
    for w in range(2):
        target_ref[w * WT:(w + 1) * WT, :] = jnp.concatenate(pieces[w], axis=0)


def statistics(x):
    center = jnp.mean(x, -1, keepdims=True)
    shifted = x - center
    inverse = lax.rsqrt(jnp.mean(shifted * shifted, -1, keepdims=True) + 1e-05)
    return shifted * inverse, inverse


def store_shares(target_ref, grads):
    count = grads.shape[0]
    first = lax.broadcasted_iota(jnp.int32, (count, 128), 0) % 8 < 4
    for quad in range(4):
        shares = ([], [])
        for pair in (2 * quad, 2 * quad + 1):
            left = grads[:, pair * 256:pair * 256 + 128]
            right = grads[:, pair * 256 + 128:pair * 256 + 256]
            shares[0].append(jnp.where(first, left, pltpu.roll(right, 4, 0)))
            shares[1].append(jnp.where(first, pltpu.roll(left, count - 4, 0), right))
        rows = slice(quad * 16, quad * 16 + 16)
        for which in range(2):
            piece = jnp.concatenate([p.reshape(count // 8, 8, 128) for p in shares[which]], axis=1)
            target_ref[:, which, rows, :] = piece.astype(target_ref.dtype)


def attention_kernel(
    own_x_ref, own_u_ref, upper_ref, corner_ref, left_ref, lrow_ref, lcol_ref, wqkv_ref, wproj_ref,
    send_ref, gp_ref, mix_ref, nkeep_ref, mkeep_ref, x_ref, u_ref,
    full_ref, proj_ref, gm_ref, nt_ref, mt_ref, mixt_ref, al_ref, gl_ref, s_ref, da_ref,
):
    windows = x_ref.shape[0] // WT
    core = lax.axis_index("core")
    half = D // 2
    assemble(full_ref, 1, own_u_ref, upper_ref, corner_ref, left_ref)
    u_ref[...] = full_ref[...].astype(jnp.bfloat16)
    assemble(full_ref, 0, own_x_ref, upper_ref, corner_ref, left_ref)
    x_ref[...] = full_ref[...].astype(jnp.bfloat16)
    normed, _ = statistics(full_ref[...])
    normed_low = normed.astype(jnp.bfloat16)
    proj_ref[...] = dot(normed_low, wqkv_ref[...]).astype(jnp.bfloat16)
    gm_ref[...] = dot(u_ref[...], wproj_ref[...], NT).astype(jnp.bfloat16)

    def place(target_ref, array):
        for b in range(D // 32):
            slot = lax.bitwise_xor(core, b % 2)
            row = pl.multiple_of(slot * half + (b // 2) * 32, 32)
            target_ref[pl.ds(row, 32), :] = array[b * 32:(b + 1) * 32, :]

    place(nt_ref, normed_low.T)

    lane = lax.broadcasted_iota(jnp.int32, (1, LANES), 1) // HD
    masks = [(lane == h).astype(jnp.float32) for h in range(PER)]
    low_masks = [m.astype(jnp.bfloat16) for m in masks]

    def stacked(array):
        return jnp.concatenate([array * m for m in low_masks], axis=0)

    def unstacked(array):
        total = array[:WT] * masks[0]
        for h in range(1, PER):
            total = total + array[h * WT:(h + 1) * WT] * masks[h]
        return total.astype(jnp.bfloat16)

    for w in range(windows):
        rows = slice(w * WT, (w + 1) * WT)
        allowed = lcol_ref[rows, :] == lrow_ref[w:w + 1, :]
        for g in range(UNITS):
            q_cols, k_cols, v_cols = (
                slice(part * D + g * LANES, part * D + (g + 1) * LANES) for part in range(3)
            )
            q = proj_ref[rows, q_cols]
            k = proj_ref[rows, k_cols]
            v = proj_ref[rows, v_cols]
            gm = gm_ref[rows, q_cols]
            s_ref[...] = dot(stacked(k), q, NT)
            da_ref[...] = dot(stacked(v), gm, NT)
            vt = v.T
            kt = k.T
            for h in range(PER):
                part = slice(h * WT, (h + 1) * WT)
                s = jnp.where(allowed, s_ref[part, :], jnp.float32(-1e30))
                e = jnp.exp2((s - jnp.max(s, 0, keepdims=True)) * jnp.float32(FACTOR * LOG2E))
                a = e * (1.0 / jnp.sum(e, 0, keepdims=True))
                al = a.astype(jnp.bfloat16)
                al_ref[part, :] = al
                ga = da_ref[part, :] * a
                gl = ((ga - a * jnp.sum(ga, 0, keepdims=True)) * jnp.float32(FACTOR)).astype(jnp.bfloat16)
                gl_ref[part, :] = gl
                chan = slice(g * LANES + h * HD, g * LANES + (h + 1) * HD)
                mixt_ref[chan, :] = dot(vt[h * HD:(h + 1) * HD, :], al)
                s_ref[h * HD:(h + 1) * HD, :] = dot(kt[h * HD:(h + 1) * HD, :], gl)
            gp_ref[rows, q_cols] = s_ref[:LANES, :].T.astype(jnp.bfloat16)
            gp_ref[rows, k_cols] = unstacked(dot(gl_ref[...], q))
            gp_ref[rows, v_cols] = unstacked(dot(al_ref[...], gm))
        mix_ref[rows, :] = mixt_ref[...].T.astype(jnp.bfloat16)

    place(mt_ref, mix_ref[...].T)
    nkeep_ref[...] = nt_ref[:half, :]
    mkeep_ref[...] = mt_ref[:half, :]
    grads = jnp.concatenate([dot(nt_ref[half:, :], gp_ref[...]), dot(mt_ref[half:, :], u_ref[...])], axis=1)
    store_shares(send_ref, grads)


def add_kernel(own_ref, got_ref, sum_ref):
    sum_ref[...] = (own_ref[...] + got_ref[...].astype(jnp.float32)).astype(jnp.bfloat16)


def sum_kernel(parts_ref, sum_ref):
    total = parts_ref[0].astype(jnp.float32)
    for part in range(1, parts_ref.shape[0]):
        total = total + parts_ref[part].astype(jnp.float32)
    sum_ref[...] = total.astype(sum_ref.dtype)


def last_kernel(share_ref, other_ref, qkv_ref, proj_ref):
    total = share_ref[...] + other_ref[...]
    for tile in range(16):
        piece = total[tile * 4:tile * 4 + 4, :]
        if tile < 12:
            qkv_ref[:, tile * 128:(tile + 1) * 128] = piece
        else:
            proj_ref[:, (tile - 12) * 128:(tile - 11) * 128] = piece


def stage_kernel(qkv_ref, proj_ref, qkv_out, proj_out, sems):
    copies = [
        pltpu.make_async_copy(qkv_ref, qkv_out, sems.at[0]),
        pltpu.make_async_copy(proj_ref, proj_out, sems.at[1]),
    ]
    for copy in copies:
        copy.start()
    for copy in copies:
        copy.wait()


def staged(w_qkv, w_proj):
    return pl.pallas_call(
        stage_kernel,
        out_shape=(
            pltpu.VMEM(w_qkv.shape, w_qkv.dtype),
            pltpu.VMEM(w_proj.shape, w_proj.dtype),
        ),
        in_specs=[pl.BlockSpec(memory_space=pltpu.HBM)] * 2,
        out_specs=(pl.BlockSpec(memory_space=pltpu.VMEM),) * 2,
        scratch_shapes=[pltpu.SemaphoreType.DMA((2,))],
        compiler_params=pltpu.CompilerParams(vmem_limit_bytes=4 * 1024 * 1024),
        cost_estimate=pl.CostEstimate(flops=0, bytes_accessed=4 * 1024 * 1024, transcendentals=0),
        name="stage_weights",
    )(w_qkv, w_proj)


def part(value, at, refs):
    own_ref, left_ref, upper_ref, corner_ref = refs
    for level in range(LEV):
        for row in range(WLAT):
            base = (level * WLAT + row) * WLON
            tokens = jnp.concatenate([value[base:base + WLON], value[WT + base:WT + base + WLON]], axis=0)
            side, body = tokens[:SLON].astype(jnp.bfloat16), tokens[SLON:].astype(jnp.bfloat16)
            if row < SLAT:
                corner_ref[at, level, row] = side
                upper_ref[at, level, row] = body
            else:
                left_ref[at, level, row - SLAT] = side
                own_ref[at, level, row - SLAT] = body


def rest_kernel(
    n_ref, m_ref, gp_ref, u_ref, x_ref, mix_ref, qkv_ref, proj_ref,
    half_ref, own_ref, left_ref, upper_ref, corner_ref,
    wqkv_ref, wproj_ref, sems,
):
    copies = [
        pltpu.make_async_copy(proj_ref, wproj_ref, sems.at[0]),
        pltpu.make_async_copy(qkv_ref, wqkv_ref, sems.at[1]),
    ]
    for copy in copies:
        copy.start()
    grads = jnp.concatenate([dot(n_ref[...], gp_ref[...]), dot(m_ref[...], u_ref[...])], axis=1)
    store_shares(half_ref, grads)
    refs = (own_ref, left_ref, upper_ref, corner_ref)
    x = x_ref[...].astype(jnp.float32)
    copies[0].wait()
    part(x + dot(mix_ref[...], wproj_ref[...]), 0, refs)
    normed, inverse = statistics(x)
    copies[1].wait()
    grad_normed = dot(gp_ref[...], wqkv_ref[...], NT)
    grad_tokens = inverse * (
        grad_normed
        - jnp.mean(grad_normed, -1, keepdims=True)
        - normed * jnp.mean(grad_normed * normed, -1, keepdims=True)
    )
    part(u_ref[...].astype(jnp.float32) + grad_tokens, 1, refs)


def call(kernel, name, outs, scratch, flops, *args, dtypes=None, limit=12, placed=False, any_args=()):
    vmem = pl.BlockSpec(memory_space=pltpu.VMEM)
    dtypes = dtypes or (jnp.bfloat16,) * len(outs)
    make = pltpu.VMEM if placed else jax.ShapeDtypeStruct
    size = sum(2 * math.prod(shape) for shape in outs)
    return pl.pallas_call(
        kernel,
        out_shape=tuple(make(shape, dtype) for shape, dtype in zip(outs, dtypes)),
        in_specs=[
            pl.BlockSpec(memory_space=pltpu.HBM) if at in any_args else vmem for at in range(len(args))
        ],
        out_specs=(vmem,) * len(outs),
        scratch_shapes=[
            pltpu.SemaphoreType.DMA(shape) if kind is None else pltpu.VMEM(shape, kind)
            for shape, kind in scratch
        ],
        compiler_params=pltpu.CompilerParams(vmem_limit_bytes=limit * 1024 * 1024),
        cost_estimate=pl.CostEstimate(flops=flops, bytes_accessed=2 * size, transcendentals=0),
        name=name,
    )(*args)


def attention(x, u, upper, corner, left, lrow, lcol, w_qkv, w_proj):
    tokens = math.prod(x.shape[:-1])
    low, full = jnp.bfloat16, jnp.float32
    return call(
        attention_kernel,
        "window_attention",
        (
            (32, 2, 64, 128), (tokens, 3 * D), (tokens, D),
            (D // 2, tokens), (D // 2, tokens), (tokens, D), (tokens, D),
        ),
        (
            ((tokens, D), full),
            ((tokens, 3 * D), low),
            ((tokens, D), low),
            ((D, tokens), low),
            ((D, tokens), low),
            ((D, WT), full),
            ((PER * WT, WT), low),
            ((PER * WT, WT), low),
            ((PER * WT, WT), full),
            ((PER * WT, WT), full),
        ),
        5_000_000_000,
        x, u, upper, corner, left, lrow, lcol, w_qkv, w_proj,
        limit=20,
    )


LAT = ("yh", "x", "core")


def passed_along(value, axis, steps):
    count = lax.axis_size(axis)
    pairs = [(source, (source + steps) % count) for source in range(count)]
    return lax.ppermute(value, axis, pairs)


def diagonal(value, steps):
    n_lat, n_lon = lax.axis_size(LAT), lax.axis_size("lon")
    pairs = [
        (a * n_lon + b, (a + steps) % n_lat * n_lon + (b + steps) % n_lon)
        for a in range(n_lat)
        for b in range(n_lon)
    ]
    return lax.ppermute(value, (*LAT, "lon"), pairs)


def per_device(inputs, cotangent, mask_ids, w_qkv, w_proj):
    body = (2, LEV, SLAT, inputs.shape[3] - SLON, D)
    side = (2, LEV, SLAT, SLON, D)
    upper, corner, left = call(
        cut_kernel, "cut_halos", (body, side, side),
        (((2, *inputs.shape[1:]), jnp.bfloat16), ((2, LEV), None)), 1000,
        *(pltpu.with_memory_space_constraint(array, pltpu.HBM) for array in (inputs, cotangent)),
        limit=8, any_args=(0, 1),
    )
    upper = passed_along(upper, LAT, 1)
    corner = diagonal(corner, 1)
    left = passed_along(left, "lon", 1)
    first_band = lax.axis_index(LAT) == 0
    wrapped = jnp.logical_and(first_band, jnp.arange(WLAT) < SLAT).astype(jnp.int32)
    groups = mask_ids + 4 * wrapped[:, None]
    windows = groups.shape[1] // WLON
    labels = groups.reshape(WLAT, windows, WLON).transpose(1, 0, 2).reshape(windows, WLAT * WLON)
    lrow = jnp.tile(labels, (1, LEV))
    lcol = lrow.reshape(windows * WT, 1)
    send, gp, mix, nkeep, mkeep, x, u = attention(
        inputs, cotangent, upper, corner, left, lrow, lcol, *staged(w_qkv, w_proj)
    )
    got = passed_along(send, "core", 1)
    half, own, left, upper, corner = call(
        rest_kernel, "own_half_and_outputs", (send.shape, body, side, body, side),
        ((w_qkv.shape, jnp.bfloat16), (w_proj.shape, jnp.bfloat16), ((2,), None)), 600_000_000,
        nkeep, mkeep, gp, u, x, mix, w_qkv, w_proj,
        dtypes=(jnp.float32,) + (jnp.bfloat16,) * 4, any_args=(6, 7), limit=16,
    )
    (sums,) = call(add_kernel, "add_halves", (send.shape,), (), 1_000_000, half, got, placed=True)
    own, left, upper, corner, sums = lax.optimization_barrier((own, left, upper, corner, sums))
    spread = lax.all_to_all(sums.reshape(8, 512, 128), ("yh", "x"), 0, 0, tiled=True)
    corner = diagonal(corner, -1)
    lower = passed_along(upper, LAT, -1)
    right = passed_along(left, "lon", -1)
    (sums,) = call(sum_kernel, "sum_parts", ((512, 128),), (), 1_000_000, spread, placed=True)
    spread = lax.all_to_all(sums.reshape(8, 64, 128), "lon", 0, 0, tiled=True)
    share = jnp.sum(spread.astype(jnp.float32), 0)
    other = passed_along(share, "dp", 1)
    grad_qkv, grad_proj = call(
        last_kernel, "last_sum", ((4, 3 * D), (4, D)), (), 1000, share, other,
        dtypes=(jnp.float32,) * 2, limit=4,
    )
    output, grad_inputs = call(
        join_kernel, "join_outputs", (inputs.shape, inputs.shape), (), 1000,
        own, right, lower, corner, limit=8,
    )
    return (output, grad_inputs, grad_qkv, grad_proj)


def solution(mesh):
    mesh = Mesh(mesh.devices.reshape(2, 2, 4, 2, 8), ("dp", "yh", "x", "core", "lon"))
    tokens = P("dp", None, LAT, "lon", None)
    return jax.shard_map(
        per_device,
        mesh=mesh,
        in_specs=(tokens, tokens, P(LAT, "lon"), P(), P()),
        out_specs=(tokens, tokens, P((*LAT, "lon"), None), P((*LAT, "lon"), None)),
        check_vma=False,
    )
```

```python
import functools
import math

import jax
import jax.numpy as jnp
from jax import lax
from jax.experimental import pallas as pl
from jax.experimental.pallas import tpu as pltpu
from jax.sharding import Mesh
from jax.sharding import PartitionSpec as P

D = 512
HEADS = 16
HD = 32
LEV = 2
WLAT = 6
WLON = 12
SLAT = 3
SLON = 6
WT = LEV * WLAT * WLON
PER = 4
LANES = PER * HD
UNITS = D // LANES
FACTOR = 1.0 / math.sqrt(HD)
LOG2E = 1.4426950408889634

NN = (((1,), (0,)), ((), ()))
NT = (((1,), (1,)), ((), ()))


def dot(left, right, dims=NN):
    return lax.dot_general(left, right, dims, preferred_element_type=jnp.float32)


def cut_kernel(x_ref, u_ref, upper_ref, corner_ref, left_ref, held_ref, sems):
    copies = []
    for at, ref in enumerate((x_ref, u_ref)):
        for level in range(LEV):
            copies.append(pltpu.make_async_copy(ref.at[0, level], held_ref.at[at, level], sems.at[at, level]))
    for copy in copies:
        copy.start()
    for copy in copies:
        copy.wait()
    for at in range(2):
        for level in range(LEV):
            for row in range(WLAT):
                tokens = held_ref[at, level, row].astype(jnp.float32)
                side = tokens[-SLON:].astype(jnp.bfloat16)
                if row < SLAT:
                    left_ref[at, level, row] = side
                else:
                    corner_ref[at, level, row - SLAT] = side
                    upper_ref[at, level, row - SLAT] = tokens[:-SLON].astype(jnp.bfloat16)


def join_kernel(own_ref, right_ref, lower_ref, corner_ref, out_ref, gin_ref):
    for at, ref in enumerate((out_ref, gin_ref)):
        for level in range(LEV):
            for row in range(WLAT):
                if row < SLAT:
                    body, side = own_ref[at, level, row], right_ref[at, level, row]
                else:
                    body, side = lower_ref[at, level, row - SLAT], corner_ref[at, level, row - SLAT]
                both = jnp.concatenate([body.astype(jnp.float32), side.astype(jnp.float32)], axis=0)
                ref[0, level, row] = both.astype(jnp.bfloat16)


def assemble(target_ref, at, own_ref, upper_ref, corner_ref, left_ref):
    pieces = ([], [])
    for level in range(LEV):
        for row in range(WLAT):
            if row < SLAT:
                side, body = corner_ref[at, level, row], upper_ref[at, level, row]
            else:
                side, body = left_ref[at, level, row - SLAT], own_ref[0, level, row - SLAT]
            side, body = side.astype(jnp.float32), body.astype(jnp.float32)
            pieces[0].append(side)
            pieces[0].append(body[:WLON - SLON])
            pieces[1].append(body[WLON - SLON:2 * WLON - SLON])
    for w in range(2):
        target_ref[w * WT:(w + 1) * WT, :] = jnp.concatenate(pieces[w], axis=0)


def statistics(x):
    center = jnp.mean(x, -1, keepdims=True)
    shifted = x - center
    inverse = lax.rsqrt(jnp.mean(shifted * shifted, -1, keepdims=True) + 1e-05)
    return shifted * inverse, inverse


def store_shares(target_ref, grads):
    count = grads.shape[0]
    first = lax.broadcasted_iota(jnp.int32, (count, 128), 0) % 8 < 4
    for quad in range(4):
        shares = ([], [])
        for pair in (2 * quad, 2 * quad + 1):
            left = grads[:, pair * 256:pair * 256 + 128]
            right = grads[:, pair * 256 + 128:pair * 256 + 256]
            shares[0].append(jnp.where(first, left, pltpu.roll(right, 4, 0)))
            shares[1].append(jnp.where(first, pltpu.roll(left, count - 4, 0), right))
        rows = slice(quad * 16, quad * 16 + 16)
        for which in range(2):
            piece = jnp.concatenate([p.reshape(count // 8, 8, 128) for p in shares[which]], axis=1)
            target_ref[:, which, rows, :] = piece.astype(target_ref.dtype)


def attention_kernel(
    own_x_ref, own_u_ref, upper_ref, corner_ref, left_ref, lrow_ref, lcol_ref, wqkv_ref, wproj_ref,
    send_ref, gp_ref, mix_ref, nkeep_ref, mkeep_ref, x_ref, u_ref,
    full_ref, proj_ref, gm_ref, nt_ref, mt_ref, mixt_ref, al_ref, gl_ref, s_ref, da_ref,
):
    windows = x_ref.shape[0] // WT
    core = lax.axis_index("core")
    half = D // 2
    assemble(full_ref, 1, own_u_ref, upper_ref, corner_ref, left_ref)
    u_ref[...] = full_ref[...].astype(jnp.bfloat16)
    assemble(full_ref, 0, own_x_ref, upper_ref, corner_ref, left_ref)
    x_ref[...] = full_ref[...].astype(jnp.bfloat16)
    normed, _ = statistics(full_ref[...])
    normed_low = normed.astype(jnp.bfloat16)
    proj_ref[...] = dot(normed_low, wqkv_ref[...]).astype(jnp.bfloat16)
    gm_ref[...] = dot(u_ref[...], wproj_ref[...], NT).astype(jnp.bfloat16)

    def place(target_ref, array):
        for b in range(D // 32):
            slot = lax.bitwise_xor(core, b % 2)
            row = pl.multiple_of(slot * half + (b // 2) * 32, 32)
            target_ref[pl.ds(row, 32), :] = array[b * 32:(b + 1) * 32, :]

    place(nt_ref, normed_low.T)

    lane = lax.broadcasted_iota(jnp.int32, (1, LANES), 1) // HD
    masks = [(lane == h).astype(jnp.float32) for h in range(PER)]
    low_masks = [m.astype(jnp.bfloat16) for m in masks]

    def stacked(array):
        return jnp.concatenate([array * m for m in low_masks], axis=0)

    def unstacked(array):
        total = array[:WT] * masks[0]
        for h in range(1, PER):
            total = total + array[h * WT:(h + 1) * WT] * masks[h]
        return total.astype(jnp.bfloat16)

    for w in range(windows):
        rows = slice(w * WT, (w + 1) * WT)
        allowed = lcol_ref[rows, :] == lrow_ref[w:w + 1, :]
        for g in range(UNITS):
            q_cols, k_cols, v_cols = (
                slice(part * D + g * LANES, part * D + (g + 1) * LANES) for part in range(3)
            )
            q = proj_ref[rows, q_cols]
            k = proj_ref[rows, k_cols]
            v = proj_ref[rows, v_cols]
            gm = gm_ref[rows, q_cols]
            s_ref[...] = dot(stacked(k), q, NT)
            da_ref[...] = dot(stacked(v), gm, NT)
            vt = v.T
            kt = k.T
            for h in range(PER):
                part = slice(h * WT, (h + 1) * WT)
                s = jnp.where(allowed, s_ref[part, :], jnp.float32(-1e30))
                e = jnp.exp2((s - jnp.max(s, 0, keepdims=True)) * jnp.float32(FACTOR * LOG2E))
                a = e * (1.0 / jnp.sum(e, 0, keepdims=True))
                al = a.astype(jnp.bfloat16)
                al_ref[part, :] = al
                ga = da_ref[part, :] * a
                gl = ((ga - a * jnp.sum(ga, 0, keepdims=True)) * jnp.float32(FACTOR)).astype(jnp.bfloat16)
                gl_ref[part, :] = gl
                chan = slice(g * LANES + h * HD, g * LANES + (h + 1) * HD)
                mixt_ref[chan, :] = dot(vt[h * HD:(h + 1) * HD, :], al)
                s_ref[h * HD:(h + 1) * HD, :] = dot(kt[h * HD:(h + 1) * HD, :], gl)
            gp_ref[rows, q_cols] = s_ref[:LANES, :].T.astype(jnp.bfloat16)
            gp_ref[rows, k_cols] = unstacked(dot(gl_ref[...], q))
            gp_ref[rows, v_cols] = unstacked(dot(al_ref[...], gm))
        mix_ref[rows, :] = mixt_ref[...].T.astype(jnp.bfloat16)

    place(mt_ref, mix_ref[...].T)
    nkeep_ref[...] = nt_ref[:half, :]
    mkeep_ref[...] = mt_ref[:half, :]
    grads = jnp.concatenate([dot(nt_ref[half:, :], gp_ref[...]), dot(mt_ref[half:, :], u_ref[...])], axis=1)
    store_shares(send_ref, grads)


def first_kernel(half_ref, got_ref, keep0_ref, send0_ref, keep1_ref, send1_ref):
    a, d = lax.axis_index("xl"), lax.axis_index("dp")

    def total(*at):
        return half_ref[at] + got_ref[at].astype(jnp.float32)

    for yh in range(2):
        keep0_ref[yh] = total(yh, 0, a)
        send0_ref[yh] = total(yh, 0, 1 - a).astype(jnp.bfloat16)
        for xl in range(2):
            for lon in range(8):
                keep1_ref[yh, xl, lon] = total(yh, 1, xl, lon, d)
                send1_ref[yh, xl, lon] = total(yh, 1, xl, lon, 1 - d).astype(jnp.bfloat16)


def second_kernel(keep0_ref, got0_ref, keep1_ref, got1_ref, own_ref, send0_ref, send1_ref):
    a, d = lax.axis_index("xl"), lax.axis_index("dp")

    def total0(*at):
        return keep0_ref[at] + got0_ref[at].astype(jnp.float32)

    def total1(*at):
        return keep1_ref[at] + got1_ref[at].astype(jnp.float32)

    for yh in range(2):
        own_ref[1, yh] = total1(yh, a)
        send1_ref[yh] = total1(yh, 1 - a).astype(jnp.bfloat16)
        for lon in range(8):
            own_ref[0, yh, lon] = total0(yh, lon, d)
            send0_ref[yh, lon] = total0(yh, lon, 1 - d).astype(jnp.bfloat16)


def third_kernel(own_ref, got0_ref, got1_ref, sum_ref):
    for xh, ref in enumerate((got0_ref, got1_ref)):
        for yh in range(2):
            sum_ref[yh, xh] = (own_ref[xh, yh] + ref[yh].astype(jnp.float32)).astype(jnp.bfloat16)


def last_kernel(share_ref, other_ref, qkv_ref, proj_ref):
    second = lax.axis_index("dp") == 1
    share, other = share_ref[...], other_ref[...]
    halves = (jnp.where(second, other, share), jnp.where(second, share, other))
    for tile in range(16):
        row = tile % 8 * 4
        piece = halves[tile // 8][row:row + 4, :]
        if tile < 12:
            qkv_ref[:, tile * 128:(tile + 1) * 128] = piece
        else:
            proj_ref[:, (tile - 12) * 128:(tile - 11) * 128] = piece


def stage_kernel(qkv_ref, proj_ref, qkv_out, proj_out, sems):
    copies = [
        pltpu.make_async_copy(qkv_ref, qkv_out, sems.at[0]),
        pltpu.make_async_copy(proj_ref, proj_out, sems.at[1]),
    ]
    for copy in copies:
        copy.start()
    for copy in copies:
        copy.wait()


def staged(w_qkv, w_proj):
    return pl.pallas_call(
        stage_kernel,
        out_shape=(
            pltpu.VMEM(w_qkv.shape, w_qkv.dtype),
            pltpu.VMEM(w_proj.shape, w_proj.dtype),
        ),
        in_specs=[pl.BlockSpec(memory_space=pltpu.HBM)] * 2,
        out_specs=(pl.BlockSpec(memory_space=pltpu.VMEM),) * 2,
        scratch_shapes=[pltpu.SemaphoreType.DMA((2,))],
        compiler_params=pltpu.CompilerParams(vmem_limit_bytes=4 * 1024 * 1024),
        cost_estimate=pl.CostEstimate(flops=0, bytes_accessed=4 * 1024 * 1024, transcendentals=0),
        name="stage_weights",
    )(w_qkv, w_proj)


def part(value, at, refs):
    own_ref, left_ref, upper_ref, corner_ref = refs
    for level in range(LEV):
        for row in range(WLAT):
            base = (level * WLAT + row) * WLON
            tokens = jnp.concatenate([value[base:base + WLON], value[WT + base:WT + base + WLON]], axis=0)
            side, body = tokens[:SLON].astype(jnp.bfloat16), tokens[SLON:].astype(jnp.bfloat16)
            if row < SLAT:
                corner_ref[at, level, row] = side
                upper_ref[at, level, row] = body
            else:
                left_ref[at, level, row - SLAT] = side
                own_ref[at, level, row - SLAT] = body


def rest_kernel(
    n_ref, m_ref, gp_ref, u_ref, x_ref, mix_ref, qkv_ref, proj_ref,
    half_ref, own_ref, left_ref, upper_ref, corner_ref,
    wqkv_ref, wproj_ref, sems,
):
    copies = [
        pltpu.make_async_copy(proj_ref, wproj_ref, sems.at[0]),
        pltpu.make_async_copy(qkv_ref, wqkv_ref, sems.at[1]),
    ]
    for copy in copies:
        copy.start()
    grads = jnp.concatenate([dot(n_ref[...], gp_ref[...]), dot(m_ref[...], u_ref[...])], axis=1)
    store_shares(half_ref, grads)
    refs = (own_ref, left_ref, upper_ref, corner_ref)
    x = x_ref[...].astype(jnp.float32)
    copies[0].wait()
    part(x + dot(mix_ref[...], wproj_ref[...]), 0, refs)
    normed, inverse = statistics(x)
    copies[1].wait()
    grad_normed = dot(gp_ref[...], wqkv_ref[...], NT)
    grad_tokens = inverse * (
        grad_normed
        - jnp.mean(grad_normed, -1, keepdims=True)
        - normed * jnp.mean(grad_normed * normed, -1, keepdims=True)
    )
    part(u_ref[...].astype(jnp.float32) + grad_tokens, 1, refs)


def call(kernel, name, outs, scratch, flops, *args, dtypes=None, limit=12, placed=False, any_args=()):
    vmem = pl.BlockSpec(memory_space=pltpu.VMEM)
    dtypes = dtypes or (jnp.bfloat16,) * len(outs)
    make = pltpu.VMEM if placed else jax.ShapeDtypeStruct
    size = sum(2 * math.prod(shape) for shape in outs)
    return pl.pallas_call(
        kernel,
        out_shape=tuple(make(shape, dtype) for shape, dtype in zip(outs, dtypes)),
        in_specs=[
            pl.BlockSpec(memory_space=pltpu.HBM) if at in any_args else vmem for at in range(len(args))
        ],
        out_specs=(vmem,) * len(outs),
        scratch_shapes=[
            pltpu.SemaphoreType.DMA(shape) if kind is None else pltpu.VMEM(shape, kind)
            for shape, kind in scratch
        ],
        compiler_params=pltpu.CompilerParams(vmem_limit_bytes=limit * 1024 * 1024),
        cost_estimate=pl.CostEstimate(flops=flops, bytes_accessed=2 * size, transcendentals=0),
        name=name,
    )(*args)


def attention(x, u, upper, corner, left, lrow, lcol, w_qkv, w_proj):
    tokens = math.prod(x.shape[:-1])
    low, full = jnp.bfloat16, jnp.float32
    return call(
        attention_kernel,
        "window_attention",
        (
            (32, 2, 64, 128), (tokens, 3 * D), (tokens, D),
            (D // 2, tokens), (D // 2, tokens), (tokens, D), (tokens, D),
        ),
        (
            ((tokens, D), full),
            ((tokens, 3 * D), low),
            ((tokens, D), low),
            ((D, tokens), low),
            ((D, tokens), low),
            ((D, WT), full),
            ((PER * WT, WT), low),
            ((PER * WT, WT), low),
            ((PER * WT, WT), full),
            ((PER * WT, WT), full),
        ),
        5_000_000_000,
        x, u, upper, corner, left, lrow, lcol, w_qkv, w_proj,
        limit=20,
    )


LAT = ("yh", "xh", "xl", "core")


def passed_along(value, axis, steps):
    count = lax.axis_size(axis)
    pairs = [(source, (source + steps) % count) for source in range(count)]
    return lax.ppermute(value, axis, pairs)


def diagonal(value, steps):
    n_lat, n_lon = lax.axis_size(LAT), lax.axis_size("lon")
    pairs = [
        (a * n_lon + b, (a + steps) % n_lat * n_lon + (b + steps) % n_lon)
        for a in range(n_lat)
        for b in range(n_lon)
    ]
    return lax.ppermute(value, (*LAT, "lon"), pairs)


def per_device(inputs, cotangent, mask_ids, w_qkv, w_proj):
    body = (2, LEV, SLAT, inputs.shape[3] - SLON, D)
    side = (2, LEV, SLAT, SLON, D)
    upper, corner, left = call(
        cut_kernel, "cut_halos", (body, side, side),
        (((2, *inputs.shape[1:]), jnp.bfloat16), ((2, LEV), None)), 1000,
        *(pltpu.with_memory_space_constraint(array, pltpu.HBM) for array in (inputs, cotangent)),
        limit=8, any_args=(0, 1),
    )
    upper = passed_along(upper, LAT, 1)
    corner = diagonal(corner, 1)
    left = passed_along(left, "lon", 1)
    first_band = lax.axis_index(LAT) == 0
    wrapped = jnp.logical_and(first_band, jnp.arange(WLAT) < SLAT).astype(jnp.int32)
    groups = mask_ids + 4 * wrapped[:, None]
    windows = groups.shape[1] // WLON
    labels = groups.reshape(WLAT, windows, WLON).transpose(1, 0, 2).reshape(windows, WLAT * WLON)
    lrow = jnp.tile(labels, (1, LEV))
    lcol = lrow.reshape(windows * WT, 1)
    send, gp, mix, nkeep, mkeep, x, u = attention(
        inputs, cotangent, upper, corner, left, lrow, lcol, *staged(w_qkv, w_proj)
    )
    got = passed_along(send, "core", 1)
    half, own, left, upper, corner = call(
        rest_kernel, "own_half_and_outputs", (send.shape, body, side, body, side),
        ((w_qkv.shape, jnp.bfloat16), (w_proj.shape, jnp.bfloat16), ((2,), None)), 600_000_000,
        nkeep, mkeep, gp, u, x, mix, w_qkv, w_proj,
        dtypes=(jnp.float32,) + (jnp.bfloat16,) * 4, any_args=(6, 7), limit=16,
    )
    low, full = jnp.bfloat16, jnp.float32
    shape = (2, 2, 2, 8, 2, 32, 128)
    keep0, send0, keep1, send1 = call(
        first_kernel, "first_sums", ((2, 8, 2, 32, 128),) * 2 + ((2, 2, 8, 32, 128),) * 2, (), 1_000_000,
        half.reshape(shape), got.reshape(shape), dtypes=(full, low) * 2, placed=True,
    )
    got0, got1 = passed_along(send0, "xl", 1), passed_along(send1, "dp", 1)
    mine, send0, send1 = call(
        second_kernel, "second_sums", ((2, 2, 8, 32, 128),) + ((2, 8, 32, 128),) * 2, (), 1_000_000,
        keep0, got0, keep1, got1, dtypes=(full, low, low), placed=True,
    )
    got0, got1 = passed_along(send0, "dp", 1), passed_along(send1, "xl", 1)
    (sums,) = call(
        third_kernel, "third_sums", ((2, 2, 8, 32, 128),), (), 1_000_000, mine, got0, got1, placed=True
    )
    own, left, upper, corner, sums = lax.optimization_barrier((own, left, upper, corner, sums))
    spread = lax.all_to_all(sums.reshape(32, 32, 128), ("yh", "xh", "lon"), 0, 0, tiled=True)
    corner = diagonal(corner, -1)
    lower = passed_along(upper, LAT, -1)
    right = passed_along(left, "lon", -1)
    share = jnp.sum(spread.astype(jnp.float32), 0)
    other = passed_along(share, "dp", 1)
    grad_qkv, grad_proj = call(
        last_kernel, "last_sum", ((4, 3 * D), (4, D)), (), 1000, share, other,
        dtypes=(jnp.float32,) * 2, limit=4,
    )
    output, grad_inputs = call(
        join_kernel, "join_outputs", (inputs.shape, inputs.shape), (), 1000,
        own, right, lower, corner, limit=8,
    )
    return (output, grad_inputs, grad_qkv, grad_proj)


def solution(mesh):
    mesh = Mesh(mesh.devices.reshape(2, 2, 2, 2, 2, 8), ("dp", *LAT, "lon"))
    tokens = P("dp", None, LAT, "lon", None)
    return jax.shard_map(
        per_device,
        mesh=mesh,
        in_specs=(tokens, tokens, P(LAT, "lon"), P(), P()),
        out_specs=(tokens, tokens, P((*LAT, "lon"), None), P((*LAT, "lon"), None)),
        check_vma=False,
    )
```

```python
import functools
import math

import jax
import jax.numpy as jnp
from jax import lax
from jax.experimental import pallas as pl
from jax.experimental.pallas import tpu as pltpu
from jax.sharding import Mesh
from jax.sharding import PartitionSpec as P

D = 512
HEADS = 16
HD = 32
LEV = 2
WLAT = 6
WLON = 12
SLAT = 3
SLON = 6
WT = LEV * WLAT * WLON
PER = 4
LANES = PER * HD
UNITS = D // LANES
FACTOR = 1.0 / math.sqrt(HD)
LOG2E = 1.4426950408889634

NN = (((1,), (0,)), ((), ()))
NT = (((1,), (1,)), ((), ()))


def dot(left, right, dims=NN):
    return lax.dot_general(left, right, dims, preferred_element_type=jnp.float32)


def cut_kernel(x_ref, u_ref, upper_ref, corner_ref, left_ref, held_ref, sems):
    copies = []
    for at, ref in enumerate((x_ref, u_ref)):
        for level in range(LEV):
            copies.append(pltpu.make_async_copy(ref.at[0, level], held_ref.at[at, level], sems.at[at, level]))
    for copy in copies:
        copy.start()
    for copy in copies:
        copy.wait()
    for at in range(2):
        for level in range(LEV):
            for row in range(WLAT):
                tokens = held_ref[at, level, row].astype(jnp.float32)
                side = tokens[-SLON:].astype(jnp.bfloat16)
                if row < SLAT:
                    left_ref[at, level, row] = side
                else:
                    corner_ref[at, level, row - SLAT] = side
                    upper_ref[at, level, row - SLAT] = tokens[:-SLON].astype(jnp.bfloat16)


def join_kernel(own_ref, right_ref, lower_ref, corner_ref, out_ref, gin_ref):
    for at, ref in enumerate((out_ref, gin_ref)):
        for level in range(LEV):
            for row in range(WLAT):
                if row < SLAT:
                    body, side = own_ref[at, level, row], right_ref[at, level, row]
                else:
                    body, side = lower_ref[at, level, row - SLAT], corner_ref[at, level, row - SLAT]
                both = jnp.concatenate([body.astype(jnp.float32), side.astype(jnp.float32)], axis=0)
                ref[0, level, row] = both.astype(jnp.bfloat16)


def assemble(target_ref, at, own_ref, upper_ref, corner_ref, left_ref):
    pieces = ([], [])
    for level in range(LEV):
        for row in range(WLAT):
            if row < SLAT:
                side, body = corner_ref[at, level, row], upper_ref[at, level, row]
            else:
                side, body = left_ref[at, level, row - SLAT], own_ref[0, level, row - SLAT]
            side, body = side.astype(jnp.float32), body.astype(jnp.float32)
            pieces[0].append(side)
            pieces[0].append(body[:WLON - SLON])
            pieces[1].append(body[WLON - SLON:2 * WLON - SLON])
    for w in range(2):
        target_ref[w * WT:(w + 1) * WT, :] = jnp.concatenate(pieces[w], axis=0)


def statistics(x):
    center = jnp.mean(x, -1, keepdims=True)
    shifted = x - center
    inverse = lax.rsqrt(jnp.mean(shifted * shifted, -1, keepdims=True) + 1e-05)
    return shifted * inverse, inverse


def store_shares(target_ref, grads):
    count = grads.shape[0]
    first = lax.broadcasted_iota(jnp.int32, (count, 128), 0) % 8 < 4
    for quad in range(4):
        shares = ([], [])
        for pair in (2 * quad, 2 * quad + 1):
            left = grads[:, pair * 256:pair * 256 + 128]
            right = grads[:, pair * 256 + 128:pair * 256 + 256]
            shares[0].append(jnp.where(first, left, pltpu.roll(right, 4, 0)))
            shares[1].append(jnp.where(first, pltpu.roll(left, count - 4, 0), right))
        rows = slice(quad * 16, quad * 16 + 16)
        for which in range(2):
            piece = jnp.concatenate([p.reshape(count // 8, 8, 128) for p in shares[which]], axis=1)
            target_ref[:, which, rows, :] = piece.astype(target_ref.dtype)


def attention_kernel(
    own_x_ref, own_u_ref, upper_ref, corner_ref, left_ref, lrow_ref, lcol_ref, wqkv_ref, wproj_ref,
    send_ref, gp_ref, mix_ref, nkeep_ref, mkeep_ref, x_ref, u_ref,
    full_ref, proj_ref, gm_ref, nt_ref, mt_ref, mixt_ref, al_ref, gl_ref, s_ref, da_ref,
):
    windows = x_ref.shape[0] // WT
    core = lax.axis_index("core")
    half = D // 2
    assemble(full_ref, 1, own_u_ref, upper_ref, corner_ref, left_ref)
    u_ref[...] = full_ref[...].astype(jnp.bfloat16)
    assemble(full_ref, 0, own_x_ref, upper_ref, corner_ref, left_ref)
    x_ref[...] = full_ref[...].astype(jnp.bfloat16)
    normed, _ = statistics(full_ref[...])
    normed_low = normed.astype(jnp.bfloat16)
    proj_ref[...] = dot(normed_low, wqkv_ref[...]).astype(jnp.bfloat16)
    gm_ref[...] = dot(u_ref[...], wproj_ref[...], NT).astype(jnp.bfloat16)

    def place(target_ref, array):
        for b in range(D // 32):
            slot = lax.bitwise_xor(core, b % 2)
            row = pl.multiple_of(slot * half + (b // 2) * 32, 32)
            target_ref[pl.ds(row, 32), :] = array[b * 32:(b + 1) * 32, :]

    place(nt_ref, normed_low.T)

    lane = lax.broadcasted_iota(jnp.int32, (1, LANES), 1) // HD
    masks = [(lane == h).astype(jnp.float32) for h in range(PER)]
    low_masks = [m.astype(jnp.bfloat16) for m in masks]

    def stacked(array):
        return jnp.concatenate([array * m for m in low_masks], axis=0)

    def unstacked(array):
        total = array[:WT] * masks[0]
        for h in range(1, PER):
            total = total + array[h * WT:(h + 1) * WT] * masks[h]
        return total.astype(jnp.bfloat16)

    for w in range(windows):
        rows = slice(w * WT, (w + 1) * WT)
        allowed = lcol_ref[rows, :] == lrow_ref[w:w + 1, :]
        for g in range(UNITS):
            q_cols, k_cols, v_cols = (
                slice(part * D + g * LANES, part * D + (g + 1) * LANES) for part in range(3)
            )
            q = proj_ref[rows, q_cols]
            k = proj_ref[rows, k_cols]
            v = proj_ref[rows, v_cols]
            gm = gm_ref[rows, q_cols]
            s_ref[...] = dot(stacked(k), q, NT)
            da_ref[...] = dot(stacked(v), gm, NT)
            vt = v.T
            kt = k.T
            for h in range(PER):
                part = slice(h * WT, (h + 1) * WT)
                s = jnp.where(allowed, s_ref[part, :], jnp.float32(-1e30))
                e = jnp.exp2((s - jnp.max(s, 0, keepdims=True)) * jnp.float32(FACTOR * LOG2E))
                a = e * (1.0 / jnp.sum(e, 0, keepdims=True))
                al = a.astype(jnp.bfloat16)
                al_ref[part, :] = al
                ga = da_ref[part, :] * a
                gl = ((ga - a * jnp.sum(ga, 0, keepdims=True)) * jnp.float32(FACTOR)).astype(jnp.bfloat16)
                gl_ref[part, :] = gl
                chan = slice(g * LANES + h * HD, g * LANES + (h + 1) * HD)
                mixt_ref[chan, :] = dot(vt[h * HD:(h + 1) * HD, :], al)
                s_ref[h * HD:(h + 1) * HD, :] = dot(kt[h * HD:(h + 1) * HD, :], gl)
            gp_ref[rows, q_cols] = s_ref[:LANES, :].T.astype(jnp.bfloat16)
            gp_ref[rows, k_cols] = unstacked(dot(gl_ref[...], q))
            gp_ref[rows, v_cols] = unstacked(dot(al_ref[...], gm))
        mix_ref[rows, :] = mixt_ref[...].T.astype(jnp.bfloat16)

    place(mt_ref, mix_ref[...].T)
    nkeep_ref[...] = nt_ref[:half, :]
    mkeep_ref[...] = mt_ref[:half, :]
    grads = jnp.concatenate([dot(nt_ref[half:, :], gp_ref[...]), dot(mt_ref[half:, :], u_ref[...])], axis=1)
    store_shares(send_ref, grads)


def add_kernel(own_ref, got_ref, sum_ref):
    sum_ref[...] = (own_ref[...] + got_ref[...].astype(jnp.float32)).astype(jnp.bfloat16)


def added(parts_ref):
    total = parts_ref[0].astype(jnp.float32)
    for at in range(1, parts_ref.shape[0]):
        total = total + parts_ref[at].astype(jnp.float32)
    return total


def sum_kernel(parts_ref, sum_ref):
    total = added(parts_ref).astype(jnp.bfloat16)
    sum_ref[0] = total
    sum_ref[1] = total


def last_kernel(parts_ref, qkv_ref, proj_ref):
    total = added(parts_ref)
    for tile in range(16):
        piece = total[tile * 4:tile * 4 + 4, :]
        if tile < 12:
            qkv_ref[:, tile * 128:(tile + 1) * 128] = piece
        else:
            proj_ref[:, (tile - 12) * 128:(tile - 11) * 128] = piece


def stage_kernel(qkv_ref, proj_ref, qkv_out, proj_out, sems):
    copies = [
        pltpu.make_async_copy(qkv_ref, qkv_out, sems.at[0]),
        pltpu.make_async_copy(proj_ref, proj_out, sems.at[1]),
    ]
    for copy in copies:
        copy.start()
    for copy in copies:
        copy.wait()


def staged(w_qkv, w_proj):
    return pl.pallas_call(
        stage_kernel,
        out_shape=(
            pltpu.VMEM(w_qkv.shape, w_qkv.dtype),
            pltpu.VMEM(w_proj.shape, w_proj.dtype),
        ),
        in_specs=[pl.BlockSpec(memory_space=pltpu.HBM)] * 2,
        out_specs=(pl.BlockSpec(memory_space=pltpu.VMEM),) * 2,
        scratch_shapes=[pltpu.SemaphoreType.DMA((2,))],
        compiler_params=pltpu.CompilerParams(vmem_limit_bytes=4 * 1024 * 1024),
        cost_estimate=pl.CostEstimate(flops=0, bytes_accessed=4 * 1024 * 1024, transcendentals=0),
        name="stage_weights",
    )(w_qkv, w_proj)


def part(value, at, refs):
    own_ref, left_ref, upper_ref, corner_ref = refs
    for level in range(LEV):
        for row in range(WLAT):
            base = (level * WLAT + row) * WLON
            tokens = jnp.concatenate([value[base:base + WLON], value[WT + base:WT + base + WLON]], axis=0)
            side, body = tokens[:SLON].astype(jnp.bfloat16), tokens[SLON:].astype(jnp.bfloat16)
            if row < SLAT:
                corner_ref[at, level, row] = side
                upper_ref[at, level, row] = body
            else:
                left_ref[at, level, row - SLAT] = side
                own_ref[at, level, row - SLAT] = body


def rest_kernel(
    n_ref, m_ref, gp_ref, u_ref, x_ref, mix_ref, qkv_ref, proj_ref,
    half_ref, own_ref, left_ref, upper_ref, corner_ref,
    wqkv_ref, wproj_ref, sems,
):
    copies = [
        pltpu.make_async_copy(proj_ref, wproj_ref, sems.at[0]),
        pltpu.make_async_copy(qkv_ref, wqkv_ref, sems.at[1]),
    ]
    for copy in copies:
        copy.start()
    grads = jnp.concatenate([dot(n_ref[...], gp_ref[...]), dot(m_ref[...], u_ref[...])], axis=1)
    store_shares(half_ref, grads)
    refs = (own_ref, left_ref, upper_ref, corner_ref)
    x = x_ref[...].astype(jnp.float32)
    copies[0].wait()
    part(x + dot(mix_ref[...], wproj_ref[...]), 0, refs)
    normed, inverse = statistics(x)
    copies[1].wait()
    grad_normed = dot(gp_ref[...], wqkv_ref[...], NT)
    grad_tokens = inverse * (
        grad_normed
        - jnp.mean(grad_normed, -1, keepdims=True)
        - normed * jnp.mean(grad_normed * normed, -1, keepdims=True)
    )
    part(u_ref[...].astype(jnp.float32) + grad_tokens, 1, refs)


def call(kernel, name, outs, scratch, flops, *args, dtypes=None, limit=12, placed=False, any_args=()):
    vmem = pl.BlockSpec(memory_space=pltpu.VMEM)
    dtypes = dtypes or (jnp.bfloat16,) * len(outs)
    make = pltpu.VMEM if placed else jax.ShapeDtypeStruct
    size = sum(2 * math.prod(shape) for shape in outs)
    return pl.pallas_call(
        kernel,
        out_shape=tuple(make(shape, dtype) for shape, dtype in zip(outs, dtypes)),
        in_specs=[
            pl.BlockSpec(memory_space=pltpu.HBM) if at in any_args else vmem for at in range(len(args))
        ],
        out_specs=(vmem,) * len(outs),
        scratch_shapes=[
            pltpu.SemaphoreType.DMA(shape) if kind is None else pltpu.VMEM(shape, kind)
            for shape, kind in scratch
        ],
        compiler_params=pltpu.CompilerParams(vmem_limit_bytes=limit * 1024 * 1024),
        cost_estimate=pl.CostEstimate(flops=flops, bytes_accessed=2 * size, transcendentals=0),
        name=name,
    )(*args)


def attention(x, u, upper, corner, left, lrow, lcol, w_qkv, w_proj):
    tokens = math.prod(x.shape[:-1])
    low, full = jnp.bfloat16, jnp.float32
    return call(
        attention_kernel,
        "window_attention",
        (
            (32, 2, 64, 128), (tokens, 3 * D), (tokens, D),
            (D // 2, tokens), (D // 2, tokens), (tokens, D), (tokens, D),
        ),
        (
            ((tokens, D), full),
            ((tokens, 3 * D), low),
            ((tokens, D), low),
            ((D, tokens), low),
            ((D, tokens), low),
            ((D, WT), full),
            ((PER * WT, WT), low),
            ((PER * WT, WT), low),
            ((PER * WT, WT), full),
            ((PER * WT, WT), full),
        ),
        5_000_000_000,
        x, u, upper, corner, left, lrow, lcol, w_qkv, w_proj,
        limit=20,
    )


LAT = ("yh", "x", "core")


def passed_along(value, axis, steps):
    count = lax.axis_size(axis)
    pairs = [(source, (source + steps) % count) for source in range(count)]
    return lax.ppermute(value, axis, pairs)


def diagonal(value, steps):
    n_lat, n_lon = lax.axis_size(LAT), lax.axis_size("lon")
    pairs = [
        (a * n_lon + b, (a + steps) % n_lat * n_lon + (b + steps) % n_lon)
        for a in range(n_lat)
        for b in range(n_lon)
    ]
    return lax.ppermute(value, (*LAT, "lon"), pairs)


def per_device(inputs, cotangent, mask_ids, w_qkv, w_proj):
    body = (2, LEV, SLAT, inputs.shape[3] - SLON, D)
    side = (2, LEV, SLAT, SLON, D)
    upper, corner, left = call(
        cut_kernel, "cut_halos", (body, side, side),
        (((2, *inputs.shape[1:]), jnp.bfloat16), ((2, LEV), None)), 1000,
        *(pltpu.with_memory_space_constraint(array, pltpu.HBM) for array in (inputs, cotangent)),
        limit=8, any_args=(0, 1),
    )
    upper = passed_along(upper, LAT, 1)
    corner = diagonal(corner, 1)
    left = passed_along(left, "lon", 1)
    first_band = lax.axis_index(LAT) == 0
    wrapped = jnp.logical_and(first_band, jnp.arange(WLAT) < SLAT).astype(jnp.int32)
    groups = mask_ids + 4 * wrapped[:, None]
    windows = groups.shape[1] // WLON
    labels = groups.reshape(WLAT, windows, WLON).transpose(1, 0, 2).reshape(windows, WLAT * WLON)
    lrow = jnp.tile(labels, (1, LEV))
    lcol = lrow.reshape(windows * WT, 1)
    send, gp, mix, nkeep, mkeep, x, u = attention(
        inputs, cotangent, upper, corner, left, lrow, lcol, *staged(w_qkv, w_proj)
    )
    got = passed_along(send, "core", 1)
    half, own, left, upper, corner = call(
        rest_kernel, "own_half_and_outputs", (send.shape, body, side, body, side),
        ((w_qkv.shape, jnp.bfloat16), (w_proj.shape, jnp.bfloat16), ((2,), None)), 600_000_000,
        nkeep, mkeep, gp, u, x, mix, w_qkv, w_proj,
        dtypes=(jnp.float32,) + (jnp.bfloat16,) * 4, any_args=(6, 7), limit=16,
    )
    (sums,) = call(add_kernel, "add_halves", (send.shape,), (), 1_000_000, half, got, placed=True)
    own, left, upper, corner, sums = lax.optimization_barrier((own, left, upper, corner, sums))
    spread = lax.all_to_all(sums.reshape(8, 512, 128), ("yh", "x"), 0, 0, tiled=True)
    corner = diagonal(corner, -1)
    lower = passed_along(upper, LAT, -1)
    right = passed_along(left, "lon", -1)
    (sums,) = call(sum_kernel, "sum_parts", ((2, 512, 128),), (), 1_000_000, spread, placed=True)
    spread = lax.all_to_all(sums.reshape(16, 64, 128), ("dp", "lon"), 0, 0, tiled=True)
    grad_qkv, grad_proj = call(
        last_kernel, "last_sum", ((4, 3 * D), (4, D)), (), 1000, spread,
        dtypes=(jnp.float32,) * 2, limit=4,
    )
    output, grad_inputs = call(
        join_kernel, "join_outputs", (inputs.shape, inputs.shape), (), 1000,
        own, right, lower, corner, limit=8,
    )
    return (output, grad_inputs, grad_qkv, grad_proj)


def solution(mesh):
    mesh = Mesh(mesh.devices.reshape(2, 2, 4, 2, 8), ("dp", "yh", "x", "core", "lon"))
    tokens = P("dp", None, LAT, "lon", None)
    return jax.shard_map(
        per_device,
        mesh=mesh,
        in_specs=(tokens, tokens, P(LAT, "lon"), P(), P()),
        out_specs=(tokens, tokens, P((*LAT, "lon"), None), P((*LAT, "lon"), None)),
        check_vma=False,
    )
```

```python
import functools
import math

import jax
import jax.numpy as jnp
from jax import lax
from jax.experimental import pallas as pl
from jax.experimental.pallas import tpu as pltpu
from jax.sharding import Mesh
from jax.sharding import PartitionSpec as P

D = 512
HEADS = 16
HD = 32
LEV = 2
WLAT = 6
WLON = 12
SLAT = 3
SLON = 6
WT = LEV * WLAT * WLON
PER = 4
LANES = PER * HD
UNITS = D // LANES
FACTOR = 1.0 / math.sqrt(HD)
LOG2E = 1.4426950408889634

NN = (((1,), (0,)), ((), ()))
NT = (((1,), (1,)), ((), ()))


def dot(left, right, dims=NN):
    return lax.dot_general(left, right, dims, preferred_element_type=jnp.float32)


def cut_kernel(x_ref, u_ref, upper_ref, corner_ref, left_ref, held_ref, sems):
    copies = []
    for at, ref in enumerate((x_ref, u_ref)):
        for level in range(LEV):
            copies.append(pltpu.make_async_copy(ref.at[0, level], held_ref.at[at, level], sems.at[at, level]))
    for copy in copies:
        copy.start()
    for copy in copies:
        copy.wait()
    for at in range(2):
        for level in range(LEV):
            for row in range(WLAT):
                tokens = held_ref[at, level, row].astype(jnp.float32)
                side = tokens[-SLON:].astype(jnp.bfloat16)
                if row < SLAT:
                    left_ref[at, level, row] = side
                else:
                    corner_ref[at, level, row - SLAT] = side
                    upper_ref[at, level, row - SLAT] = tokens[:-SLON].astype(jnp.bfloat16)


def joined(body, side):
    both = jnp.concatenate([body.astype(jnp.float32), side.astype(jnp.float32)], axis=0)
    return both.astype(jnp.bfloat16)


def rows_kernel(own_ref, right_ref, rows_ref):
    for at in range(2):
        for level in range(LEV):
            for row in range(SLAT):
                rows_ref[at, level, row] = joined(own_ref[at, level, row], right_ref[at, level, row])


def join_kernel(own_ref, right_ref, lower_ref, out_ref, gin_ref):
    for at, ref in enumerate((out_ref, gin_ref)):
        for level in range(LEV):
            for row in range(SLAT):
                ref[0, level, row] = joined(own_ref[at, level, SLAT + row], right_ref[at, level, SLAT + row])
                ref[0, level, SLAT + row] = lower_ref[at, level, row]


def assemble(target_ref, at, own_ref, upper_ref, corner_ref, left_ref):
    pieces = ([], [])
    for level in range(LEV):
        for row in range(WLAT):
            if row < SLAT:
                side, body = corner_ref[at, level, row], upper_ref[at, level, row]
            else:
                side, body = left_ref[at, level, row - SLAT], own_ref[0, level, row - SLAT]
            side, body = side.astype(jnp.float32), body.astype(jnp.float32)
            pieces[0].append(side)
            pieces[0].append(body[:WLON - SLON])
            pieces[1].append(body[WLON - SLON:2 * WLON - SLON])
    for w in range(2):
        target_ref[w * WT:(w + 1) * WT, :] = jnp.concatenate(pieces[w], axis=0)


def statistics(x):
    center = jnp.mean(x, -1, keepdims=True)
    shifted = x - center
    inverse = lax.rsqrt(jnp.mean(shifted * shifted, -1, keepdims=True) + 1e-05)
    return shifted * inverse, inverse


def store_shares(target_ref, grads):
    count = grads.shape[0]
    first = lax.broadcasted_iota(jnp.int32, (count, 128), 0) % 8 < 4
    for quad in range(4):
        shares = ([], [])
        for pair in (2 * quad, 2 * quad + 1):
            left = grads[:, pair * 256:pair * 256 + 128]
            right = grads[:, pair * 256 + 128:pair * 256 + 256]
            shares[0].append(jnp.where(first, left, pltpu.roll(right, 4, 0)))
            shares[1].append(jnp.where(first, pltpu.roll(left, count - 4, 0), right))
        rows = slice(quad * 16, quad * 16 + 16)
        for which in range(2):
            piece = jnp.concatenate([p.reshape(count // 8, 8, 128) for p in shares[which]], axis=1)
            target_ref[:, which, rows, :] = piece.astype(target_ref.dtype)


def attention_kernel(
    own_x_ref, own_u_ref, upper_ref, corner_ref, left_ref, lrow_ref, lcol_ref, wqkv_ref, wproj_ref,
    send_ref, gp_ref, mix_ref, nkeep_ref, mkeep_ref, x_ref, u_ref,
    full_ref, proj_ref, gm_ref, nt_ref, mt_ref, mixt_ref, al_ref, gl_ref, s_ref, da_ref,
):
    windows = x_ref.shape[0] // WT
    core = lax.axis_index("core")
    half = D // 2
    assemble(full_ref, 1, own_u_ref, upper_ref, corner_ref, left_ref)
    u_ref[...] = full_ref[...].astype(jnp.bfloat16)
    assemble(full_ref, 0, own_x_ref, upper_ref, corner_ref, left_ref)
    x_ref[...] = full_ref[...].astype(jnp.bfloat16)
    normed, _ = statistics(full_ref[...])
    normed_low = normed.astype(jnp.bfloat16)
    proj_ref[...] = dot(normed_low, wqkv_ref[...]).astype(jnp.bfloat16)
    gm_ref[...] = dot(u_ref[...], wproj_ref[...], NT).astype(jnp.bfloat16)

    def place(target_ref, array):
        for b in range(D // 32):
            slot = lax.bitwise_xor(core, b % 2)
            row = pl.multiple_of(slot * half + (b // 2) * 32, 32)
            target_ref[pl.ds(row, 32), :] = array[b * 32:(b + 1) * 32, :]

    place(nt_ref, normed_low.T)

    lane = lax.broadcasted_iota(jnp.int32, (1, LANES), 1) // HD
    masks = [(lane == h).astype(jnp.float32) for h in range(PER)]
    low_masks = [m.astype(jnp.bfloat16) for m in masks]

    def stacked(array):
        return jnp.concatenate([array * m for m in low_masks], axis=0)

    def unstacked(array):
        total = array[:WT] * masks[0]
        for h in range(1, PER):
            total = total + array[h * WT:(h + 1) * WT] * masks[h]
        return total.astype(jnp.bfloat16)

    for w in range(windows):
        rows = slice(w * WT, (w + 1) * WT)
        allowed = lcol_ref[rows, :] == lrow_ref[w:w + 1, :]
        for g in range(UNITS):
            q_cols, k_cols, v_cols = (
                slice(part * D + g * LANES, part * D + (g + 1) * LANES) for part in range(3)
            )
            q = proj_ref[rows, q_cols]
            k = proj_ref[rows, k_cols]
            v = proj_ref[rows, v_cols]
            gm = gm_ref[rows, q_cols]
            s_ref[...] = dot(stacked(k), q, NT)
            da_ref[...] = dot(stacked(v), gm, NT)
            vt = v.T
            kt = k.T
            for h in range(PER):
                part = slice(h * WT, (h + 1) * WT)
                s = jnp.where(allowed, s_ref[part, :], jnp.float32(-1e30))
                e = jnp.exp2((s - jnp.max(s, 0, keepdims=True)) * jnp.float32(FACTOR * LOG2E))
                a = e * (1.0 / jnp.sum(e, 0, keepdims=True))
                al = a.astype(jnp.bfloat16)
                al_ref[part, :] = al
                ga = da_ref[part, :] * a
                gl = ((ga - a * jnp.sum(ga, 0, keepdims=True)) * jnp.float32(FACTOR)).astype(jnp.bfloat16)
                gl_ref[part, :] = gl
                chan = slice(g * LANES + h * HD, g * LANES + (h + 1) * HD)
                mixt_ref[chan, :] = dot(vt[h * HD:(h + 1) * HD, :], al)
                s_ref[h * HD:(h + 1) * HD, :] = dot(kt[h * HD:(h + 1) * HD, :], gl)
            gp_ref[rows, q_cols] = s_ref[:LANES, :].T.astype(jnp.bfloat16)
            gp_ref[rows, k_cols] = unstacked(dot(gl_ref[...], q))
            gp_ref[rows, v_cols] = unstacked(dot(al_ref[...], gm))
        mix_ref[rows, :] = mixt_ref[...].T.astype(jnp.bfloat16)

    place(mt_ref, mix_ref[...].T)
    nkeep_ref[...] = nt_ref[:half, :]
    mkeep_ref[...] = mt_ref[:half, :]
    grads = jnp.concatenate([dot(nt_ref[half:, :], gp_ref[...]), dot(mt_ref[half:, :], u_ref[...])], axis=1)
    store_shares(send_ref, grads)


def add_kernel(own_ref, got_ref, sum_ref):
    sum_ref[...] = (own_ref[...] + got_ref[...].astype(jnp.float32)).astype(jnp.bfloat16)


def added(parts_ref):
    total = parts_ref[0].astype(jnp.float32)
    for at in range(1, parts_ref.shape[0]):
        total = total + parts_ref[at].astype(jnp.float32)
    return total


def sum_kernel(parts_ref, sum_ref):
    total = added(parts_ref).astype(jnp.bfloat16)
    sum_ref[0] = total
    sum_ref[1] = total


def last_kernel(parts_ref, qkv_ref, proj_ref):
    total = added(parts_ref)
    for tile in range(16):
        piece = total[tile * 4:tile * 4 + 4, :]
        if tile < 12:
            qkv_ref[:, tile * 128:(tile + 1) * 128] = piece
        else:
            proj_ref[:, (tile - 12) * 128:(tile - 11) * 128] = piece


def stage_kernel(qkv_ref, proj_ref, qkv_out, proj_out, sems):
    copies = [
        pltpu.make_async_copy(qkv_ref, qkv_out, sems.at[0]),
        pltpu.make_async_copy(proj_ref, proj_out, sems.at[1]),
    ]
    for copy in copies:
        copy.start()
    for copy in copies:
        copy.wait()


def staged(w_qkv, w_proj):
    return pl.pallas_call(
        stage_kernel,
        out_shape=(
            pltpu.VMEM(w_qkv.shape, w_qkv.dtype),
            pltpu.VMEM(w_proj.shape, w_proj.dtype),
        ),
        in_specs=[pl.BlockSpec(memory_space=pltpu.HBM)] * 2,
        out_specs=(pl.BlockSpec(memory_space=pltpu.VMEM),) * 2,
        scratch_shapes=[pltpu.SemaphoreType.DMA((2,))],
        compiler_params=pltpu.CompilerParams(vmem_limit_bytes=4 * 1024 * 1024),
        cost_estimate=pl.CostEstimate(flops=0, bytes_accessed=4 * 1024 * 1024, transcendentals=0),
        name="stage_weights",
    )(w_qkv, w_proj)


def part(value, at, refs):
    own_ref, left_ref = refs
    for level in range(LEV):
        for row in range(WLAT):
            base = (level * WLAT + row) * WLON
            tokens = jnp.concatenate([value[base:base + WLON], value[WT + base:WT + base + WLON]], axis=0)
            left_ref[at, level, row] = tokens[:SLON].astype(jnp.bfloat16)
            own_ref[at, level, row] = tokens[SLON:].astype(jnp.bfloat16)


def rest_kernel(
    n_ref, m_ref, gp_ref, u_ref, x_ref, mix_ref, qkv_ref, proj_ref,
    half_ref, own_ref, left_ref,
    wqkv_ref, wproj_ref, sems,
):
    copies = [
        pltpu.make_async_copy(proj_ref, wproj_ref, sems.at[0]),
        pltpu.make_async_copy(qkv_ref, wqkv_ref, sems.at[1]),
    ]
    for copy in copies:
        copy.start()
    grads = jnp.concatenate([dot(n_ref[...], gp_ref[...]), dot(m_ref[...], u_ref[...])], axis=1)
    store_shares(half_ref, grads)
    refs = (own_ref, left_ref)
    x = x_ref[...].astype(jnp.float32)
    copies[0].wait()
    part(x + dot(mix_ref[...], wproj_ref[...]), 0, refs)
    normed, inverse = statistics(x)
    copies[1].wait()
    grad_normed = dot(gp_ref[...], wqkv_ref[...], NT)
    grad_tokens = inverse * (
        grad_normed
        - jnp.mean(grad_normed, -1, keepdims=True)
        - normed * jnp.mean(grad_normed * normed, -1, keepdims=True)
    )
    part(u_ref[...].astype(jnp.float32) + grad_tokens, 1, refs)


def call(kernel, name, outs, scratch, flops, *args, dtypes=None, limit=12, placed=False, any_args=()):
    vmem = pl.BlockSpec(memory_space=pltpu.VMEM)
    dtypes = dtypes or (jnp.bfloat16,) * len(outs)
    make = pltpu.VMEM if placed else jax.ShapeDtypeStruct
    size = sum(2 * math.prod(shape) for shape in outs)
    return pl.pallas_call(
        kernel,
        out_shape=tuple(make(shape, dtype) for shape, dtype in zip(outs, dtypes)),
        in_specs=[
            pl.BlockSpec(memory_space=pltpu.HBM) if at in any_args else vmem for at in range(len(args))
        ],
        out_specs=(vmem,) * len(outs),
        scratch_shapes=[
            pltpu.SemaphoreType.DMA(shape) if kind is None else pltpu.VMEM(shape, kind)
            for shape, kind in scratch
        ],
        compiler_params=pltpu.CompilerParams(vmem_limit_bytes=limit * 1024 * 1024),
        cost_estimate=pl.CostEstimate(flops=flops, bytes_accessed=2 * size, transcendentals=0),
        name=name,
    )(*args)


def attention(x, u, upper, corner, left, lrow, lcol, w_qkv, w_proj):
    tokens = math.prod(x.shape[:-1])
    low, full = jnp.bfloat16, jnp.float32
    return call(
        attention_kernel,
        "window_attention",
        (
            (32, 2, 64, 128), (tokens, 3 * D), (tokens, D),
            (D // 2, tokens), (D // 2, tokens), (tokens, D), (tokens, D),
        ),
        (
            ((tokens, D), full),
            ((tokens, 3 * D), low),
            ((tokens, D), low),
            ((D, tokens), low),
            ((D, tokens), low),
            ((D, WT), full),
            ((PER * WT, WT), low),
            ((PER * WT, WT), low),
            ((PER * WT, WT), full),
            ((PER * WT, WT), full),
        ),
        5_000_000_000,
        x, u, upper, corner, left, lrow, lcol, w_qkv, w_proj,
        limit=20,
    )


LAT = ("yh", "x", "core")


def passed_along(value, axis, steps):
    count = lax.axis_size(axis)
    pairs = [(source, (source + steps) % count) for source in range(count)]
    return lax.ppermute(value, axis, pairs)


def diagonal(value, steps):
    n_lat, n_lon = lax.axis_size(LAT), lax.axis_size("lon")
    pairs = [
        (a * n_lon + b, (a + steps) % n_lat * n_lon + (b + steps) % n_lon)
        for a in range(n_lat)
        for b in range(n_lon)
    ]
    return lax.ppermute(value, (*LAT, "lon"), pairs)


def per_device(inputs, cotangent, mask_ids, w_qkv, w_proj):
    body = (2, LEV, SLAT, inputs.shape[3] - SLON, D)
    side = (2, LEV, SLAT, SLON, D)
    upper, corner, left = call(
        cut_kernel, "cut_halos", (body, side, side),
        (((2, *inputs.shape[1:]), jnp.bfloat16), ((2, LEV), None)), 1000,
        *(pltpu.with_memory_space_constraint(array, pltpu.HBM) for array in (inputs, cotangent)),
        limit=8, any_args=(0, 1),
    )
    upper = passed_along(upper, LAT, 1)
    corner = diagonal(corner, 1)
    left = passed_along(left, "lon", 1)
    first_band = lax.axis_index(LAT) == 0
    wrapped = jnp.logical_and(first_band, jnp.arange(WLAT) < SLAT).astype(jnp.int32)
    groups = mask_ids + 4 * wrapped[:, None]
    windows = groups.shape[1] // WLON
    labels = groups.reshape(WLAT, windows, WLON).transpose(1, 0, 2).reshape(windows, WLAT * WLON)
    lrow = jnp.tile(labels, (1, LEV))
    lcol = lrow.reshape(windows * WT, 1)
    send, gp, mix, nkeep, mkeep, x, u = attention(
        inputs, cotangent, upper, corner, left, lrow, lcol, *staged(w_qkv, w_proj)
    )
    got = passed_along(send, "core", 1)
    half, own, left = call(
        rest_kernel, "own_half_and_outputs",
        (send.shape, (2, *inputs.shape[1:3], body[3], D), (2, *inputs.shape[1:3], SLON, D)),
        ((w_qkv.shape, jnp.bfloat16), (w_proj.shape, jnp.bfloat16), ((2,), None)), 600_000_000,
        nkeep, mkeep, gp, u, x, mix, w_qkv, w_proj,
        dtypes=(jnp.float32,) + (jnp.bfloat16,) * 2, any_args=(6, 7), limit=16,
    )
    (sums,) = call(add_kernel, "add_halves", (send.shape,), (), 1_000_000, half, got, placed=True)
    right = passed_along(left, "lon", -1)
    spread = lax.all_to_all(sums.reshape(8, 512, 128), ("yh", "x"), 0, 0, tiled=True)
    spread, right = lax.optimization_barrier((spread, right))
    (sums,) = call(sum_kernel, "sum_parts", ((2, 512, 128),), (), 1_000_000, spread, placed=True)
    spread = lax.all_to_all(sums.reshape(16, 64, 128), ("dp", "lon"), 0, 0, tiled=True)
    grad_qkv, grad_proj = call(
        last_kernel, "last_sum", ((4, 3 * D), (4, D)), (), 1000, spread,
        dtypes=(jnp.float32,) * 2, limit=4,
    )
    (rows,) = call(rows_kernel, "halo_rows", ((2, LEV, SLAT, *inputs.shape[3:]),), (), 1000, own, right, limit=8)
    lower = passed_along(rows, LAT, -1)
    output, grad_inputs = call(
        join_kernel, "join_outputs", (inputs.shape, inputs.shape), (), 1000, own, right, lower, limit=8
    )
    return (output, grad_inputs, grad_qkv, grad_proj)


def solution(mesh):
    mesh = Mesh(mesh.devices.reshape(2, 2, 4, 2, 8), ("dp", "yh", "x", "core", "lon"))
    tokens = P("dp", None, LAT, "lon", None)
    return jax.shard_map(
        per_device,
        mesh=mesh,
        in_specs=(tokens, tokens, P(LAT, "lon"), P(), P()),
        out_specs=(tokens, tokens, P((*LAT, "lon"), None), P((*LAT, "lon"), None)),
        check_vma=False,
    )
```

```python
import functools
import math

import jax
import jax.numpy as jnp
from jax import lax
from jax.experimental import pallas as pl
from jax.experimental.pallas import tpu as pltpu
from jax.sharding import Mesh
from jax.sharding import PartitionSpec as P

D = 512
HEADS = 16
HD = 32
LEV = 2
WLAT = 6
WLON = 12
SLAT = 3
SLON = 6
WT = LEV * WLAT * WLON
PER = 8
LANES = PER * HD
MAIN = 128
REST = WT - MAIN
WIDE = PER * WT
UNITS = D // LANES
FACTOR = 1.0 / math.sqrt(HD)
LOG2E = 1.4426950408889634

NN = (((1,), (0,)), ((), ()))
NT = (((1,), (1,)), ((), ()))


def dot(left, right, dims=NN):
    return lax.dot_general(left, right, dims, preferred_element_type=jnp.float32)


def cut_kernel(x_ref, u_ref, upper_ref, corner_ref, left_ref, held_ref, sems):
    copies = []
    for at, ref in enumerate((x_ref, u_ref)):
        for level in range(LEV):
            copies.append(pltpu.make_async_copy(ref.at[0, level], held_ref.at[at, level], sems.at[at, level]))
    for copy in copies:
        copy.start()
    for copy in copies:
        copy.wait()
    for at in range(2):
        for level in range(LEV):
            for row in range(WLAT):
                tokens = held_ref[at, level, row].astype(jnp.float32)
                side = tokens[-SLON:].astype(jnp.bfloat16)
                if row < SLAT:
                    left_ref[at, level, row] = side
                else:
                    corner_ref[at, level, row - SLAT] = side
                    upper_ref[at, level, row - SLAT] = tokens[:-SLON].astype(jnp.bfloat16)


def joined(body, side):
    both = jnp.concatenate([body.astype(jnp.float32), side.astype(jnp.float32)], axis=0)
    return both.astype(jnp.bfloat16)


def rows_kernel(own_ref, right_ref, rows_ref):
    for at in range(2):
        for level in range(LEV):
            for row in range(SLAT):
                rows_ref[at, level, row] = joined(own_ref[at, level, row], right_ref[at, level, row])


def join_kernel(own_ref, right_ref, lower_ref, out_ref, gin_ref):
    for at, ref in enumerate((out_ref, gin_ref)):
        for level in range(LEV):
            for row in range(SLAT):
                ref[0, level, row] = joined(own_ref[at, level, SLAT + row], right_ref[at, level, SLAT + row])
                ref[0, level, SLAT + row] = lower_ref[at, level, row]


def assemble(target_ref, at, own_ref, upper_ref, corner_ref, left_ref):
    pieces = ([], [])
    for level in range(LEV):
        for row in range(WLAT):
            if row < SLAT:
                side, body = corner_ref[at, level, row], upper_ref[at, level, row]
            else:
                side, body = left_ref[at, level, row - SLAT], own_ref[0, level, row - SLAT]
            side, body = side.astype(jnp.float32), body.astype(jnp.float32)
            pieces[0].append(side)
            pieces[0].append(body[:WLON - SLON])
            pieces[1].append(body[WLON - SLON:2 * WLON - SLON])
    for w in range(2):
        target_ref[w * WT:(w + 1) * WT, :] = jnp.concatenate(pieces[w], axis=0)


def statistics(x):
    center = jnp.mean(x, -1, keepdims=True)
    shifted = x - center
    inverse = lax.rsqrt(jnp.mean(shifted * shifted, -1, keepdims=True) + 1e-05)
    return shifted * inverse, inverse


def store_shares(target_ref, grads):
    count = grads.shape[0]
    first = lax.broadcasted_iota(jnp.int32, (count, 128), 0) % 8 < 4
    for quad in range(4):
        shares = ([], [])
        for pair in (2 * quad, 2 * quad + 1):
            left = grads[:, pair * 256:pair * 256 + 128]
            right = grads[:, pair * 256 + 128:pair * 256 + 256]
            shares[0].append(jnp.where(first, left, pltpu.roll(right, 4, 0)))
            shares[1].append(jnp.where(first, pltpu.roll(left, count - 4, 0), right))
        rows = slice(quad * 16, quad * 16 + 16)
        for which in range(2):
            piece = jnp.concatenate([p.reshape(count // 8, 8, 128) for p in shares[which]], axis=1)
            target_ref[:, which, rows, :] = piece.astype(target_ref.dtype)


def attention_kernel(
    own_x_ref, own_u_ref, upper_ref, corner_ref, left_ref, lrow_ref, lcol_ref, wqkv_ref, wproj_ref,
    send_ref, gp_ref, mix_ref, nkeep_ref, mkeep_ref, x_ref, u_ref,
    full_ref, proj_ref, gm_ref, nt_ref, mt_ref, al_ref, gl_ref, s_ref, da_ref, qs_ref, gs_ref,
):
    windows = x_ref.shape[0] // WT
    core = lax.axis_index("core")
    half = D // 2
    assemble(full_ref, 1, own_u_ref, upper_ref, corner_ref, left_ref)
    u_ref[...] = full_ref[...].astype(jnp.bfloat16)
    assemble(full_ref, 0, own_x_ref, upper_ref, corner_ref, left_ref)
    x_ref[...] = full_ref[...].astype(jnp.bfloat16)
    normed, _ = statistics(full_ref[...])
    normed_low = normed.astype(jnp.bfloat16)
    proj_ref[...] = dot(normed_low, wqkv_ref[...]).astype(jnp.bfloat16)
    gm_ref[...] = dot(u_ref[...], wproj_ref[...], NT).astype(jnp.bfloat16)

    def place(target_ref, array):
        for b in range(D // 32):
            slot = lax.bitwise_xor(core, b % 2)
            row = pl.multiple_of(slot * half + (b // 2) * 32, 32)
            target_ref[pl.ds(row, 32), :] = array[b * 32:(b + 1) * 32, :]

    place(nt_ref, normed_low.T)

    lane = lax.broadcasted_iota(jnp.int32, (1, LANES), 1) // HD
    masks = [(lane == h).astype(jnp.float32) for h in range(PER)]
    low_masks = [m.astype(jnp.bfloat16) for m in masks]
    tiles = [slice(t * MAIN, (t + 1) * MAIN) for t in range(PER + 1)]

    def stack(target_ref, array):
        for h in range(PER):
            target_ref[tiles[h], :] = array[:MAIN] * low_masks[h]
            rest = PER * MAIN + h * REST
            target_ref[rest:rest + REST, :] = array[MAIN:] * low_masks[h]

    def mix(target_ref, rows, cols, left, weights_ref):
        turned = left.T
        for pair in range(PER // 2):
            both = slice(pair * 2 * MAIN, (pair + 1) * 2 * MAIN)
            mixed = dot(turned[pair * 2 * HD:(pair + 1) * 2 * HD, :], weights_ref[:, both])
            s_ref[pair * 2 * HD:pair * 2 * HD + HD, :MAIN] = mixed[:HD, :MAIN]
            s_ref[pair * 2 * HD + HD:(pair + 1) * 2 * HD, :MAIN] = mixed[HD:, MAIN:]
        rest = dot(weights_ref[:, tiles[PER]].T, left)
        total = rest[:REST] * masks[0]
        for h in range(1, PER):
            total = total + rest[h * REST:(h + 1) * REST] * masks[h]
        target_ref[rows.start:rows.start + MAIN, cols] = s_ref[:LANES, :MAIN].T.astype(jnp.bfloat16)
        target_ref[rows.start + MAIN:rows.stop, cols] = total.astype(jnp.bfloat16)

    for w in range(windows):
        rows = slice(w * WT, (w + 1) * WT)
        labels = lcol_ref[rows, :]
        allowed = [labels == lrow_ref[w:w + 1, tiles[at]] for at in range(2)]
        for g in range(UNITS):
            q_cols, k_cols, v_cols = (
                slice(part * D + g * LANES, part * D + (g + 1) * LANES) for part in range(3)
            )
            k = proj_ref[rows, k_cols]
            v = proj_ref[rows, v_cols]
            stack(qs_ref, proj_ref[rows, q_cols])
            stack(gs_ref, gm_ref[rows, q_cols])
            s_ref[:WT, :] = dot(k, qs_ref[...], NT)
            da_ref[...] = dot(v, gs_ref[...], NT)
            for t in range(PER + 1):
                s = jnp.where(allowed[t // PER], s_ref[:WT, tiles[t]], jnp.float32(-1e30))
                e = jnp.exp2((s - jnp.max(s, 0, keepdims=True)) * jnp.float32(FACTOR * LOG2E))
                a = e * (1.0 / jnp.sum(e, 0, keepdims=True))
                al_ref[:, tiles[t]] = a.astype(jnp.bfloat16)
                ga = da_ref[:, tiles[t]] * a
                gl = (ga - a * jnp.sum(ga, 0, keepdims=True)) * jnp.float32(FACTOR)
                gl_ref[:, tiles[t]] = gl.astype(jnp.bfloat16)
            gp_ref[rows, k_cols] = dot(gl_ref[...], qs_ref[...]).astype(jnp.bfloat16)
            gp_ref[rows, v_cols] = dot(al_ref[...], gs_ref[...]).astype(jnp.bfloat16)
            mix(mix_ref, rows, q_cols, v, al_ref)
            mix(gp_ref, rows, q_cols, k, gl_ref)

    place(mt_ref, mix_ref[...].T)
    nkeep_ref[...] = nt_ref[:half, :]
    mkeep_ref[...] = mt_ref[:half, :]
    grads = jnp.concatenate([dot(nt_ref[half:, :], gp_ref[...]), dot(mt_ref[half:, :], u_ref[...])], axis=1)
    store_shares(send_ref, grads)


def add_kernel(own_ref, got_ref, sum_ref):
    sum_ref[...] = (own_ref[...] + got_ref[...].astype(jnp.float32)).astype(jnp.bfloat16)


def added(parts_ref):
    total = parts_ref[0].astype(jnp.float32)
    for at in range(1, parts_ref.shape[0]):
        total = total + parts_ref[at].astype(jnp.float32)
    return total


def sum_kernel(parts_ref, sum_ref):
    total = added(parts_ref).astype(jnp.bfloat16)
    sum_ref[0] = total
    sum_ref[1] = total


def last_kernel(parts_ref, qkv_ref, proj_ref):
    total = added(parts_ref)
    for tile in range(16):
        piece = total[tile * 4:tile * 4 + 4, :]
        if tile < 12:
            qkv_ref[:, tile * 128:(tile + 1) * 128] = piece
        else:
            proj_ref[:, (tile - 12) * 128:(tile - 11) * 128] = piece


def stage_kernel(qkv_ref, proj_ref, qkv_out, proj_out, sems):
    copies = [
        pltpu.make_async_copy(qkv_ref, qkv_out, sems.at[0]),
        pltpu.make_async_copy(proj_ref, proj_out, sems.at[1]),
    ]
    for copy in copies:
        copy.start()
    for copy in copies:
        copy.wait()


def staged(w_qkv, w_proj):
    return pl.pallas_call(
        stage_kernel,
        out_shape=(
            pltpu.VMEM(w_qkv.shape, w_qkv.dtype),
            pltpu.VMEM(w_proj.shape, w_proj.dtype),
        ),
        in_specs=[pl.BlockSpec(memory_space=pltpu.HBM)] * 2,
        out_specs=(pl.BlockSpec(memory_space=pltpu.VMEM),) * 2,
        scratch_shapes=[pltpu.SemaphoreType.DMA((2,))],
        compiler_params=pltpu.CompilerParams(vmem_limit_bytes=4 * 1024 * 1024),
        cost_estimate=pl.CostEstimate(flops=0, bytes_accessed=4 * 1024 * 1024, transcendentals=0),
        name="stage_weights",
    )(w_qkv, w_proj)


def part(value, at, refs):
    own_ref, left_ref = refs
    for level in range(LEV):
        for row in range(WLAT):
            base = (level * WLAT + row) * WLON
            tokens = jnp.concatenate([value[base:base + WLON], value[WT + base:WT + base + WLON]], axis=0)
            left_ref[at, level, row] = tokens[:SLON].astype(jnp.bfloat16)
            own_ref[at, level, row] = tokens[SLON:].astype(jnp.bfloat16)


def rest_kernel(
    n_ref, m_ref, gp_ref, u_ref, x_ref, mix_ref, qkv_ref, proj_ref,
    half_ref, own_ref, left_ref,
    wqkv_ref, wproj_ref, sems,
):
    copies = [
        pltpu.make_async_copy(proj_ref, wproj_ref, sems.at[0]),
        pltpu.make_async_copy(qkv_ref, wqkv_ref, sems.at[1]),
    ]
    for copy in copies:
        copy.start()
    grads = jnp.concatenate([dot(n_ref[...], gp_ref[...]), dot(m_ref[...], u_ref[...])], axis=1)
    store_shares(half_ref, grads)
    refs = (own_ref, left_ref)
    x = x_ref[...].astype(jnp.float32)
    copies[0].wait()
    part(x + dot(mix_ref[...], wproj_ref[...]), 0, refs)
    normed, inverse = statistics(x)
    copies[1].wait()
    grad_normed = dot(gp_ref[...], wqkv_ref[...], NT)
    grad_tokens = inverse * (
        grad_normed
        - jnp.mean(grad_normed, -1, keepdims=True)
        - normed * jnp.mean(grad_normed * normed, -1, keepdims=True)
    )
    part(u_ref[...].astype(jnp.float32) + grad_tokens, 1, refs)


def call(kernel, name, outs, scratch, flops, *args, dtypes=None, limit=12, placed=False, any_args=()):
    vmem = pl.BlockSpec(memory_space=pltpu.VMEM)
    dtypes = dtypes or (jnp.bfloat16,) * len(outs)
    make = pltpu.VMEM if placed else jax.ShapeDtypeStruct
    size = sum(2 * math.prod(shape) for shape in outs)
    return pl.pallas_call(
        kernel,
        out_shape=tuple(make(shape, dtype) for shape, dtype in zip(outs, dtypes)),
        in_specs=[
            pl.BlockSpec(memory_space=pltpu.HBM) if at in any_args else vmem for at in range(len(args))
        ],
        out_specs=(vmem,) * len(outs),
        scratch_shapes=[
            pltpu.SemaphoreType.DMA(shape) if kind is None else pltpu.VMEM(shape, kind)
            for shape, kind in scratch
        ],
        compiler_params=pltpu.CompilerParams(vmem_limit_bytes=limit * 1024 * 1024),
        cost_estimate=pl.CostEstimate(flops=flops, bytes_accessed=2 * size, transcendentals=0),
        name=name,
    )(*args)


def attention(x, u, upper, corner, left, lrow, lcol, w_qkv, w_proj):
    tokens = math.prod(x.shape[:-1])
    low, full = jnp.bfloat16, jnp.float32
    return call(
        attention_kernel,
        "window_attention",
        (
            (32, 2, 64, 128), (tokens, 3 * D), (tokens, D),
            (D // 2, tokens), (D // 2, tokens), (tokens, D), (tokens, D),
        ),
        (
            ((tokens, D), full),
            ((tokens, 3 * D), low),
            ((tokens, D), low),
            ((D, tokens), low),
            ((D, tokens), low),
            ((WT, WIDE), low),
            ((WT, WIDE), low),
            ((LANES, WIDE), full),
            ((WT, WIDE), full),
            ((WIDE, LANES), low),
            ((WIDE, LANES), low),
        ),
        5_000_000_000,
        x, u, upper, corner, left, lrow, lcol, w_qkv, w_proj,
        limit=20,
    )


LAT = ("yh", "x", "core")


def passed_along(value, axis, steps):
    count = lax.axis_size(axis)
    pairs = [(source, (source + steps) % count) for source in range(count)]
    return lax.ppermute(value, axis, pairs)


def diagonal(value, steps):
    n_lat, n_lon = lax.axis_size(LAT), lax.axis_size("lon")
    pairs = [
        (a * n_lon + b, (a + steps) % n_lat * n_lon + (b + steps) % n_lon)
        for a in range(n_lat)
        for b in range(n_lon)
    ]
    return lax.ppermute(value, (*LAT, "lon"), pairs)


def per_device(inputs, cotangent, mask_ids, w_qkv, w_proj):
    body = (2, LEV, SLAT, inputs.shape[3] - SLON, D)
    side = (2, LEV, SLAT, SLON, D)
    upper, corner, left = call(
        cut_kernel, "cut_halos", (body, side, side),
        (((2, *inputs.shape[1:]), jnp.bfloat16), ((2, LEV), None)), 1000,
        *(pltpu.with_memory_space_constraint(array, pltpu.HBM) for array in (inputs, cotangent)),
        limit=8, any_args=(0, 1),
    )
    upper = passed_along(upper, LAT, 1)
    corner = diagonal(corner, 1)
    left = passed_along(left, "lon", 1)
    first_band = lax.axis_index(LAT) == 0
    wrapped = jnp.logical_and(first_band, jnp.arange(WLAT) < SLAT).astype(jnp.int32)
    groups = mask_ids + 4 * wrapped[:, None]
    windows = groups.shape[1] // WLON
    labels = groups.reshape(WLAT, windows, WLON).transpose(1, 0, 2).reshape(windows, WLAT * WLON)
    labels = jnp.tile(labels, (1, LEV))
    lcol = labels.reshape(windows * WT, 1)
    lrow = jnp.concatenate([labels[:, :MAIN], jnp.tile(labels[:, MAIN:], (1, PER))], axis=1)
    send, gp, mix, nkeep, mkeep, x, u = attention(
        inputs, cotangent, upper, corner, left, lrow, lcol, *staged(w_qkv, w_proj)
    )
    got = passed_along(send, "core", 1)
    half, own, left = call(
        rest_kernel, "own_half_and_outputs",
        (send.shape, (2, *inputs.shape[1:3], body[3], D), (2, *inputs.shape[1:3], SLON, D)),
        ((w_qkv.shape, jnp.bfloat16), (w_proj.shape, jnp.bfloat16), ((2,), None)), 600_000_000,
        nkeep, mkeep, gp, u, x, mix, w_qkv, w_proj,
        dtypes=(jnp.float32,) + (jnp.bfloat16,) * 2, any_args=(6, 7), limit=16,
    )
    (sums,) = call(add_kernel, "add_halves", (send.shape,), (), 1_000_000, half, got, placed=True)
    right = passed_along(left, "lon", -1)
    spread = lax.all_to_all(sums.reshape(8, 512, 128), ("yh", "x"), 0, 0, tiled=True)
    spread, right = lax.optimization_barrier((spread, right))
    (sums,) = call(sum_kernel, "sum_parts", ((2, 512, 128),), (), 1_000_000, spread, placed=True)
    spread = lax.all_to_all(sums.reshape(16, 64, 128), ("dp", "lon"), 0, 0, tiled=True)
    grad_qkv, grad_proj = call(
        last_kernel, "last_sum", ((4, 3 * D), (4, D)), (), 1000, spread,
        dtypes=(jnp.float32,) * 2, limit=4,
    )
    (rows,) = call(rows_kernel, "halo_rows", ((2, LEV, SLAT, *inputs.shape[3:]),), (), 1000, own, right, limit=8)
    lower = passed_along(rows, LAT, -1)
    output, grad_inputs = call(
        join_kernel, "join_outputs", (inputs.shape, inputs.shape), (), 1000, own, right, lower, limit=8
    )
    return (output, grad_inputs, grad_qkv, grad_proj)


def solution(mesh):
    mesh = Mesh(mesh.devices.reshape(2, 2, 4, 2, 8), ("dp", "yh", "x", "core", "lon"))
    tokens = P("dp", None, LAT, "lon", None)
    return jax.shard_map(
        per_device,
        mesh=mesh,
        in_specs=(tokens, tokens, P(LAT, "lon"), P(), P()),
        out_specs=(tokens, tokens, P((*LAT, "lon"), None), P((*LAT, "lon"), None)),
        check_vma=False,
    )
```

```python
import functools
import math

import jax
import jax.numpy as jnp
from jax import lax
from jax.experimental import pallas as pl
from jax.experimental.pallas import tpu as pltpu
from jax.sharding import Mesh
from jax.sharding import PartitionSpec as P

D = 512
HEADS = 16
HD = 32
LEV = 2
WLAT = 6
WLON = 12
SLAT = 3
SLON = 6
WT = LEV * WLAT * WLON
PER = 8
LANES = PER * HD
MAIN = 128
REST = WT - MAIN
WIDE = PER * WT
UNITS = D // LANES
FACTOR = 1.0 / math.sqrt(HD)
LOG2E = 1.4426950408889634

NN = (((1,), (0,)), ((), ()))
NT = (((1,), (1,)), ((), ()))


def dot(left, right, dims=NN):
    return lax.dot_general(left, right, dims, preferred_element_type=jnp.float32)


def cut_kernel(x_ref, u_ref, upper_ref, corner_ref, left_ref, held_ref, sems):
    copies = []
    for at, ref in enumerate((x_ref, u_ref)):
        for level in range(LEV):
            copies.append(pltpu.make_async_copy(ref.at[0, level], held_ref.at[at, level], sems.at[at, level]))
    for copy in copies:
        copy.start()
    for copy in copies:
        copy.wait()
    for at in range(2):
        for level in range(LEV):
            for row in range(WLAT):
                tokens = held_ref[at, level, row].astype(jnp.float32)
                side = tokens[-SLON:].astype(jnp.bfloat16)
                if row < SLAT:
                    left_ref[at, level, row] = side
                else:
                    corner_ref[at, level, row - SLAT] = side
                    upper_ref[at, level, row - SLAT] = tokens[:-SLON].astype(jnp.bfloat16)


def joined(body, side):
    both = jnp.concatenate([body.astype(jnp.float32), side.astype(jnp.float32)], axis=0)
    return both.astype(jnp.bfloat16)


def rows_kernel(own_ref, right_ref, rows_ref):
    for at in range(2):
        for level in range(LEV):
            for row in range(SLAT):
                rows_ref[at, level, row] = joined(own_ref[at, level, row], right_ref[at, level, row])


def join_kernel(own_ref, right_ref, lower_ref, out_ref, gin_ref):
    for at, ref in enumerate((out_ref, gin_ref)):
        for level in range(LEV):
            for row in range(SLAT):
                ref[0, level, row] = joined(own_ref[at, level, SLAT + row], right_ref[at, level, SLAT + row])
                ref[0, level, SLAT + row] = lower_ref[at, level, row]


def assemble(target_ref, at, own_ref, upper_ref, corner_ref, left_ref):
    pieces = ([], [])
    for level in range(LEV):
        for row in range(WLAT):
            if row < SLAT:
                side, body = corner_ref[at, level, row], upper_ref[at, level, row]
            else:
                side, body = left_ref[at, level, row - SLAT], own_ref[0, level, row - SLAT]
            side, body = side.astype(jnp.float32), body.astype(jnp.float32)
            pieces[0].append(side)
            pieces[0].append(body[:WLON - SLON])
            pieces[1].append(body[WLON - SLON:2 * WLON - SLON])
    for w in range(2):
        target_ref[w * WT:(w + 1) * WT, :] = jnp.concatenate(pieces[w], axis=0)


def statistics(x):
    center = jnp.mean(x, -1, keepdims=True)
    shifted = x - center
    inverse = lax.rsqrt(jnp.mean(shifted * shifted, -1, keepdims=True) + 1e-05)
    return shifted * inverse, inverse


def store_shares(target_ref, grads):
    count = grads.shape[0]
    first = lax.broadcasted_iota(jnp.int32, (count, 128), 0) % 8 < 4
    for quad in range(4):
        shares = ([], [])
        for pair in (2 * quad, 2 * quad + 1):
            left = grads[:, pair * 256:pair * 256 + 128]
            right = grads[:, pair * 256 + 128:pair * 256 + 256]
            shares[0].append(jnp.where(first, left, pltpu.roll(right, 4, 0)))
            shares[1].append(jnp.where(first, pltpu.roll(left, count - 4, 0), right))
        rows = slice(quad * 16, quad * 16 + 16)
        for which in range(2):
            piece = jnp.concatenate([p.reshape(count // 8, 8, 128) for p in shares[which]], axis=1)
            target_ref[:, which, rows, :] = piece.astype(target_ref.dtype)


def attention_kernel(
    own_x_ref, own_u_ref, upper_ref, corner_ref, left_ref, lrow_ref, lcol_ref, wqkv_ref, wproj_ref,
    send_ref, gp_ref, mix_ref, nkeep_ref, mkeep_ref, x_ref, u_ref,
    full_ref, proj_ref, gm_ref, nt_ref, mt_ref, al_ref, gl_ref, s_ref, da_ref, qs_ref, gs_ref,
):
    windows = x_ref.shape[0] // WT
    core = lax.axis_index("core")
    half = D // 2
    assemble(full_ref, 1, own_u_ref, upper_ref, corner_ref, left_ref)
    u_ref[...] = full_ref[...].astype(jnp.bfloat16)
    assemble(full_ref, 0, own_x_ref, upper_ref, corner_ref, left_ref)
    x_ref[...] = full_ref[...].astype(jnp.bfloat16)
    normed, _ = statistics(full_ref[...])
    normed_low = normed.astype(jnp.bfloat16)
    proj_ref[...] = dot(normed_low, wqkv_ref[...]).astype(jnp.bfloat16)
    gm_ref[...] = dot(u_ref[...], wproj_ref[...], NT).astype(jnp.bfloat16)

    def place(target_ref, array):
        for b in range(D // 32):
            slot = lax.bitwise_xor(core, b % 2)
            row = pl.multiple_of(slot * half + (b // 2) * 32, 32)
            target_ref[pl.ds(row, 32), :] = array[b * 32:(b + 1) * 32, :]

    place(nt_ref, normed_low.T)

    lane = lax.broadcasted_iota(jnp.int32, (1, LANES), 1) // HD
    masks = [(lane == h).astype(jnp.float32) for h in range(PER)]
    low_masks = [m.astype(jnp.bfloat16) for m in masks]
    tiles = [slice(t * MAIN, (t + 1) * MAIN) for t in range(PER + 1)]

    def stack(target_ref, array):
        for h in range(PER):
            target_ref[tiles[h], :] = array[:MAIN] * low_masks[h]
            rest = PER * MAIN + h * REST
            target_ref[rest:rest + REST, :] = array[MAIN:] * low_masks[h]

    def mix(target_ref, rows, cols, left, weights_ref):
        turned = left.T
        for pair in range(PER // 2):
            both = slice(pair * 2 * MAIN, (pair + 1) * 2 * MAIN)
            mixed = dot(turned[pair * 2 * HD:(pair + 1) * 2 * HD, :], weights_ref[:, both])
            s_ref[pair * 2 * HD:pair * 2 * HD + HD, :MAIN] = mixed[:HD, :MAIN]
            s_ref[pair * 2 * HD + HD:(pair + 1) * 2 * HD, :MAIN] = mixed[HD:, MAIN:]
        rest = dot(weights_ref[:, tiles[PER]].T, left)
        total = rest[:REST] * masks[0]
        for h in range(1, PER):
            total = total + rest[h * REST:(h + 1) * REST] * masks[h]
        target_ref[rows.start:rows.start + MAIN, cols] = s_ref[:LANES, :MAIN].T.astype(jnp.bfloat16)
        target_ref[rows.start + MAIN:rows.stop, cols] = total.astype(jnp.bfloat16)

    for w in range(windows):
        rows = slice(w * WT, (w + 1) * WT)
        labels = lcol_ref[rows, :]
        allowed = [labels == lrow_ref[w:w + 1, tiles[at]] for at in range(2)]
        for g in range(UNITS):
            q_cols, k_cols, v_cols = (
                slice(part * D + g * LANES, part * D + (g + 1) * LANES) for part in range(3)
            )
            k = proj_ref[rows, k_cols]
            v = proj_ref[rows, v_cols]
            stack(qs_ref, proj_ref[rows, q_cols])
            stack(gs_ref, gm_ref[rows, q_cols])
            s_ref[:WT, :] = dot(k, qs_ref[...], NT)
            da_ref[...] = dot(v, gs_ref[...], NT)
            for t in range(PER + 1):
                s = jnp.where(allowed[t // PER], s_ref[:WT, tiles[t]], jnp.float32(-1e30))
                e = jnp.exp2((s - jnp.max(s, 0, keepdims=True)) * jnp.float32(FACTOR * LOG2E))
                a = e * (1.0 / jnp.sum(e, 0, keepdims=True))
                al_ref[:, tiles[t]] = a.astype(jnp.bfloat16)
                ga = da_ref[:, tiles[t]] * a
                gl = (ga - a * jnp.sum(ga, 0, keepdims=True)) * jnp.float32(FACTOR)
                gl_ref[:, tiles[t]] = gl.astype(jnp.bfloat16)
            gp_ref[rows, k_cols] = dot(gl_ref[...], qs_ref[...]).astype(jnp.bfloat16)
            gp_ref[rows, v_cols] = dot(al_ref[...], gs_ref[...]).astype(jnp.bfloat16)
            mix(mix_ref, rows, q_cols, v, al_ref)
            mix(gp_ref, rows, q_cols, k, gl_ref)

    place(mt_ref, mix_ref[...].T)
    nkeep_ref[...] = nt_ref[:half, :]
    mkeep_ref[...] = mt_ref[:half, :]
    grads = jnp.concatenate([dot(nt_ref[half:, :], gp_ref[...]), dot(mt_ref[half:, :], u_ref[...])], axis=1)
    store_shares(send_ref, grads)


def first_kernel(half_ref, got_ref, keep0_ref, send0_ref, keep1_ref, send1_ref):
    a, d = lax.axis_index("xl"), lax.axis_index("dp")

    def total(*at):
        return half_ref[at] + got_ref[at].astype(jnp.float32)

    for yh in range(2):
        keep0_ref[yh] = total(yh, 0, a)
        send0_ref[yh] = total(yh, 0, 1 - a).astype(jnp.bfloat16)
        for xl in range(2):
            for lon in range(8):
                keep1_ref[yh, xl, lon] = total(yh, 1, xl, lon, d)
                send1_ref[yh, xl, lon] = total(yh, 1, xl, lon, 1 - d).astype(jnp.bfloat16)


def second_kernel(keep0_ref, got0_ref, keep1_ref, got1_ref, own_ref, send0_ref, send1_ref):
    a, d = lax.axis_index("xl"), lax.axis_index("dp")

    def total0(*at):
        return keep0_ref[at] + got0_ref[at].astype(jnp.float32)

    def total1(*at):
        return keep1_ref[at] + got1_ref[at].astype(jnp.float32)

    for yh in range(2):
        own_ref[1, yh] = total1(yh, a)
        send1_ref[yh] = total1(yh, 1 - a).astype(jnp.bfloat16)
        for lon in range(8):
            own_ref[0, yh, lon] = total0(yh, lon, d)
            send0_ref[yh, lon] = total0(yh, lon, 1 - d).astype(jnp.bfloat16)


def third_kernel(own_ref, got0_ref, got1_ref, sum_ref):
    for xh, ref in enumerate((got0_ref, got1_ref)):
        for yh in range(2):
            sum_ref[yh, xh] = (own_ref[xh, yh] + ref[yh].astype(jnp.float32)).astype(jnp.bfloat16)


def last_kernel(share_ref, other_ref, qkv_ref, proj_ref):
    second = lax.axis_index("dp") == 1
    share, other = share_ref[...], other_ref[...]
    halves = (jnp.where(second, other, share), jnp.where(second, share, other))
    for tile in range(16):
        row = tile % 8 * 4
        piece = halves[tile // 8][row:row + 4, :]
        if tile < 12:
            qkv_ref[:, tile * 128:(tile + 1) * 128] = piece
        else:
            proj_ref[:, (tile - 12) * 128:(tile - 11) * 128] = piece


def stage_kernel(qkv_ref, proj_ref, qkv_out, proj_out, sems):
    copies = [
        pltpu.make_async_copy(qkv_ref, qkv_out, sems.at[0]),
        pltpu.make_async_copy(proj_ref, proj_out, sems.at[1]),
    ]
    for copy in copies:
        copy.start()
    for copy in copies:
        copy.wait()


def staged(w_qkv, w_proj):
    return pl.pallas_call(
        stage_kernel,
        out_shape=(
            pltpu.VMEM(w_qkv.shape, w_qkv.dtype),
            pltpu.VMEM(w_proj.shape, w_proj.dtype),
        ),
        in_specs=[pl.BlockSpec(memory_space=pltpu.HBM)] * 2,
        out_specs=(pl.BlockSpec(memory_space=pltpu.VMEM),) * 2,
        scratch_shapes=[pltpu.SemaphoreType.DMA((2,))],
        compiler_params=pltpu.CompilerParams(vmem_limit_bytes=4 * 1024 * 1024),
        cost_estimate=pl.CostEstimate(flops=0, bytes_accessed=4 * 1024 * 1024, transcendentals=0),
        name="stage_weights",
    )(w_qkv, w_proj)


def part(value, at, refs):
    own_ref, left_ref = refs
    for level in range(LEV):
        for row in range(WLAT):
            base = (level * WLAT + row) * WLON
            tokens = jnp.concatenate([value[base:base + WLON], value[WT + base:WT + base + WLON]], axis=0)
            left_ref[at, level, row] = tokens[:SLON].astype(jnp.bfloat16)
            own_ref[at, level, row] = tokens[SLON:].astype(jnp.bfloat16)


def rest_kernel(
    n_ref, m_ref, gp_ref, u_ref, x_ref, mix_ref, qkv_ref, proj_ref,
    half_ref, own_ref, left_ref,
    wqkv_ref, wproj_ref, sems,
):
    copies = [
        pltpu.make_async_copy(proj_ref, wproj_ref, sems.at[0]),
        pltpu.make_async_copy(qkv_ref, wqkv_ref, sems.at[1]),
    ]
    for copy in copies:
        copy.start()
    grads = jnp.concatenate([dot(n_ref[...], gp_ref[...]), dot(m_ref[...], u_ref[...])], axis=1)
    store_shares(half_ref, grads)
    refs = (own_ref, left_ref)
    x = x_ref[...].astype(jnp.float32)
    copies[0].wait()
    part(x + dot(mix_ref[...], wproj_ref[...]), 0, refs)
    normed, inverse = statistics(x)
    copies[1].wait()
    grad_normed = dot(gp_ref[...], wqkv_ref[...], NT)
    grad_tokens = inverse * (
        grad_normed
        - jnp.mean(grad_normed, -1, keepdims=True)
        - normed * jnp.mean(grad_normed * normed, -1, keepdims=True)
    )
    part(u_ref[...].astype(jnp.float32) + grad_tokens, 1, refs)


def call(kernel, name, outs, scratch, flops, *args, dtypes=None, limit=12, placed=False, any_args=()):
    vmem = pl.BlockSpec(memory_space=pltpu.VMEM)
    dtypes = dtypes or (jnp.bfloat16,) * len(outs)
    make = pltpu.VMEM if placed else jax.ShapeDtypeStruct
    size = sum(2 * math.prod(shape) for shape in outs)
    return pl.pallas_call(
        kernel,
        out_shape=tuple(make(shape, dtype) for shape, dtype in zip(outs, dtypes)),
        in_specs=[
            pl.BlockSpec(memory_space=pltpu.HBM) if at in any_args else vmem for at in range(len(args))
        ],
        out_specs=(vmem,) * len(outs),
        scratch_shapes=[
            pltpu.SemaphoreType.DMA(shape) if kind is None else pltpu.VMEM(shape, kind)
            for shape, kind in scratch
        ],
        compiler_params=pltpu.CompilerParams(vmem_limit_bytes=limit * 1024 * 1024),
        cost_estimate=pl.CostEstimate(flops=flops, bytes_accessed=2 * size, transcendentals=0),
        name=name,
    )(*args)


def attention(x, u, upper, corner, left, lrow, lcol, w_qkv, w_proj):
    tokens = math.prod(x.shape[:-1])
    low, full = jnp.bfloat16, jnp.float32
    return call(
        attention_kernel,
        "window_attention",
        (
            (32, 2, 64, 128), (tokens, 3 * D), (tokens, D),
            (D // 2, tokens), (D // 2, tokens), (tokens, D), (tokens, D),
        ),
        (
            ((tokens, D), full),
            ((tokens, 3 * D), low),
            ((tokens, D), low),
            ((D, tokens), low),
            ((D, tokens), low),
            ((WT, WIDE), low),
            ((WT, WIDE), low),
            ((LANES, WIDE), full),
            ((WT, WIDE), full),
            ((WIDE, LANES), low),
            ((WIDE, LANES), low),
        ),
        5_000_000_000,
        x, u, upper, corner, left, lrow, lcol, w_qkv, w_proj,
        limit=20,
    )


LAT = ("yh", "xh", "xl", "core")


def passed_along(value, axis, steps):
    count = lax.axis_size(axis)
    pairs = [(source, (source + steps) % count) for source in range(count)]
    return lax.ppermute(value, axis, pairs)


def diagonal(value, steps):
    n_lat, n_lon = lax.axis_size(LAT), lax.axis_size("lon")
    pairs = [
        (a * n_lon + b, (a + steps) % n_lat * n_lon + (b + steps) % n_lon)
        for a in range(n_lat)
        for b in range(n_lon)
    ]
    return lax.ppermute(value, (*LAT, "lon"), pairs)


def per_device(inputs, cotangent, mask_ids, w_qkv, w_proj):
    body = (2, LEV, SLAT, inputs.shape[3] - SLON, D)
    side = (2, LEV, SLAT, SLON, D)
    upper, corner, left = call(
        cut_kernel, "cut_halos", (body, side, side),
        (((2, *inputs.shape[1:]), jnp.bfloat16), ((2, LEV), None)), 1000,
        *(pltpu.with_memory_space_constraint(array, pltpu.HBM) for array in (inputs, cotangent)),
        limit=8, any_args=(0, 1),
    )
    upper = passed_along(upper, LAT, 1)
    corner = diagonal(corner, 1)
    left = passed_along(left, "lon", 1)
    first_band = lax.axis_index(LAT) == 0
    wrapped = jnp.logical_and(first_band, jnp.arange(WLAT) < SLAT).astype(jnp.int32)
    groups = mask_ids + 4 * wrapped[:, None]
    windows = groups.shape[1] // WLON
    labels = groups.reshape(WLAT, windows, WLON).transpose(1, 0, 2).reshape(windows, WLAT * WLON)
    labels = jnp.tile(labels, (1, LEV))
    lcol = labels.reshape(windows * WT, 1)
    lrow = jnp.concatenate([labels[:, :MAIN], jnp.tile(labels[:, MAIN:], (1, PER))], axis=1)
    send, gp, mix, nkeep, mkeep, x, u = attention(
        inputs, cotangent, upper, corner, left, lrow, lcol, *staged(w_qkv, w_proj)
    )
    got = passed_along(send, "core", 1)
    half, own, left = call(
        rest_kernel, "own_half_and_outputs",
        (send.shape, (2, *inputs.shape[1:3], body[3], D), (2, *inputs.shape[1:3], SLON, D)),
        ((w_qkv.shape, jnp.bfloat16), (w_proj.shape, jnp.bfloat16), ((2,), None)), 600_000_000,
        nkeep, mkeep, gp, u, x, mix, w_qkv, w_proj,
        dtypes=(jnp.float32,) + (jnp.bfloat16,) * 2, any_args=(6, 7), limit=16,
    )
    low, full = jnp.bfloat16, jnp.float32
    shape = (2, 2, 2, 8, 2, 32, 128)
    keep0, send0, keep1, send1 = call(
        first_kernel, "first_sums", ((2, 8, 2, 32, 128),) * 2 + ((2, 2, 8, 32, 128),) * 2, (), 1_000_000,
        half.reshape(shape), got.reshape(shape), dtypes=(full, low) * 2,
    )
    got0, got1 = passed_along(send0, "xl", 1), passed_along(send1, "dp", 1)
    right = passed_along(left, "lon", -1)
    got0, got1, right = lax.optimization_barrier((got0, got1, right))
    mine, send0, send1 = call(
        second_kernel, "second_sums", ((2, 2, 8, 32, 128),) + ((2, 8, 32, 128),) * 2, (), 1_000_000,
        keep0, got0, keep1, got1, dtypes=(full, low, low),
    )
    got0, got1 = passed_along(send0, "dp", 1), passed_along(send1, "xl", 1)
    (sums,) = call(
        third_kernel, "third_sums", ((2, 2, 8, 32, 128),), (), 1_000_000, mine, got0, got1
    )
    spread = lax.all_to_all(sums.reshape(32, 32, 128), ("yh", "xh", "lon"), 0, 0, tiled=True)
    share = jnp.sum(spread.astype(jnp.float32), 0)
    other = passed_along(share, "dp", 1)
    grad_qkv, grad_proj = call(
        last_kernel, "last_sum", ((4, 3 * D), (4, D)), (), 1000, share, other,
        dtypes=(jnp.float32,) * 2, limit=4,
    )
    (rows,) = call(rows_kernel, "halo_rows", ((2, LEV, SLAT, *inputs.shape[3:]),), (), 1000, own, right, limit=8)
    lower = passed_along(rows, LAT, -1)
    output, grad_inputs = call(
        join_kernel, "join_outputs", (inputs.shape, inputs.shape), (), 1000, own, right, lower, limit=8
    )
    return (output, grad_inputs, grad_qkv, grad_proj)


def solution(mesh):
    mesh = Mesh(mesh.devices.reshape(2, 2, 2, 2, 2, 8), ("dp", *LAT, "lon"))
    tokens = P("dp", None, LAT, "lon", None)
    return jax.shard_map(
        per_device,
        mesh=mesh,
        in_specs=(tokens, tokens, P(LAT, "lon"), P(), P()),
        out_specs=(tokens, tokens, P((*LAT, "lon"), None), P((*LAT, "lon"), None)),
        check_vma=False,
    )
```

```python
import functools
import math

import jax
import jax.numpy as jnp
from jax import lax
from jax.experimental import pallas as pl
from jax.experimental.pallas import tpu as pltpu
from jax.sharding import Mesh
from jax.sharding import PartitionSpec as P

D = 512
HEADS = 16
HD = 32
LEV = 2
WLAT = 6
WLON = 12
SLAT = 3
SLON = 6
WT = LEV * WLAT * WLON
PER = 8
LANES = PER * HD
MAIN = 128
REST = WT - MAIN
WIDE = PER * WT
UNITS = D // LANES
FACTOR = 1.0 / math.sqrt(HD)
LOG2E = 1.4426950408889634

NN = (((1,), (0,)), ((), ()))
NT = (((1,), (1,)), ((), ()))


def dot(left, right, dims=NN):
    return lax.dot_general(left, right, dims, preferred_element_type=jnp.float32)


def cut_kernel(x_ref, u_ref, upper_ref, corner_ref, left_ref, held_ref, sems):
    copies = []
    for at, ref in enumerate((x_ref, u_ref)):
        for level in range(LEV):
            copies.append(pltpu.make_async_copy(ref.at[0, level], held_ref.at[at, level], sems.at[at, level]))
    for copy in copies:
        copy.start()
    for copy in copies:
        copy.wait()
    for at in range(2):
        for level in range(LEV):
            for row in range(WLAT):
                tokens = held_ref[at, level, row].astype(jnp.float32)
                side = tokens[-SLON:].astype(jnp.bfloat16)
                if row < SLAT:
                    left_ref[at, level, row] = side
                else:
                    corner_ref[at, level, row - SLAT] = side
                    upper_ref[at, level, row - SLAT] = tokens[:-SLON].astype(jnp.bfloat16)


def joined(body, side):
    both = jnp.concatenate([body.astype(jnp.float32), side.astype(jnp.float32)], axis=0)
    return both.astype(jnp.bfloat16)


def rows_kernel(own_ref, right_ref, rows_ref):
    for at in range(2):
        for level in range(LEV):
            for row in range(SLAT):
                rows_ref[at, level, row] = joined(own_ref[at, level, row], right_ref[at, level, row])


def join_kernel(own_ref, right_ref, lower_ref, out_ref, gin_ref):
    for at, ref in enumerate((out_ref, gin_ref)):
        for level in range(LEV):
            for row in range(SLAT):
                ref[0, level, row] = joined(own_ref[at, level, SLAT + row], right_ref[at, level, SLAT + row])
                ref[0, level, SLAT + row] = lower_ref[at, level, row]


def assemble(target_ref, at, own_ref, upper_ref, corner_ref, left_ref):
    pieces = ([], [])
    for level in range(LEV):
        for row in range(WLAT):
            if row < SLAT:
                side, body = corner_ref[at, level, row], upper_ref[at, level, row]
            else:
                side, body = left_ref[at, level, row - SLAT], own_ref[0, level, row - SLAT]
            side, body = side.astype(jnp.float32), body.astype(jnp.float32)
            pieces[0].append(side)
            pieces[0].append(body[:WLON - SLON])
            pieces[1].append(body[WLON - SLON:2 * WLON - SLON])
    for w in range(2):
        target_ref[w * WT:(w + 1) * WT, :] = jnp.concatenate(pieces[w], axis=0)


def statistics(x):
    center = jnp.mean(x, -1, keepdims=True)
    shifted = x - center
    inverse = lax.rsqrt(jnp.mean(shifted * shifted, -1, keepdims=True) + 1e-05)
    return shifted * inverse, inverse


def store_shares(target_ref, grads):
    count = grads.shape[0]
    first = lax.broadcasted_iota(jnp.int32, (count, 128), 0) % 8 < 4
    for quad in range(4):
        shares = ([], [])
        for pair in (2 * quad, 2 * quad + 1):
            left = grads[:, pair * 256:pair * 256 + 128]
            right = grads[:, pair * 256 + 128:pair * 256 + 256]
            shares[0].append(jnp.where(first, left, pltpu.roll(right, 4, 0)))
            shares[1].append(jnp.where(first, pltpu.roll(left, count - 4, 0), right))
        rows = slice(quad * 16, quad * 16 + 16)
        for which in range(2):
            piece = jnp.concatenate([p.reshape(count // 8, 8, 128) for p in shares[which]], axis=1)
            target_ref[:, which, rows, :] = piece.astype(target_ref.dtype)


def attention_kernel(
    own_x_ref, own_u_ref, left_ref, corner_ref, upper_ref, lrow_ref, lcol_ref, wqkv_ref, wproj_ref,
    send_ref, gp_ref, mix_ref, nkeep_ref, mkeep_ref, x_ref, u_ref,
    full_ref, proj_ref, gm_ref, nt_ref, mt_ref, al_ref, gl_ref, s_ref, da_ref, qs_ref, gs_ref,
):
    windows = x_ref.shape[0] // WT
    core = lax.axis_index("core")
    half = D // 2
    assemble(full_ref, 1, own_u_ref, upper_ref, corner_ref, left_ref)
    u_ref[...] = full_ref[...].astype(jnp.bfloat16)
    assemble(full_ref, 0, own_x_ref, upper_ref, corner_ref, left_ref)
    x_ref[...] = full_ref[...].astype(jnp.bfloat16)
    normed, _ = statistics(full_ref[...])
    normed_low = normed.astype(jnp.bfloat16)
    proj_ref[...] = dot(normed_low, wqkv_ref[...]).astype(jnp.bfloat16)
    gm_ref[...] = dot(u_ref[...], wproj_ref[...], NT).astype(jnp.bfloat16)

    def place(target_ref, array):
        for b in range(D // 32):
            slot = lax.bitwise_xor(core, b % 2)
            row = pl.multiple_of(slot * half + (b // 2) * 32, 32)
            target_ref[pl.ds(row, 32), :] = array[b * 32:(b + 1) * 32, :]

    place(nt_ref, normed_low.T)

    lane = lax.broadcasted_iota(jnp.int32, (1, LANES), 1) // HD
    masks = [(lane == h).astype(jnp.float32) for h in range(PER)]
    low_masks = [m.astype(jnp.bfloat16) for m in masks]
    tiles = [slice(t * MAIN, (t + 1) * MAIN) for t in range(PER + 1)]

    def stack(target_ref, array):
        for h in range(PER):
            target_ref[tiles[h], :] = array[:MAIN] * low_masks[h]
            rest = PER * MAIN + h * REST
            target_ref[rest:rest + REST, :] = array[MAIN:] * low_masks[h]

    def mix(target_ref, rows, cols, left, weights_ref):
        turned = left.T
        for pair in range(PER // 2):
            both = slice(pair * 2 * MAIN, (pair + 1) * 2 * MAIN)
            mixed = dot(turned[pair * 2 * HD:(pair + 1) * 2 * HD, :], weights_ref[:, both])
            s_ref[pair * 2 * HD:pair * 2 * HD + HD, :MAIN] = mixed[:HD, :MAIN]
            s_ref[pair * 2 * HD + HD:(pair + 1) * 2 * HD, :MAIN] = mixed[HD:, MAIN:]
        rest = dot(weights_ref[:, tiles[PER]].T, left)
        total = rest[:REST] * masks[0]
        for h in range(1, PER):
            total = total + rest[h * REST:(h + 1) * REST] * masks[h]
        target_ref[rows.start:rows.start + MAIN, cols] = s_ref[:LANES, :MAIN].T.astype(jnp.bfloat16)
        target_ref[rows.start + MAIN:rows.stop, cols] = total.astype(jnp.bfloat16)

    for w in range(windows):
        rows = slice(w * WT, (w + 1) * WT)
        labels = lcol_ref[rows, :]
        allowed = [labels == lrow_ref[w:w + 1, tiles[at]] for at in range(2)]
        for g in range(UNITS):
            q_cols, k_cols, v_cols = (
                slice(part * D + g * LANES, part * D + (g + 1) * LANES) for part in range(3)
            )
            k = proj_ref[rows, k_cols]
            v = proj_ref[rows, v_cols]
            stack(qs_ref, proj_ref[rows, q_cols])
            stack(gs_ref, gm_ref[rows, q_cols])
            s_ref[:WT, :] = dot(k, qs_ref[...], NT)
            da_ref[...] = dot(v, gs_ref[...], NT)
            for t in range(PER + 1):
                s = jnp.where(allowed[t // PER], s_ref[:WT, tiles[t]], jnp.float32(-1e30))
                e = jnp.exp2((s - jnp.max(s, 0, keepdims=True)) * jnp.float32(FACTOR * LOG2E))
                a = e * (1.0 / jnp.sum(e, 0, keepdims=True))
                al_ref[:, tiles[t]] = a.astype(jnp.bfloat16)
                ga = da_ref[:, tiles[t]] * a
                gl = (ga - a * jnp.sum(ga, 0, keepdims=True)) * jnp.float32(FACTOR)
                gl_ref[:, tiles[t]] = gl.astype(jnp.bfloat16)
            gp_ref[rows, k_cols] = dot(gl_ref[...], qs_ref[...]).astype(jnp.bfloat16)
            gp_ref[rows, v_cols] = dot(al_ref[...], gs_ref[...]).astype(jnp.bfloat16)
            mix(mix_ref, rows, q_cols, v, al_ref)
            mix(gp_ref, rows, q_cols, k, gl_ref)

    place(mt_ref, mix_ref[...].T)
    nkeep_ref[...] = nt_ref[:half, :]
    mkeep_ref[...] = mt_ref[:half, :]
    grads = jnp.concatenate([dot(nt_ref[half:, :], gp_ref[...]), dot(mt_ref[half:, :], u_ref[...])], axis=1)
    store_shares(send_ref, grads)


def add_kernel(own_ref, got_ref, sum_ref):
    sum_ref[...] = (own_ref[...] + got_ref[...].astype(jnp.float32)).astype(jnp.bfloat16)


def added(parts_ref):
    total = parts_ref[0].astype(jnp.float32)
    for at in range(1, parts_ref.shape[0]):
        total = total + parts_ref[at].astype(jnp.float32)
    return total


def sum_kernel(parts_ref, sum_ref):
    total = added(parts_ref).astype(jnp.bfloat16)
    sum_ref[0] = total
    sum_ref[1] = total


def last_kernel(parts_ref, qkv_ref, proj_ref):
    total = added(parts_ref)
    for tile in range(16):
        piece = total[tile * 4:tile * 4 + 4, :]
        if tile < 12:
            qkv_ref[:, tile * 128:(tile + 1) * 128] = piece
        else:
            proj_ref[:, (tile - 12) * 128:(tile - 11) * 128] = piece


def stage_kernel(qkv_ref, proj_ref, qkv_out, proj_out, sems):
    copies = [
        pltpu.make_async_copy(qkv_ref, qkv_out, sems.at[0]),
        pltpu.make_async_copy(proj_ref, proj_out, sems.at[1]),
    ]
    for copy in copies:
        copy.start()
    for copy in copies:
        copy.wait()


def staged(w_qkv, w_proj):
    return pl.pallas_call(
        stage_kernel,
        out_shape=(
            pltpu.VMEM(w_qkv.shape, w_qkv.dtype),
            pltpu.VMEM(w_proj.shape, w_proj.dtype),
        ),
        in_specs=[pl.BlockSpec(memory_space=pltpu.HBM)] * 2,
        out_specs=(pl.BlockSpec(memory_space=pltpu.VMEM),) * 2,
        scratch_shapes=[pltpu.SemaphoreType.DMA((2,))],
        compiler_params=pltpu.CompilerParams(vmem_limit_bytes=4 * 1024 * 1024),
        cost_estimate=pl.CostEstimate(flops=0, bytes_accessed=4 * 1024 * 1024, transcendentals=0),
        name="stage_weights",
    )(w_qkv, w_proj)


def part(value, at, refs):
    own_ref, left_ref = refs
    for level in range(LEV):
        for row in range(WLAT):
            base = (level * WLAT + row) * WLON
            tokens = jnp.concatenate([value[base:base + WLON], value[WT + base:WT + base + WLON]], axis=0)
            left_ref[at, level, row] = tokens[:SLON].astype(jnp.bfloat16)
            own_ref[at, level, row] = tokens[SLON:].astype(jnp.bfloat16)


def rest_kernel(
    n_ref, m_ref, gp_ref, u_ref, x_ref, mix_ref, qkv_ref, proj_ref,
    half_ref, own_ref, left_ref,
    wqkv_ref, wproj_ref, sems,
):
    copies = [
        pltpu.make_async_copy(proj_ref, wproj_ref, sems.at[0]),
        pltpu.make_async_copy(qkv_ref, wqkv_ref, sems.at[1]),
    ]
    for copy in copies:
        copy.start()
    grads = jnp.concatenate([dot(n_ref[...], gp_ref[...]), dot(m_ref[...], u_ref[...])], axis=1)
    store_shares(half_ref, grads)
    refs = (own_ref, left_ref)
    x = x_ref[...].astype(jnp.float32)
    copies[0].wait()
    part(x + dot(mix_ref[...], wproj_ref[...]), 0, refs)
    normed, inverse = statistics(x)
    copies[1].wait()
    grad_normed = dot(gp_ref[...], wqkv_ref[...], NT)
    grad_tokens = inverse * (
        grad_normed
        - jnp.mean(grad_normed, -1, keepdims=True)
        - normed * jnp.mean(grad_normed * normed, -1, keepdims=True)
    )
    part(u_ref[...].astype(jnp.float32) + grad_tokens, 1, refs)


def call(kernel, name, outs, scratch, flops, *args, dtypes=None, limit=12, placed=False, any_args=()):
    vmem = pl.BlockSpec(memory_space=pltpu.VMEM)
    dtypes = dtypes or (jnp.bfloat16,) * len(outs)
    make = pltpu.VMEM if placed else jax.ShapeDtypeStruct
    size = sum(2 * math.prod(shape) for shape in outs)
    return pl.pallas_call(
        kernel,
        out_shape=tuple(make(shape, dtype) for shape, dtype in zip(outs, dtypes)),
        in_specs=[
            pl.BlockSpec(memory_space=pltpu.HBM) if at in any_args else vmem for at in range(len(args))
        ],
        out_specs=(vmem,) * len(outs),
        scratch_shapes=[
            pltpu.SemaphoreType.DMA(shape) if kind is None else pltpu.VMEM(shape, kind)
            for shape, kind in scratch
        ],
        compiler_params=pltpu.CompilerParams(vmem_limit_bytes=limit * 1024 * 1024),
        cost_estimate=pl.CostEstimate(flops=flops, bytes_accessed=2 * size, transcendentals=0),
        name=name,
    )(*args)


def attention(x, u, upper, corner, left, lrow, lcol, w_qkv, w_proj):
    tokens = math.prod(x.shape[:-1])
    low, full = jnp.bfloat16, jnp.float32
    return call(
        attention_kernel,
        "window_attention",
        (
            (32, 2, 64, 128), (tokens, 3 * D), (tokens, D),
            (D // 2, tokens), (D // 2, tokens), (tokens, D), (tokens, D),
        ),
        (
            ((tokens, D), full),
            ((tokens, 3 * D), low),
            ((tokens, D), low),
            ((D, tokens), low),
            ((D, tokens), low),
            ((WT, WIDE), low),
            ((WT, WIDE), low),
            ((LANES, WIDE), full),
            ((WT, WIDE), full),
            ((WIDE, LANES), low),
            ((WIDE, LANES), low),
        ),
        5_000_000_000,
        x, u, left, corner, upper, lrow, lcol, w_qkv, w_proj,
        limit=20,
    )


LAT = ("yh", "x", "core")


def passed_along(value, axis, steps):
    count = lax.axis_size(axis)
    pairs = [(source, (source + steps) % count) for source in range(count)]
    return lax.ppermute(value, axis, pairs)


def diagonal(value, steps):
    n_lat, n_lon = lax.axis_size(LAT), lax.axis_size("lon")
    pairs = [
        (a * n_lon + b, (a + steps) % n_lat * n_lon + (b + steps) % n_lon)
        for a in range(n_lat)
        for b in range(n_lon)
    ]
    return lax.ppermute(value, (*LAT, "lon"), pairs)


def per_device(inputs, cotangent, mask_ids, w_qkv, w_proj):
    body = (2, LEV, SLAT, inputs.shape[3] - SLON, D)
    side = (2, LEV, SLAT, SLON, D)
    upper, corner, left = call(
        cut_kernel, "cut_halos", (body, side, side),
        (((2, *inputs.shape[1:]), jnp.bfloat16), ((2, LEV), None)), 1000,
        *(pltpu.with_memory_space_constraint(array, pltpu.HBM) for array in (inputs, cotangent)),
        limit=8, any_args=(0, 1),
    )
    left = passed_along(left, "lon", 1)
    corner = diagonal(corner, 1)
    upper = passed_along(upper, LAT, 1)
    first_band = lax.axis_index(LAT) == 0
    wrapped = jnp.logical_and(first_band, jnp.arange(WLAT) < SLAT).astype(jnp.int32)
    groups = mask_ids + 4 * wrapped[:, None]
    windows = groups.shape[1] // WLON
    labels = groups.reshape(WLAT, windows, WLON).transpose(1, 0, 2).reshape(windows, WLAT * WLON)
    labels = jnp.tile(labels, (1, LEV))
    lcol = labels.reshape(windows * WT, 1)
    lrow = jnp.concatenate([labels[:, :MAIN], jnp.tile(labels[:, MAIN:], (1, PER))], axis=1)
    send, gp, mix, nkeep, mkeep, x, u = attention(
        inputs, cotangent, upper, corner, left, lrow, lcol, *staged(w_qkv, w_proj)
    )
    got = passed_along(send, "core", 1)
    half, own, left = call(
        rest_kernel, "own_half_and_outputs",
        (send.shape, (2, *inputs.shape[1:3], body[3], D), (2, *inputs.shape[1:3], SLON, D)),
        ((w_qkv.shape, jnp.bfloat16), (w_proj.shape, jnp.bfloat16), ((2,), None)), 600_000_000,
        nkeep, mkeep, gp, u, x, mix, w_qkv, w_proj,
        dtypes=(jnp.float32,) + (jnp.bfloat16,) * 2, any_args=(6, 7), limit=16,
    )
    (sums,) = call(add_kernel, "add_halves", (send.shape,), (), 1_000_000, half, got, placed=True)
    right = passed_along(left, "lon", -1)
    spread = lax.all_to_all(sums.reshape(8, 512, 128), ("yh", "x"), 0, 0, tiled=True)
    spread, right = lax.optimization_barrier((spread, right))
    (sums,) = call(sum_kernel, "sum_parts", ((2, 512, 128),), (), 1_000_000, spread, placed=True)
    spread = lax.all_to_all(sums.reshape(16, 64, 128), ("dp", "lon"), 0, 0, tiled=True)
    grad_qkv, grad_proj = call(
        last_kernel, "last_sum", ((4, 3 * D), (4, D)), (), 1000, spread,
        dtypes=(jnp.float32,) * 2, limit=4,
    )
    (rows,) = call(rows_kernel, "halo_rows", ((2, LEV, SLAT, *inputs.shape[3:]),), (), 1000, own, right, limit=8)
    lower = passed_along(rows, LAT, -1)
    output, grad_inputs = call(
        join_kernel, "join_outputs", (inputs.shape, inputs.shape), (), 1000, own, right, lower, limit=8
    )
    return (output, grad_inputs, grad_qkv, grad_proj)


def solution(mesh):
    mesh = Mesh(mesh.devices.reshape(2, 2, 4, 2, 8), ("dp", "yh", "x", "core", "lon"))
    tokens = P("dp", None, LAT, "lon", None)
    return jax.shard_map(
        per_device,
        mesh=mesh,
        in_specs=(tokens, tokens, P(LAT, "lon"), P(), P()),
        out_specs=(tokens, tokens, P((*LAT, "lon"), None), P((*LAT, "lon"), None)),
        check_vma=False,
    )
```

```python
import functools
import math

import jax
import jax.numpy as jnp
from jax import lax
from jax.experimental import pallas as pl
from jax.experimental.pallas import tpu as pltpu
from jax.sharding import Mesh
from jax.sharding import PartitionSpec as P

D = 512
HEADS = 16
HD = 32
LEV = 2
WLAT = 6
WLON = 12
SLAT = 3
SLON = 6
WT = LEV * WLAT * WLON
PER = 8
LANES = PER * HD
MAIN = 128
REST = WT - MAIN
WIDE = PER * WT
UNITS = D // LANES
FACTOR = 1.0 / math.sqrt(HD)
LOG2E = 1.4426950408889634

NN = (((1,), (0,)), ((), ()))
NT = (((1,), (1,)), ((), ()))


def dot(left, right, dims=NN):
    return lax.dot_general(left, right, dims, preferred_element_type=jnp.float32)


def cut_kernel(x_ref, u_ref, upper_ref, corner_ref, left_ref, held_ref, sems):
    copies = []
    for at, ref in enumerate((x_ref, u_ref)):
        for level in range(LEV):
            copies.append(pltpu.make_async_copy(ref.at[0, level], held_ref.at[at, level], sems.at[at, level]))
    for copy in copies:
        copy.start()
    for copy in copies:
        copy.wait()
    for at in range(2):
        for level in range(LEV):
            for row in range(WLAT):
                tokens = held_ref[at, level, row].astype(jnp.float32)
                side = tokens[-SLON:].astype(jnp.bfloat16)
                if row < SLAT:
                    left_ref[at, level, row] = side
                else:
                    corner_ref[at, level, row - SLAT] = side
                    upper_ref[at, level, row - SLAT] = tokens[:-SLON].astype(jnp.bfloat16)


def joined(body, side):
    both = jnp.concatenate([body.astype(jnp.float32), side.astype(jnp.float32)], axis=0)
    return both.astype(jnp.bfloat16)


def rows_kernel(own_ref, right_ref, rows_ref):
    for at in range(2):
        for level in range(LEV):
            for row in range(SLAT):
                rows_ref[at, level, row] = joined(own_ref[at, level, row], right_ref[at, level, row])


def join_kernel(own_ref, right_ref, lower_ref, out_ref, gin_ref):
    for at, ref in enumerate((out_ref, gin_ref)):
        for level in range(LEV):
            for row in range(SLAT):
                ref[0, level, row] = joined(own_ref[at, level, SLAT + row], right_ref[at, level, SLAT + row])
                ref[0, level, SLAT + row] = lower_ref[at, level, row]


def assemble(target_ref, at, own_ref, upper_ref, corner_ref, left_ref):
    pieces = ([], [])
    for level in range(LEV):
        for row in range(WLAT):
            if row < SLAT:
                side, body = corner_ref[at, level, row], upper_ref[at, level, row]
            else:
                side, body = left_ref[at, level, row - SLAT], own_ref[0, level, row - SLAT]
            side, body = side.astype(jnp.float32), body.astype(jnp.float32)
            pieces[0].append(side)
            pieces[0].append(body[:WLON - SLON])
            pieces[1].append(body[WLON - SLON:2 * WLON - SLON])
    for w in range(2):
        target_ref[w * WT:(w + 1) * WT, :] = jnp.concatenate(pieces[w], axis=0)


def statistics(x):
    center = jnp.mean(x, -1, keepdims=True)
    shifted = x - center
    inverse = lax.rsqrt(jnp.mean(shifted * shifted, -1, keepdims=True) + 1e-05)
    return shifted * inverse, inverse


def store_shares(target_ref, grads):
    count = grads.shape[0]
    first = lax.broadcasted_iota(jnp.int32, (count, 128), 0) % 8 < 4
    for quad in range(4):
        shares = ([], [])
        for pair in (2 * quad, 2 * quad + 1):
            left = grads[:, pair * 256:pair * 256 + 128]
            right = grads[:, pair * 256 + 128:pair * 256 + 256]
            shares[0].append(jnp.where(first, left, pltpu.roll(right, 4, 0)))
            shares[1].append(jnp.where(first, pltpu.roll(left, count - 4, 0), right))
        rows = slice(quad * 16, quad * 16 + 16)
        for which in range(2):
            piece = jnp.concatenate([p.reshape(count // 8, 8, 128) for p in shares[which]], axis=1)
            target_ref[:, which, rows, :] = piece.astype(target_ref.dtype)


def attention_kernel(
    own_x_ref, own_u_ref, upper_ref, corner_ref, left_ref, lrow_ref, lcol_ref, wqkv_ref, wproj_ref,
    send_ref, gp_ref, mix_ref, nkeep_ref, mkeep_ref, x_ref, u_ref,
    full_ref, proj_ref, gm_ref, nt_ref, mt_ref, al_ref, gl_ref, s_ref, da_ref, qs_ref, gs_ref,
):
    windows = x_ref.shape[0] // WT
    core = lax.axis_index("core")
    half = D // 2
    assemble(full_ref, 1, own_u_ref, upper_ref, corner_ref, left_ref)
    u_ref[...] = full_ref[...].astype(jnp.bfloat16)
    assemble(full_ref, 0, own_x_ref, upper_ref, corner_ref, left_ref)
    x_ref[...] = full_ref[...].astype(jnp.bfloat16)
    normed, _ = statistics(full_ref[...])
    normed_low = normed.astype(jnp.bfloat16)
    proj_ref[...] = dot(normed_low, wqkv_ref[...]).astype(jnp.bfloat16)
    gm_ref[...] = dot(u_ref[...], wproj_ref[...], NT).astype(jnp.bfloat16)

    def place(target_ref, array):
        for b in range(D // 32):
            slot = lax.bitwise_xor(core, b % 2)
            row = pl.multiple_of(slot * half + (b // 2) * 32, 32)
            target_ref[pl.ds(row, 32), :] = array[b * 32:(b + 1) * 32, :]

    place(nt_ref, normed_low.T)

    lane = lax.broadcasted_iota(jnp.int32, (1, LANES), 1) // HD
    masks = [(lane == h).astype(jnp.float32) for h in range(PER)]
    low_masks = [m.astype(jnp.bfloat16) for m in masks]
    tiles = [slice(t * MAIN, (t + 1) * MAIN) for t in range(PER + 1)]

    def stack(target_ref, array):
        for h in range(PER):
            target_ref[tiles[h], :] = array[:MAIN] * low_masks[h]
            rest = PER * MAIN + h * REST
            target_ref[rest:rest + REST, :] = array[MAIN:] * low_masks[h]

    def mix(target_ref, rows, cols, left, weights_ref):
        turned = left.T
        for pair in range(PER // 2):
            both = slice(pair * 2 * MAIN, (pair + 1) * 2 * MAIN)
            mixed = dot(turned[pair * 2 * HD:(pair + 1) * 2 * HD, :], weights_ref[:, both])
            s_ref[pair * 2 * HD:pair * 2 * HD + HD, :MAIN] = mixed[:HD, :MAIN]
            s_ref[pair * 2 * HD + HD:(pair + 1) * 2 * HD, :MAIN] = mixed[HD:, MAIN:]
        rest = dot(weights_ref[:, tiles[PER]].T, left)
        total = rest[:REST] * masks[0]
        for h in range(1, PER):
            total = total + rest[h * REST:(h + 1) * REST] * masks[h]
        target_ref[rows.start:rows.start + MAIN, cols] = s_ref[:LANES, :MAIN].T.astype(jnp.bfloat16)
        target_ref[rows.start + MAIN:rows.stop, cols] = total.astype(jnp.bfloat16)

    for w in range(windows):
        rows = slice(w * WT, (w + 1) * WT)
        labels = lcol_ref[rows, :]
        allowed = [labels == lrow_ref[w:w + 1, tiles[at]] for at in range(2)]
        for g in range(UNITS):
            q_cols, k_cols, v_cols = (
                slice(part * D + g * LANES, part * D + (g + 1) * LANES) for part in range(3)
            )
            k = proj_ref[rows, k_cols]
            v = proj_ref[rows, v_cols]
            stack(qs_ref, proj_ref[rows, q_cols])
            stack(gs_ref, gm_ref[rows, q_cols])
            s_ref[:WT, :] = dot(k, qs_ref[...], NT)
            da_ref[...] = dot(v, gs_ref[...], NT)
            for t in range(PER + 1):
                s = jnp.where(allowed[t // PER], s_ref[:WT, tiles[t]], jnp.float32(-1e30))
                e = jnp.exp2((s - jnp.max(s, 0, keepdims=True)) * jnp.float32(FACTOR * LOG2E))
                a = e * (1.0 / jnp.sum(e, 0, keepdims=True))
                al_ref[:, tiles[t]] = a.astype(jnp.bfloat16)
                ga = da_ref[:, tiles[t]] * a
                gl = (ga - a * jnp.sum(ga, 0, keepdims=True)) * jnp.float32(FACTOR)
                gl_ref[:, tiles[t]] = gl.astype(jnp.bfloat16)
            gp_ref[rows, k_cols] = dot(gl_ref[...], qs_ref[...]).astype(jnp.bfloat16)
            gp_ref[rows, v_cols] = dot(al_ref[...], gs_ref[...]).astype(jnp.bfloat16)
            mix(mix_ref, rows, q_cols, v, al_ref)
            mix(gp_ref, rows, q_cols, k, gl_ref)

    place(mt_ref, mix_ref[...].T)
    nkeep_ref[...] = nt_ref[:half, :]
    mkeep_ref[...] = mt_ref[:half, :]
    grads = jnp.concatenate([dot(nt_ref[half:, :], gp_ref[...]), dot(mt_ref[half:, :], u_ref[...])], axis=1)
    store_shares(send_ref, grads)


def add_kernel(own_ref, got_ref, sum_ref):
    for yh in range(own_ref.shape[0]):
        for x in range(own_ref.shape[1]):
            total = own_ref[yh, x] + got_ref[yh, x].astype(jnp.float32)
            sum_ref[x, yh] = total.astype(jnp.bfloat16)


def added(parts_ref):
    total = parts_ref[0].astype(jnp.float32)
    for at in range(1, parts_ref.shape[0]):
        total = total + parts_ref[at].astype(jnp.float32)
    return total


def sum_kernel(parts_ref, sum_ref):
    total = added(parts_ref).astype(jnp.bfloat16).reshape(8, 64, 128)
    sum_ref[:, 0] = total
    sum_ref[:, 1] = total


def last_kernel(parts_ref, qkv_ref, proj_ref):
    total = added(parts_ref)
    for tile in range(16):
        piece = total[tile * 4:tile * 4 + 4, :]
        if tile < 12:
            qkv_ref[:, tile * 128:(tile + 1) * 128] = piece
        else:
            proj_ref[:, (tile - 12) * 128:(tile - 11) * 128] = piece


def stage_kernel(qkv_ref, proj_ref, qkv_out, proj_out, sems):
    copies = [
        pltpu.make_async_copy(qkv_ref, qkv_out, sems.at[0]),
        pltpu.make_async_copy(proj_ref, proj_out, sems.at[1]),
    ]
    for copy in copies:
        copy.start()
    for copy in copies:
        copy.wait()


def staged(w_qkv, w_proj):
    return pl.pallas_call(
        stage_kernel,
        out_shape=(
            pltpu.VMEM(w_qkv.shape, w_qkv.dtype),
            pltpu.VMEM(w_proj.shape, w_proj.dtype),
        ),
        in_specs=[pl.BlockSpec(memory_space=pltpu.HBM)] * 2,
        out_specs=(pl.BlockSpec(memory_space=pltpu.VMEM),) * 2,
        scratch_shapes=[pltpu.SemaphoreType.DMA((2,))],
        compiler_params=pltpu.CompilerParams(vmem_limit_bytes=4 * 1024 * 1024),
        cost_estimate=pl.CostEstimate(flops=0, bytes_accessed=4 * 1024 * 1024, transcendentals=0),
        name="stage_weights",
    )(w_qkv, w_proj)


def part(value, at, refs):
    own_ref, left_ref = refs
    for level in range(LEV):
        for row in range(WLAT):
            base = (level * WLAT + row) * WLON
            tokens = jnp.concatenate([value[base:base + WLON], value[WT + base:WT + base + WLON]], axis=0)
            left_ref[at, level, row] = tokens[:SLON].astype(jnp.bfloat16)
            own_ref[at, level, row] = tokens[SLON:].astype(jnp.bfloat16)


def rest_kernel(
    n_ref, m_ref, gp_ref, u_ref, x_ref, mix_ref, qkv_ref, proj_ref,
    half_ref, own_ref, left_ref,
    wqkv_ref, wproj_ref, sems,
):
    copies = [
        pltpu.make_async_copy(proj_ref, wproj_ref, sems.at[0]),
        pltpu.make_async_copy(qkv_ref, wqkv_ref, sems.at[1]),
    ]
    for copy in copies:
        copy.start()
    grads = jnp.concatenate([dot(n_ref[...], gp_ref[...]), dot(m_ref[...], u_ref[...])], axis=1)
    store_shares(half_ref, grads)
    refs = (own_ref, left_ref)
    x = x_ref[...].astype(jnp.float32)
    copies[0].wait()
    part(x + dot(mix_ref[...], wproj_ref[...]), 0, refs)
    normed, inverse = statistics(x)
    copies[1].wait()
    grad_normed = dot(gp_ref[...], wqkv_ref[...], NT)
    grad_tokens = inverse * (
        grad_normed
        - jnp.mean(grad_normed, -1, keepdims=True)
        - normed * jnp.mean(grad_normed * normed, -1, keepdims=True)
    )
    part(u_ref[...].astype(jnp.float32) + grad_tokens, 1, refs)


def call(kernel, name, outs, scratch, flops, *args, dtypes=None, limit=12, placed=False, any_args=()):
    vmem = pl.BlockSpec(memory_space=pltpu.VMEM)
    dtypes = dtypes or (jnp.bfloat16,) * len(outs)
    make = pltpu.VMEM if placed else jax.ShapeDtypeStruct
    size = sum(2 * math.prod(shape) for shape in outs)
    return pl.pallas_call(
        kernel,
        out_shape=tuple(make(shape, dtype) for shape, dtype in zip(outs, dtypes)),
        in_specs=[
            pl.BlockSpec(memory_space=pltpu.HBM) if at in any_args else vmem for at in range(len(args))
        ],
        out_specs=(vmem,) * len(outs),
        scratch_shapes=[
            pltpu.SemaphoreType.DMA(shape) if kind is None else pltpu.VMEM(shape, kind)
            for shape, kind in scratch
        ],
        compiler_params=pltpu.CompilerParams(vmem_limit_bytes=limit * 1024 * 1024),
        cost_estimate=pl.CostEstimate(flops=flops, bytes_accessed=2 * size, transcendentals=0),
        name=name,
    )(*args)


def attention(x, u, upper, corner, left, lrow, lcol, w_qkv, w_proj):
    tokens = math.prod(x.shape[:-1])
    low, full = jnp.bfloat16, jnp.float32
    return call(
        attention_kernel,
        "window_attention",
        (
            (32, 2, 64, 128), (tokens, 3 * D), (tokens, D),
            (D // 2, tokens), (D // 2, tokens), (tokens, D), (tokens, D),
        ),
        (
            ((tokens, D), full),
            ((tokens, 3 * D), low),
            ((tokens, D), low),
            ((D, tokens), low),
            ((D, tokens), low),
            ((WT, WIDE), low),
            ((WT, WIDE), low),
            ((LANES, WIDE), full),
            ((WT, WIDE), full),
            ((WIDE, LANES), low),
            ((WIDE, LANES), low),
        ),
        5_000_000_000,
        x, u, upper, corner, left, lrow, lcol, w_qkv, w_proj,
        limit=20,
    )


LAT = ("yh", "x", "core")


def passed_along(value, axis, steps):
    count = lax.axis_size(axis)
    pairs = [(source, (source + steps) % count) for source in range(count)]
    return lax.ppermute(value, axis, pairs)


def diagonal(value, steps):
    n_lat, n_lon = lax.axis_size(LAT), lax.axis_size("lon")
    pairs = [
        (a * n_lon + b, (a + steps) % n_lat * n_lon + (b + steps) % n_lon)
        for a in range(n_lat)
        for b in range(n_lon)
    ]
    return lax.ppermute(value, (*LAT, "lon"), pairs)


def per_device(inputs, cotangent, mask_ids, w_qkv, w_proj):
    body = (2, LEV, SLAT, inputs.shape[3] - SLON, D)
    side = (2, LEV, SLAT, SLON, D)
    upper, corner, left = call(
        cut_kernel, "cut_halos", (body, side, side),
        (((2, *inputs.shape[1:]), jnp.bfloat16), ((2, LEV), None)), 1000,
        *(pltpu.with_memory_space_constraint(array, pltpu.HBM) for array in (inputs, cotangent)),
        limit=8, any_args=(0, 1),
    )
    upper = passed_along(upper, LAT, 1)
    corner = diagonal(corner, 1)
    left = passed_along(left, "lon", 1)
    first_band = lax.axis_index(LAT) == 0
    wrapped = jnp.logical_and(first_band, jnp.arange(WLAT) < SLAT).astype(jnp.int32)
    groups = mask_ids + 4 * wrapped[:, None]
    windows = groups.shape[1] // WLON
    labels = groups.reshape(WLAT, windows, WLON).transpose(1, 0, 2).reshape(windows, WLAT * WLON)
    labels = jnp.tile(labels, (1, LEV))
    lcol = labels.reshape(windows * WT, 1)
    lrow = jnp.concatenate([labels[:, :MAIN], jnp.tile(labels[:, MAIN:], (1, PER))], axis=1)
    send, gp, mix, nkeep, mkeep, x, u = attention(
        inputs, cotangent, upper, corner, left, lrow, lcol, *staged(w_qkv, w_proj)
    )
    got = passed_along(send, "core", 1)
    half, own, left = call(
        rest_kernel, "own_half_and_outputs",
        (send.shape, (2, *inputs.shape[1:3], body[3], D), (2, *inputs.shape[1:3], SLON, D)),
        ((w_qkv.shape, jnp.bfloat16), (w_proj.shape, jnp.bfloat16), ((2,), None)), 600_000_000,
        nkeep, mkeep, gp, u, x, mix, w_qkv, w_proj,
        dtypes=(jnp.float32,) + (jnp.bfloat16,) * 2, any_args=(6, 7), limit=16,
    )
    ranks = (2, 4, 8, 64, 128)
    (sums,) = call(
        add_kernel, "add_halves", ((4, 2, 8, 64, 128),), (), 1_000_000,
        half.reshape(ranks), got.reshape(ranks), placed=True,
    )
    right = passed_along(left, "lon", -1)
    spread = lax.all_to_all(sums.reshape(8, 512, 128), ("x", "yh"), 0, 0, tiled=True)
    spread, right = lax.optimization_barrier((spread, right))
    (sums,) = call(sum_kernel, "sum_parts", ((8, 2, 64, 128),), (), 1_000_000, spread, placed=True)
    spread = lax.all_to_all(sums.reshape(16, 64, 128), ("lon", "dp"), 0, 0, tiled=True)
    grad_qkv, grad_proj = call(
        last_kernel, "last_sum", ((4, 3 * D), (4, D)), (), 1000, spread,
        dtypes=(jnp.float32,) * 2, limit=4,
    )
    (rows,) = call(rows_kernel, "halo_rows", ((2, LEV, SLAT, *inputs.shape[3:]),), (), 1000, own, right, limit=8)
    lower = passed_along(rows, LAT, -1)
    output, grad_inputs = call(
        join_kernel, "join_outputs", (inputs.shape, inputs.shape), (), 1000, own, right, lower, limit=8
    )
    return (output, grad_inputs, grad_qkv, grad_proj)


def solution(mesh):
    mesh = Mesh(mesh.devices.reshape(2, 2, 4, 2, 8), ("dp", "yh", "x", "core", "lon"))
    tokens = P("dp", None, LAT, "lon", None)
    return jax.shard_map(
        per_device,
        mesh=mesh,
        in_specs=(tokens, tokens, P(LAT, "lon"), P(), P()),
        out_specs=(tokens, tokens, P((*LAT, "lon"), None), P((*LAT, "lon"), None)),
        check_vma=False,
    )
```

```python
import functools
import math

import jax
import jax.numpy as jnp
from jax import lax
from jax.experimental import pallas as pl
from jax.experimental.pallas import tpu as pltpu
from jax.sharding import Mesh
from jax.sharding import PartitionSpec as P

D = 512
HEADS = 16
HD = 32
LEV = 2
WLAT = 6
WLON = 12
SLAT = 3
SLON = 6
WT = LEV * WLAT * WLON
PER = 8
LANES = PER * HD
MAIN = 128
REST = WT - MAIN
WIDE = PER * WT
UNITS = D // LANES
FACTOR = 1.0 / math.sqrt(HD)
LOG2E = 1.4426950408889634

NN = (((1,), (0,)), ((), ()))
NT = (((1,), (1,)), ((), ()))


def dot(left, right, dims=NN):
    return lax.dot_general(left, right, dims, preferred_element_type=jnp.float32)


def cut_kernel(x_ref, u_ref, upper_ref, corner_ref, left_ref, held_ref, sems):
    copies = []
    for at, ref in enumerate((x_ref, u_ref)):
        for level in range(LEV):
            copies.append(pltpu.make_async_copy(ref.at[0, level], held_ref.at[at, level], sems.at[at, level]))
    for copy in copies:
        copy.start()
    for copy in copies:
        copy.wait()
    for at in range(2):
        for level in range(LEV):
            for row in range(WLAT):
                tokens = held_ref[at, level, row].astype(jnp.float32)
                side = tokens[-SLON:].astype(jnp.bfloat16)
                if row < SLAT:
                    left_ref[at, level, row] = side
                else:
                    corner_ref[at, level, row - SLAT] = side
                    upper_ref[at, level, row - SLAT] = tokens[:-SLON].astype(jnp.bfloat16)


def joined(body, side):
    both = jnp.concatenate([body.astype(jnp.float32), side.astype(jnp.float32)], axis=0)
    return both.astype(jnp.bfloat16)


def rows_kernel(own_ref, right_ref, rows_ref):
    for at in range(2):
        for level in range(LEV):
            for row in range(SLAT):
                rows_ref[at, level, row] = joined(own_ref[at, level, row], right_ref[at, level, row])


def join_kernel(own_ref, right_ref, lower_ref, out_ref, gin_ref):
    for at, ref in enumerate((out_ref, gin_ref)):
        for level in range(LEV):
            for row in range(SLAT):
                ref[0, level, row] = joined(own_ref[at, level, SLAT + row], right_ref[at, level, SLAT + row])
                ref[0, level, SLAT + row] = lower_ref[at, level, row]


def assemble(target_ref, at, own_ref, upper_ref, corner_ref, left_ref):
    pieces = ([], [])
    for level in range(LEV):
        for row in range(WLAT):
            if row < SLAT:
                side, body = corner_ref[at, level, row], upper_ref[at, level, row]
            else:
                side, body = left_ref[at, level, row - SLAT], own_ref[0, level, row - SLAT]
            side, body = side.astype(jnp.float32), body.astype(jnp.float32)
            pieces[0].append(side)
            pieces[0].append(body[:WLON - SLON])
            pieces[1].append(body[WLON - SLON:2 * WLON - SLON])
    for w in range(2):
        target_ref[w * WT:(w + 1) * WT, :] = jnp.concatenate(pieces[w], axis=0)


def statistics(x):
    center = jnp.mean(x, -1, keepdims=True)
    shifted = x - center
    inverse = lax.rsqrt(jnp.mean(shifted * shifted, -1, keepdims=True) + 1e-05)
    return shifted * inverse, inverse


def store_shares(target_ref, grads):
    count = grads.shape[0]
    first = lax.broadcasted_iota(jnp.int32, (count, 128), 0) % 8 < 4
    for quad in range(4):
        shares = ([], [])
        for pair in (2 * quad, 2 * quad + 1):
            left = grads[:, pair * 256:pair * 256 + 128]
            right = grads[:, pair * 256 + 128:pair * 256 + 256]
            shares[0].append(jnp.where(first, left, pltpu.roll(right, 4, 0)))
            shares[1].append(jnp.where(first, pltpu.roll(left, count - 4, 0), right))
        rows = slice(quad * 16, quad * 16 + 16)
        for which in range(2):
            piece = jnp.concatenate([p.reshape(count // 8, 8, 128) for p in shares[which]], axis=1)
            target_ref[:, which, rows, :] = piece.astype(target_ref.dtype)


def attention_kernel(
    own_x_ref, own_u_ref, upper_ref, corner_ref, left_ref, lrow_ref, lcol_ref, wqkv_ref, wproj_ref,
    send_ref, gp_ref, mix_ref, nkeep_ref, mkeep_ref, x_ref, u_ref,
    full_ref, proj_ref, gm_ref, nt_ref, mt_ref, al_ref, gl_ref, s_ref, da_ref, qs_ref, gs_ref,
):
    windows = x_ref.shape[0] // WT
    core = lax.axis_index("core")
    half = D // 2
    assemble(full_ref, 1, own_u_ref, upper_ref, corner_ref, left_ref)
    u_ref[...] = full_ref[...].astype(jnp.bfloat16)
    assemble(full_ref, 0, own_x_ref, upper_ref, corner_ref, left_ref)
    x_ref[...] = full_ref[...].astype(jnp.bfloat16)
    normed, _ = statistics(full_ref[...])
    normed_low = normed.astype(jnp.bfloat16)
    proj_ref[...] = dot(normed_low, wqkv_ref[...]).astype(jnp.bfloat16)
    gm_ref[...] = dot(u_ref[...], wproj_ref[...], NT).astype(jnp.bfloat16)

    def place(target_ref, array):
        for b in range(D // 32):
            slot = lax.bitwise_xor(core, b % 2)
            row = pl.multiple_of(slot * half + (b // 2) * 32, 32)
            target_ref[pl.ds(row, 32), :] = array[b * 32:(b + 1) * 32, :]

    place(nt_ref, normed_low.T)

    lane = lax.broadcasted_iota(jnp.int32, (1, LANES), 1) // HD
    masks = [(lane == h).astype(jnp.float32) for h in range(PER)]
    low_masks = [m.astype(jnp.bfloat16) for m in masks]
    tiles = [slice(t * MAIN, (t + 1) * MAIN) for t in range(PER + 1)]

    def stack(target_ref, array):
        for h in range(PER):
            target_ref[tiles[h], :] = array[:MAIN] * low_masks[h]
            rest = PER * MAIN + h * REST
            target_ref[rest:rest + REST, :] = array[MAIN:] * low_masks[h]

    def mix(target_ref, rows, cols, left, weights_ref):
        turned = left.T
        for pair in range(PER // 2):
            both = slice(pair * 2 * MAIN, (pair + 1) * 2 * MAIN)
            mixed = dot(turned[pair * 2 * HD:(pair + 1) * 2 * HD, :], weights_ref[:, both])
            s_ref[pair * 2 * HD:pair * 2 * HD + HD, :MAIN] = mixed[:HD, :MAIN]
            s_ref[pair * 2 * HD + HD:(pair + 1) * 2 * HD, :MAIN] = mixed[HD:, MAIN:]
        rest = dot(weights_ref[:, tiles[PER]].T, left)
        total = rest[:REST] * masks[0]
        for h in range(1, PER):
            total = total + rest[h * REST:(h + 1) * REST] * masks[h]
        target_ref[rows.start:rows.start + MAIN, cols] = s_ref[:LANES, :MAIN].T.astype(jnp.bfloat16)
        target_ref[rows.start + MAIN:rows.stop, cols] = total.astype(jnp.bfloat16)

    for w in range(windows):
        rows = slice(w * WT, (w + 1) * WT)
        labels = lcol_ref[rows, :]
        allowed = [labels == lrow_ref[w:w + 1, tiles[at]] for at in range(2)]
        for g in range(UNITS):
            q_cols, k_cols, v_cols = (
                slice(part * D + g * LANES, part * D + (g + 1) * LANES) for part in range(3)
            )
            k = proj_ref[rows, k_cols]
            v = proj_ref[rows, v_cols]
            stack(qs_ref, proj_ref[rows, q_cols])
            stack(gs_ref, gm_ref[rows, q_cols])
            s_ref[:WT, :] = dot(k, qs_ref[...], NT)
            da_ref[...] = dot(v, gs_ref[...], NT)
            for t in range(PER + 1):
                s = jnp.where(allowed[t // PER], s_ref[:WT, tiles[t]], jnp.float32(-1e30))
                e = jnp.exp2((s - jnp.max(s, 0, keepdims=True)) * jnp.float32(FACTOR * LOG2E))
                a = e * (1.0 / jnp.sum(e, 0, keepdims=True))
                al_ref[:, tiles[t]] = a.astype(jnp.bfloat16)
                ga = da_ref[:, tiles[t]] * a
                gl = (ga - a * jnp.sum(ga, 0, keepdims=True)) * jnp.float32(FACTOR)
                gl_ref[:, tiles[t]] = gl.astype(jnp.bfloat16)
            gp_ref[rows, k_cols] = dot(gl_ref[...], qs_ref[...]).astype(jnp.bfloat16)
            gp_ref[rows, v_cols] = dot(al_ref[...], gs_ref[...]).astype(jnp.bfloat16)
            mix(mix_ref, rows, q_cols, v, al_ref)
            mix(gp_ref, rows, q_cols, k, gl_ref)

    place(mt_ref, mix_ref[...].T)
    nkeep_ref[...] = nt_ref[:half, :]
    mkeep_ref[...] = mt_ref[:half, :]
    grads = jnp.concatenate([dot(nt_ref[half:, :], gp_ref[...]), dot(mt_ref[half:, :], u_ref[...])], axis=1)
    store_shares(send_ref, grads)


def add_kernel(own_ref, got_ref, sum_ref):
    for yh in range(own_ref.shape[0]):
        for x in range(own_ref.shape[1]):
            total = own_ref[yh, x] + got_ref[yh, x].astype(jnp.float32)
            sum_ref[x, yh] = total.astype(jnp.bfloat16)


def added(parts_ref):
    total = parts_ref[0].astype(jnp.float32)
    for at in range(1, parts_ref.shape[0]):
        total = total + parts_ref[at].astype(jnp.float32)
    return total


def sum_kernel(parts_ref, sum_ref):
    total = added(parts_ref).astype(jnp.bfloat16)
    sum_ref[0] = total
    sum_ref[1] = total


def last_kernel(parts_ref, qkv_ref, proj_ref):
    total = added(parts_ref)
    for tile in range(16):
        piece = total[tile * 4:tile * 4 + 4, :]
        if tile < 12:
            qkv_ref[:, tile * 128:(tile + 1) * 128] = piece
        else:
            proj_ref[:, (tile - 12) * 128:(tile - 11) * 128] = piece


def stage_kernel(qkv_ref, proj_ref, qkv_out, proj_out, sems):
    copies = [
        pltpu.make_async_copy(qkv_ref, qkv_out, sems.at[0]),
        pltpu.make_async_copy(proj_ref, proj_out, sems.at[1]),
    ]
    for copy in copies:
        copy.start()
    for copy in copies:
        copy.wait()


def staged(w_qkv, w_proj):
    return pl.pallas_call(
        stage_kernel,
        out_shape=(
            pltpu.VMEM(w_qkv.shape, w_qkv.dtype),
            pltpu.VMEM(w_proj.shape, w_proj.dtype),
        ),
        in_specs=[pl.BlockSpec(memory_space=pltpu.HBM)] * 2,
        out_specs=(pl.BlockSpec(memory_space=pltpu.VMEM),) * 2,
        scratch_shapes=[pltpu.SemaphoreType.DMA((2,))],
        compiler_params=pltpu.CompilerParams(vmem_limit_bytes=4 * 1024 * 1024),
        cost_estimate=pl.CostEstimate(flops=0, bytes_accessed=4 * 1024 * 1024, transcendentals=0),
        name="stage_weights",
    )(w_qkv, w_proj)


def part(value, at, refs):
    own_ref, left_ref = refs
    for level in range(LEV):
        for row in range(WLAT):
            base = (level * WLAT + row) * WLON
            tokens = jnp.concatenate([value[base:base + WLON], value[WT + base:WT + base + WLON]], axis=0)
            left_ref[at, level, row] = tokens[:SLON].astype(jnp.bfloat16)
            own_ref[at, level, row] = tokens[SLON:].astype(jnp.bfloat16)


def rest_kernel(
    n_ref, m_ref, gp_ref, u_ref, x_ref, mix_ref, qkv_ref, proj_ref,
    half_ref, own_ref, left_ref,
    wqkv_ref, wproj_ref, sems,
):
    copies = [
        pltpu.make_async_copy(proj_ref, wproj_ref, sems.at[0]),
        pltpu.make_async_copy(qkv_ref, wqkv_ref, sems.at[1]),
    ]
    for copy in copies:
        copy.start()
    grads = jnp.concatenate([dot(n_ref[...], gp_ref[...]), dot(m_ref[...], u_ref[...])], axis=1)
    store_shares(half_ref, grads)
    refs = (own_ref, left_ref)
    x = x_ref[...].astype(jnp.float32)
    copies[0].wait()
    part(x + dot(mix_ref[...], wproj_ref[...]), 0, refs)
    normed, inverse = statistics(x)
    copies[1].wait()
    grad_normed = dot(gp_ref[...], wqkv_ref[...], NT)
    grad_tokens = inverse * (
        grad_normed
        - jnp.mean(grad_normed, -1, keepdims=True)
        - normed * jnp.mean(grad_normed * normed, -1, keepdims=True)
    )
    part(u_ref[...].astype(jnp.float32) + grad_tokens, 1, refs)


def call(kernel, name, outs, scratch, flops, *args, dtypes=None, limit=12, placed=False, any_args=()):
    vmem = pl.BlockSpec(memory_space=pltpu.VMEM)
    dtypes = dtypes or (jnp.bfloat16,) * len(outs)
    make = pltpu.VMEM if placed else jax.ShapeDtypeStruct
    size = sum(2 * math.prod(shape) for shape in outs)
    return pl.pallas_call(
        kernel,
        out_shape=tuple(make(shape, dtype) for shape, dtype in zip(outs, dtypes)),
        in_specs=[
            pl.BlockSpec(memory_space=pltpu.HBM) if at in any_args else vmem for at in range(len(args))
        ],
        out_specs=(vmem,) * len(outs),
        scratch_shapes=[
            pltpu.SemaphoreType.DMA(shape) if kind is None else pltpu.VMEM(shape, kind)
            for shape, kind in scratch
        ],
        compiler_params=pltpu.CompilerParams(vmem_limit_bytes=limit * 1024 * 1024),
        cost_estimate=pl.CostEstimate(flops=flops, bytes_accessed=2 * size, transcendentals=0),
        name=name,
    )(*args)


def attention(x, u, upper, corner, left, lrow, lcol, w_qkv, w_proj):
    tokens = math.prod(x.shape[:-1])
    low, full = jnp.bfloat16, jnp.float32
    return call(
        attention_kernel,
        "window_attention",
        (
            (32, 2, 64, 128), (tokens, 3 * D), (tokens, D),
            (D // 2, tokens), (D // 2, tokens), (tokens, D), (tokens, D),
        ),
        (
            ((tokens, D), full),
            ((tokens, 3 * D), low),
            ((tokens, D), low),
            ((D, tokens), low),
            ((D, tokens), low),
            ((WT, WIDE), low),
            ((WT, WIDE), low),
            ((LANES, WIDE), full),
            ((WT, WIDE), full),
            ((WIDE, LANES), low),
            ((WIDE, LANES), low),
        ),
        5_000_000_000,
        x, u, upper, corner, left, lrow, lcol, w_qkv, w_proj,
        limit=20,
    )


LAT = ("yh", "x", "core")


def passed_along(value, axis, steps):
    count = lax.axis_size(axis)
    pairs = [(source, (source + steps) % count) for source in range(count)]
    return lax.ppermute(value, axis, pairs)


def diagonal(value, steps):
    n_lat, n_lon = lax.axis_size(LAT), lax.axis_size("lon")
    pairs = [
        (a * n_lon + b, (a + steps) % n_lat * n_lon + (b + steps) % n_lon)
        for a in range(n_lat)
        for b in range(n_lon)
    ]
    return lax.ppermute(value, (*LAT, "lon"), pairs)


def per_device(inputs, cotangent, mask_ids, w_qkv, w_proj):
    body = (2, LEV, SLAT, inputs.shape[3] - SLON, D)
    side = (2, LEV, SLAT, SLON, D)
    upper, corner, left = call(
        cut_kernel, "cut_halos", (body, side, side),
        (((2, *inputs.shape[1:]), jnp.bfloat16), ((2, LEV), None)), 1000,
        *(pltpu.with_memory_space_constraint(array, pltpu.HBM) for array in (inputs, cotangent)),
        limit=8, any_args=(0, 1),
    )
    upper = passed_along(upper, LAT, 1)
    corner = diagonal(corner, 1)
    left = passed_along(left, "lon", 1)
    first_band = lax.axis_index(LAT) == 0
    wrapped = jnp.logical_and(first_band, jnp.arange(WLAT) < SLAT).astype(jnp.int32)
    groups = mask_ids + 4 * wrapped[:, None]
    windows = groups.shape[1] // WLON
    labels = groups.reshape(WLAT, windows, WLON).transpose(1, 0, 2).reshape(windows, WLAT * WLON)
    labels = jnp.tile(labels, (1, LEV))
    lcol = labels.reshape(windows * WT, 1)
    lrow = jnp.concatenate([labels[:, :MAIN], jnp.tile(labels[:, MAIN:], (1, PER))], axis=1)
    send, gp, mix, nkeep, mkeep, x, u = attention(
        inputs, cotangent, upper, corner, left, lrow, lcol, *staged(w_qkv, w_proj)
    )
    got = passed_along(send, "core", 1)
    half, own, left = call(
        rest_kernel, "own_half_and_outputs",
        (send.shape, (2, *inputs.shape[1:3], body[3], D), (2, *inputs.shape[1:3], SLON, D)),
        ((w_qkv.shape, jnp.bfloat16), (w_proj.shape, jnp.bfloat16), ((2,), None)), 600_000_000,
        nkeep, mkeep, gp, u, x, mix, w_qkv, w_proj,
        dtypes=(jnp.float32,) + (jnp.bfloat16,) * 2, any_args=(6, 7), limit=16,
    )
    ranks = (2, 4, 8, 64, 128)
    (sums,) = call(
        add_kernel, "add_halves", ((4, 2, 8, 64, 128),), (), 1_000_000,
        half.reshape(ranks), got.reshape(ranks), placed=True,
    )
    right = passed_along(left, "lon", -1)
    spread = lax.all_to_all(sums.reshape(8, 512, 128), ("x", "yh"), 0, 0, tiled=True)
    spread, right = lax.optimization_barrier((spread, right))
    (sums,) = call(sum_kernel, "sum_parts", ((2, 512, 128),), (), 1_000_000, spread, placed=True)
    spread = lax.all_to_all(sums.reshape(16, 64, 128), ("dp", "lon"), 0, 0, tiled=True)
    grad_qkv, grad_proj = call(
        last_kernel, "last_sum", ((4, 3 * D), (4, D)), (), 1000, spread,
        dtypes=(jnp.float32,) * 2, limit=4,
    )
    (rows,) = call(rows_kernel, "halo_rows", ((2, LEV, SLAT, *inputs.shape[3:]),), (), 1000, own, right, limit=8)
    lower = passed_along(rows, LAT, -1)
    output, grad_inputs = call(
        join_kernel, "join_outputs", (inputs.shape, inputs.shape), (), 1000, own, right, lower, limit=8
    )
    return (output, grad_inputs, grad_qkv, grad_proj)


def solution(mesh):
    mesh = Mesh(mesh.devices.reshape(2, 2, 4, 2, 8), ("dp", "yh", "x", "core", "lon"))
    tokens = P("dp", None, LAT, "lon", None)
    return jax.shard_map(
        per_device,
        mesh=mesh,
        in_specs=(tokens, tokens, P(LAT, "lon"), P(), P()),
        out_specs=(tokens, tokens, P((*LAT, "lon"), None), P((*LAT, "lon"), None)),
        check_vma=False,
    )
```

```python
import functools
import math

import jax
import jax.numpy as jnp
from jax import lax
from jax.experimental import pallas as pl
from jax.experimental.pallas import tpu as pltpu
from jax.sharding import Mesh
from jax.sharding import PartitionSpec as P

D = 512
HEADS = 16
HD = 32
LEV = 2
WLAT = 6
WLON = 12
SLAT = 3
SLON = 6
WT = LEV * WLAT * WLON
PER = 8
LANES = PER * HD
MAIN = 128
REST = WT - MAIN
WIDE = PER * WT
UNITS = D // LANES
FACTOR = 1.0 / math.sqrt(HD)
LOG2E = 1.4426950408889634

NN = (((1,), (0,)), ((), ()))
NT = (((1,), (1,)), ((), ()))


def dot(left, right, dims=NN):
    return lax.dot_general(left, right, dims, preferred_element_type=jnp.float32)


def cut_kernel(x_ref, u_ref, upper_ref, corner_ref, left_ref, held_ref, sems):
    copies = []
    for at, ref in enumerate((x_ref, u_ref)):
        for level in range(LEV):
            copies.append(pltpu.make_async_copy(ref.at[0, level], held_ref.at[at, level], sems.at[at, level]))
    for copy in copies:
        copy.start()
    for at in range(2):
        for level in range(LEV):
            copies[at * LEV + level].wait()
            for row in range(WLAT):
                tokens = held_ref[at, level, row].astype(jnp.float32)
                side = tokens[-SLON:].astype(jnp.bfloat16)
                if row < SLAT:
                    left_ref[at, level, row] = side
                else:
                    corner_ref[at, level, row - SLAT] = side
                    upper_ref[at, level, row - SLAT] = tokens[:-SLON].astype(jnp.bfloat16)


def joined(body, side):
    both = jnp.concatenate([body.astype(jnp.float32), side.astype(jnp.float32)], axis=0)
    return both.astype(jnp.bfloat16)


def rows_kernel(own_ref, right_ref, rows_ref):
    for at in range(2):
        for level in range(LEV):
            for row in range(SLAT):
                rows_ref[at, level, row] = joined(own_ref[at, level, row], right_ref[at, level, row])


def join_kernel(own_ref, right_ref, lower_ref, out_ref, gin_ref):
    for at, ref in enumerate((out_ref, gin_ref)):
        for level in range(LEV):
            for row in range(SLAT):
                ref[0, level, row] = joined(own_ref[at, level, SLAT + row], right_ref[at, level, SLAT + row])
                ref[0, level, SLAT + row] = lower_ref[at, level, row]


def assemble(target_ref, at, own_ref, upper_ref, corner_ref, left_ref):
    pieces = ([], [])
    for level in range(LEV):
        for row in range(WLAT):
            if row < SLAT:
                side, body = corner_ref[at, level, row], upper_ref[at, level, row]
            else:
                side, body = left_ref[at, level, row - SLAT], own_ref[0, level, row - SLAT]
            side, body = side.astype(jnp.float32), body.astype(jnp.float32)
            pieces[0].append(side)
            pieces[0].append(body[:WLON - SLON])
            pieces[1].append(body[WLON - SLON:2 * WLON - SLON])
    for w in range(2):
        target_ref[w * WT:(w + 1) * WT, :] = jnp.concatenate(pieces[w], axis=0)


def statistics(x):
    center = jnp.mean(x, -1, keepdims=True)
    shifted = x - center
    inverse = lax.rsqrt(jnp.mean(shifted * shifted, -1, keepdims=True) + 1e-05)
    return shifted * inverse, inverse


def store_shares(target_ref, grads):
    count = grads.shape[0]
    first = lax.broadcasted_iota(jnp.int32, (count, 128), 0) % 8 < 4
    for quad in range(4):
        shares = ([], [])
        for pair in (2 * quad, 2 * quad + 1):
            left = grads[:, pair * 256:pair * 256 + 128]
            right = grads[:, pair * 256 + 128:pair * 256 + 256]
            shares[0].append(jnp.where(first, left, pltpu.roll(right, 4, 0)))
            shares[1].append(jnp.where(first, pltpu.roll(left, count - 4, 0), right))
        rows = slice(quad * 16, quad * 16 + 16)
        for which in range(2):
            piece = jnp.concatenate([p.reshape(count // 8, 8, 128) for p in shares[which]], axis=1)
            target_ref[:, which, rows, :] = piece.astype(target_ref.dtype)


def attention_kernel(
    own_x_ref, own_u_ref, upper_ref, corner_ref, left_ref, lrow_ref, lcol_ref, wqkv_ref, wproj_ref,
    send_ref, gp_ref, mix_ref, nkeep_ref, mkeep_ref, x_ref, u_ref,
    full_ref, proj_ref, gm_ref, nt_ref, mt_ref, al_ref, gl_ref, s_ref, da_ref, qs_ref, gs_ref,
):
    windows = x_ref.shape[0] // WT
    core = lax.axis_index("core")
    half = D // 2
    assemble(full_ref, 1, own_u_ref, upper_ref, corner_ref, left_ref)
    u_ref[...] = full_ref[...].astype(jnp.bfloat16)
    assemble(full_ref, 0, own_x_ref, upper_ref, corner_ref, left_ref)
    x_ref[...] = full_ref[...].astype(jnp.bfloat16)
    normed, _ = statistics(full_ref[...])
    normed_low = normed.astype(jnp.bfloat16)
    proj_ref[...] = dot(normed_low, wqkv_ref[...]).astype(jnp.bfloat16)
    gm_ref[...] = dot(u_ref[...], wproj_ref[...], NT).astype(jnp.bfloat16)

    def place(target_ref, array):
        for b in range(D // 32):
            slot = lax.bitwise_xor(core, b % 2)
            row = pl.multiple_of(slot * half + (b // 2) * 32, 32)
            target_ref[pl.ds(row, 32), :] = array[b * 32:(b + 1) * 32, :]

    place(nt_ref, normed_low.T)

    lane = lax.broadcasted_iota(jnp.int32, (1, LANES), 1) // HD
    masks = [(lane == h).astype(jnp.float32) for h in range(PER)]
    low_masks = [m.astype(jnp.bfloat16) for m in masks]
    tiles = [slice(t * MAIN, (t + 1) * MAIN) for t in range(PER + 1)]

    def stack(target_ref, array):
        for h in range(PER):
            target_ref[tiles[h], :] = array[:MAIN] * low_masks[h]
            rest = PER * MAIN + h * REST
            target_ref[rest:rest + REST, :] = array[MAIN:] * low_masks[h]

    def mix(target_ref, rows, cols, left, weights_ref):
        turned = left.T
        for pair in range(PER // 2):
            both = slice(pair * 2 * MAIN, (pair + 1) * 2 * MAIN)
            mixed = dot(turned[pair * 2 * HD:(pair + 1) * 2 * HD, :], weights_ref[:, both])
            s_ref[pair * 2 * HD:pair * 2 * HD + HD, :MAIN] = mixed[:HD, :MAIN]
            s_ref[pair * 2 * HD + HD:(pair + 1) * 2 * HD, :MAIN] = mixed[HD:, MAIN:]
        rest = dot(weights_ref[:, tiles[PER]].T, left)
        total = rest[:REST] * masks[0]
        for h in range(1, PER):
            total = total + rest[h * REST:(h + 1) * REST] * masks[h]
        target_ref[rows.start:rows.start + MAIN, cols] = s_ref[:LANES, :MAIN].T.astype(jnp.bfloat16)
        target_ref[rows.start + MAIN:rows.stop, cols] = total.astype(jnp.bfloat16)

    for w in range(windows):
        rows = slice(w * WT, (w + 1) * WT)
        labels = lcol_ref[rows, :]
        allowed = [labels == lrow_ref[w:w + 1, tiles[at]] for at in range(2)]
        for g in range(UNITS):
            q_cols, k_cols, v_cols = (
                slice(part * D + g * LANES, part * D + (g + 1) * LANES) for part in range(3)
            )
            k = proj_ref[rows, k_cols]
            v = proj_ref[rows, v_cols]
            stack(qs_ref, proj_ref[rows, q_cols])
            stack(gs_ref, gm_ref[rows, q_cols])
            s_ref[:WT, :] = dot(k, qs_ref[...], NT)
            da_ref[...] = dot(v, gs_ref[...], NT)
            for t in range(PER + 1):
                s = jnp.where(allowed[t // PER], s_ref[:WT, tiles[t]], jnp.float32(-1e30))
                e = jnp.exp2((s - jnp.max(s, 0, keepdims=True)) * jnp.float32(FACTOR * LOG2E))
                a = e * (1.0 / jnp.sum(e, 0, keepdims=True))
                al_ref[:, tiles[t]] = a.astype(jnp.bfloat16)
                ga = da_ref[:, tiles[t]] * a
                gl = (ga - a * jnp.sum(ga, 0, keepdims=True)) * jnp.float32(FACTOR)
                gl_ref[:, tiles[t]] = gl.astype(jnp.bfloat16)
            gp_ref[rows, k_cols] = dot(gl_ref[...], qs_ref[...]).astype(jnp.bfloat16)
            gp_ref[rows, v_cols] = dot(al_ref[...], gs_ref[...]).astype(jnp.bfloat16)
            mix(mix_ref, rows, q_cols, v, al_ref)
            mix(gp_ref, rows, q_cols, k, gl_ref)

    place(mt_ref, mix_ref[...].T)
    nkeep_ref[...] = nt_ref[:half, :]
    mkeep_ref[...] = mt_ref[:half, :]
    grads = jnp.concatenate([dot(nt_ref[half:, :], gp_ref[...]), dot(mt_ref[half:, :], u_ref[...])], axis=1)
    store_shares(send_ref, grads)


def add_kernel(own_ref, got_ref, sum_ref):
    for yh in range(own_ref.shape[0]):
        for x in range(own_ref.shape[1]):
            total = own_ref[yh, x] + got_ref[yh, x].astype(jnp.float32)
            sum_ref[x, yh] = total.astype(jnp.bfloat16)


def added(parts_ref):
    total = parts_ref[0].astype(jnp.float32)
    for at in range(1, parts_ref.shape[0]):
        total = total + parts_ref[at].astype(jnp.float32)
    return total


def sum_kernel(parts_ref, sum_ref):
    total = added(parts_ref).astype(jnp.bfloat16)
    sum_ref[0] = total
    sum_ref[1] = total


def last_kernel(parts_ref, qkv_ref, proj_ref):
    total = added(parts_ref)
    for tile in range(16):
        piece = total[tile * 4:tile * 4 + 4, :]
        if tile < 12:
            qkv_ref[:, tile * 128:(tile + 1) * 128] = piece
        else:
            proj_ref[:, (tile - 12) * 128:(tile - 11) * 128] = piece


def stage_kernel(qkv_ref, proj_ref, qkv_out, proj_out, sems):
    copies = [
        pltpu.make_async_copy(qkv_ref, qkv_out, sems.at[0]),
        pltpu.make_async_copy(proj_ref, proj_out, sems.at[1]),
    ]
    for copy in copies:
        copy.start()
    for copy in copies:
        copy.wait()


def staged(w_qkv, w_proj):
    return pl.pallas_call(
        stage_kernel,
        out_shape=(
            pltpu.VMEM(w_qkv.shape, w_qkv.dtype),
            pltpu.VMEM(w_proj.shape, w_proj.dtype),
        ),
        in_specs=[pl.BlockSpec(memory_space=pltpu.HBM)] * 2,
        out_specs=(pl.BlockSpec(memory_space=pltpu.VMEM),) * 2,
        scratch_shapes=[pltpu.SemaphoreType.DMA((2,))],
        compiler_params=pltpu.CompilerParams(vmem_limit_bytes=4 * 1024 * 1024),
        cost_estimate=pl.CostEstimate(flops=0, bytes_accessed=4 * 1024 * 1024, transcendentals=0),
        name="stage_weights",
    )(w_qkv, w_proj)


def part(value, at, refs):
    own_ref, left_ref = refs
    for level in range(LEV):
        for row in range(WLAT):
            base = (level * WLAT + row) * WLON
            tokens = jnp.concatenate([value[base:base + WLON], value[WT + base:WT + base + WLON]], axis=0)
            left_ref[at, level, row] = tokens[:SLON].astype(jnp.bfloat16)
            own_ref[at, level, row] = tokens[SLON:].astype(jnp.bfloat16)


def rest_kernel(
    n_ref, m_ref, gp_ref, u_ref, x_ref, mix_ref, qkv_ref, proj_ref,
    half_ref, own_ref, left_ref,
    wqkv_ref, wproj_ref, sems,
):
    copies = [
        pltpu.make_async_copy(proj_ref, wproj_ref, sems.at[0]),
        pltpu.make_async_copy(qkv_ref, wqkv_ref, sems.at[1]),
    ]
    for copy in copies:
        copy.start()
    grads = jnp.concatenate([dot(n_ref[...], gp_ref[...]), dot(m_ref[...], u_ref[...])], axis=1)
    store_shares(half_ref, grads)
    refs = (own_ref, left_ref)
    x = x_ref[...].astype(jnp.float32)
    copies[0].wait()
    part(x + dot(mix_ref[...], wproj_ref[...]), 0, refs)
    normed, inverse = statistics(x)
    copies[1].wait()
    grad_normed = dot(gp_ref[...], wqkv_ref[...], NT)
    grad_tokens = inverse * (
        grad_normed
        - jnp.mean(grad_normed, -1, keepdims=True)
        - normed * jnp.mean(grad_normed * normed, -1, keepdims=True)
    )
    part(u_ref[...].astype(jnp.float32) + grad_tokens, 1, refs)


def call(kernel, name, outs, scratch, flops, *args, dtypes=None, limit=12, placed=False, any_args=()):
    vmem = pl.BlockSpec(memory_space=pltpu.VMEM)
    dtypes = dtypes or (jnp.bfloat16,) * len(outs)
    make = pltpu.VMEM if placed else jax.ShapeDtypeStruct
    size = sum(2 * math.prod(shape) for shape in outs)
    return pl.pallas_call(
        kernel,
        out_shape=tuple(make(shape, dtype) for shape, dtype in zip(outs, dtypes)),
        in_specs=[
            pl.BlockSpec(memory_space=pltpu.HBM) if at in any_args else vmem for at in range(len(args))
        ],
        out_specs=(vmem,) * len(outs),
        scratch_shapes=[
            pltpu.SemaphoreType.DMA(shape) if kind is None else pltpu.VMEM(shape, kind)
            for shape, kind in scratch
        ],
        compiler_params=pltpu.CompilerParams(vmem_limit_bytes=limit * 1024 * 1024),
        cost_estimate=pl.CostEstimate(flops=flops, bytes_accessed=2 * size, transcendentals=0),
        name=name,
    )(*args)


def attention(x, u, upper, corner, left, lrow, lcol, w_qkv, w_proj):
    tokens = math.prod(x.shape[:-1])
    low, full = jnp.bfloat16, jnp.float32
    return call(
        attention_kernel,
        "window_attention",
        (
            (32, 2, 64, 128), (tokens, 3 * D), (tokens, D),
            (D // 2, tokens), (D // 2, tokens), (tokens, D), (tokens, D),
        ),
        (
            ((tokens, D), full),
            ((tokens, 3 * D), low),
            ((tokens, D), low),
            ((D, tokens), low),
            ((D, tokens), low),
            ((WT, WIDE), low),
            ((WT, WIDE), low),
            ((LANES, WIDE), full),
            ((WT, WIDE), full),
            ((WIDE, LANES), low),
            ((WIDE, LANES), low),
        ),
        5_000_000_000,
        x, u, upper, corner, left, lrow, lcol, w_qkv, w_proj,
        limit=20,
    )


LAT = ("yh", "x", "core")


def passed_along(value, axis, steps):
    count = lax.axis_size(axis)
    pairs = [(source, (source + steps) % count) for source in range(count)]
    return lax.ppermute(value, axis, pairs)


def diagonal(value, steps):
    n_lat, n_lon = lax.axis_size(LAT), lax.axis_size("lon")
    pairs = [
        (a * n_lon + b, (a + steps) % n_lat * n_lon + (b + steps) % n_lon)
        for a in range(n_lat)
        for b in range(n_lon)
    ]
    return lax.ppermute(value, (*LAT, "lon"), pairs)


def per_device(inputs, cotangent, mask_ids, w_qkv, w_proj):
    body = (2, LEV, SLAT, inputs.shape[3] - SLON, D)
    side = (2, LEV, SLAT, SLON, D)
    upper, corner, left = call(
        cut_kernel, "cut_halos", (body, side, side),
        (((2, *inputs.shape[1:]), jnp.bfloat16), ((2, LEV), None)), 1000,
        *(pltpu.with_memory_space_constraint(array, pltpu.HBM) for array in (inputs, cotangent)),
        limit=8, any_args=(0, 1),
    )
    upper = passed_along(upper, LAT, 1)
    corner = diagonal(corner, 1)
    left = passed_along(left, "lon", 1)
    first_band = lax.axis_index(LAT) == 0
    wrapped = jnp.logical_and(first_band, jnp.arange(WLAT) < SLAT).astype(jnp.int32)
    groups = mask_ids + 4 * wrapped[:, None]
    windows = groups.shape[1] // WLON
    labels = groups.reshape(WLAT, windows, WLON).transpose(1, 0, 2).reshape(windows, WLAT * WLON)
    labels = jnp.tile(labels, (1, LEV))
    lcol = labels.reshape(windows * WT, 1)
    lrow = jnp.concatenate([labels[:, :MAIN], jnp.tile(labels[:, MAIN:], (1, PER))], axis=1)
    send, gp, mix, nkeep, mkeep, x, u = attention(
        inputs, cotangent, upper, corner, left, lrow, lcol, *staged(w_qkv, w_proj)
    )
    got = passed_along(send, "core", 1)
    half, own, left = call(
        rest_kernel, "own_half_and_outputs",
        (send.shape, (2, *inputs.shape[1:3], body[3], D), (2, *inputs.shape[1:3], SLON, D)),
        ((w_qkv.shape, jnp.bfloat16), (w_proj.shape, jnp.bfloat16), ((2,), None)), 600_000_000,
        nkeep, mkeep, gp, u, x, mix, w_qkv, w_proj,
        dtypes=(jnp.float32,) + (jnp.bfloat16,) * 2, any_args=(6, 7), limit=16,
    )
    ranks = (2, 4, 8, 64, 128)
    (sums,) = call(
        add_kernel, "add_halves", ((4, 2, 8, 64, 128),), (), 1_000_000,
        half.reshape(ranks), got.reshape(ranks), placed=True,
    )
    right = passed_along(left, "lon", -1)
    spread = lax.all_to_all(sums.reshape(8, 512, 128), ("x", "yh"), 0, 0, tiled=True)
    spread, right = lax.optimization_barrier((spread, right))
    (sums,) = call(sum_kernel, "sum_parts", ((2, 512, 128),), (), 1_000_000, spread, placed=True)
    spread = lax.all_to_all(sums.reshape(16, 64, 128), ("dp", "lon"), 0, 0, tiled=True)
    grad_qkv, grad_proj = call(
        last_kernel, "last_sum", ((4, 3 * D), (4, D)), (), 1000, spread,
        dtypes=(jnp.float32,) * 2, limit=4,
    )
    (rows,) = call(rows_kernel, "halo_rows", ((2, LEV, SLAT, *inputs.shape[3:]),), (), 1000, own, right, limit=8)
    lower = passed_along(rows, LAT, -1)
    output, grad_inputs = call(
        join_kernel, "join_outputs", (inputs.shape, inputs.shape), (), 1000, own, right, lower, limit=8
    )
    return (output, grad_inputs, grad_qkv, grad_proj)


def solution(mesh):
    mesh = Mesh(mesh.devices.reshape(2, 2, 4, 2, 8), ("dp", "yh", "x", "core", "lon"))
    tokens = P("dp", None, LAT, "lon", None)
    return jax.shard_map(
        per_device,
        mesh=mesh,
        in_specs=(tokens, tokens, P(LAT, "lon"), P(), P()),
        out_specs=(tokens, tokens, P((*LAT, "lon"), None), P((*LAT, "lon"), None)),
        check_vma=False,
    )
```
